32 devices in a mesh: scene: 4 (over y, x), dom: 8 (over z, core).
Axes of the slice: x: 2, y: 2, z: 4, core: 2. Of those that a mesh axis runs over, the one named last changes fastest.
Arguments:
- features: bfloat16 [256, 64, 512], P(('scene', 'dom')), parts along dimension 0, may hold values from -6 to 6
- cotangent: bfloat16 [256, 64, 512], P(('scene', 'dom')), parts along dimension 0, may hold values from -6 to 6
- weight: bfloat16 [27, 64, 64], replicated, may hold values from -0.15625 to 0.15625
- mask_words: int32 [256, 18], P(('scene', 'dom')), parts along dimension 0, may hold values from 0 to 1073741823, as said below
- neighbors: int32 [256, 26], P(('scene', 'dom')), parts along dimension 0, may hold values from -1 to 63, as said below
Outputs:
- out_features: bfloat16 [256, 64, 512], P(('scene', 'dom')), parts along dimension 0
- in_grad: bfloat16 [256, 64, 512], P(('scene', 'dom')), parts along dimension 0
- weight_grad: float32 [108, 64, 64], P('scene'), parts along dimension 0
The draws below stay inside these ranges and needn't reach their ends.
There are 4 independent parts, one for each index of `scene`. The reference program is written for one: setup_inputs(seed, part) draws one part's arguments, and reference() takes and returns one part's arrays. A program takes and returns all parts, laid end to end along the dimension named above; an argument that names none is the same for every part. Nothing has to cross between parts.
Inputs may be any that keep to these rules, and one draw needn't show every extreme that they name: `mask_words`: bit r of word w is voxel 30 w + r of the leaf; bits at or past 512 are 0; unused slots have all bits 0. An id is owner * 8 + slot, owner being the index along dom. All leaves at one leaf position along the first dimension have the same owner; a neighbor at first offset -1 is owned by the same device or the one below it, at +1 by the same device or the one above it. The table is symmetric: b is listed as a neighbor of a at offset (p, q, r) exactly when a is listed for b at (-p, -q, -r). Used slots of a device come first; unused slots list no neighbors. At most 4 leaves of one device have a neighbor owned by one given adjacent device, and some device reaches that in every draw; some device uses all 8 slots in every draw.
All inputs are finite; a program needn't handle non-finite values.
Results may differ from the reference program's by a relative error of at most 0.001.
Values may be sent and summed in bfloat16 or wider, within the bound.
No kernel may reach another device: no remote copies, remote signals or barrier semaphores. Data moves between devices by JAX's collectives and lax.ppermute only.
A program may use at most 256 MiB of HBM per device.

```python
import jax
import jax.numpy as jnp
from jax import lax

C = 64
LEAF = 8
LEAF_DEV = 8
PLANES = 4
CROSS_Y = 4
CROSS_Z = 1
VOXELS = 512
MASK_WORDS = 18
SLOTS = 64


def leaf_layout(key):
    devices = SLOTS // LEAF_DEV
    cross_cells = CROSS_Y * CROSS_Z
    positions = PLANES * cross_cells
    key_full, key_count, key_rank = jax.random.split(jax.random.fold_in(key, 17), 3)
    full_device = jax.random.randint(key_full, (), 0, devices - 1)
    device_ids = jnp.arange(devices, dtype=jnp.int32)
    place_ids = jnp.arange(positions, dtype=jnp.int32)
    plane_of = place_ids // cross_cells
    counts = jax.random.randint(key_count, (devices,), LEAF_DEV // 4, LEAF_DEV + 1)
    counts = jnp.where(device_ids == full_device, LEAF_DEV, counts)
    counts = jnp.where(device_ids == full_device + 1, jnp.maximum(counts, cross_cells), counts)
    forced_full = (device_ids[:, None] == full_device) & (plane_of[None, :] >= PLANES - 2)
    forced_next = (device_ids[:, None] == full_device + 1) & (plane_of[None, :] == 0)
    forced = forced_full | forced_next
    scores = jax.random.randint(key_rank, (devices, positions), 0, 1 << 20) * positions + place_ids[None, :]
    scores = jnp.where(forced, place_ids[None, :] - positions, scores)
    sorting = jnp.argsort(scores, axis=1)
    rank_table = jnp.argsort(sorting, axis=1)
    occupied = rank_table < counts[:, None]
    slot_of = jnp.where(occupied, jnp.cumsum(occupied.astype(jnp.int32), axis=1) - 1, -1)
    place_key = jnp.where(occupied, place_ids[None, :], place_ids[None, :] + positions)
    place_of_slot = jnp.argsort(place_key, axis=1)[:, :LEAF_DEV].astype(jnp.int32)
    slot_used = jnp.arange(LEAF_DEV, dtype=jnp.int32)[None, :] < counts[:, None]
    return (slot_of.astype(jnp.int32), place_of_slot, slot_used)


def draw_neighbors(key, part):
    slot_of, place_of_slot, slot_used = leaf_layout(key)
    devices = SLOTS // LEAF_DEV
    cross_cells = CROSS_Y * CROSS_Z
    positions = PLANES * cross_cells
    device_ids = jnp.arange(devices, dtype=jnp.int32)[:, None]
    plane_x = device_ids * PLANES + place_of_slot // cross_cells
    coord_y = place_of_slot // CROSS_Z % CROSS_Y
    coord_z = place_of_slot % CROSS_Z
    flat_slots = slot_of.reshape(-1)
    columns = []
    for tap_number in range(27):
        if tap_number == 13:
            continue
        step_x = tap_number // 9 - 1
        step_y = tap_number // 3 % 3 - 1
        step_z = tap_number % 3 - 1
        near_x = plane_x + step_x
        near_y = coord_y + step_y
        near_z = coord_z + step_z
        inside = (near_x >= 0) & (near_x < devices * PLANES) & (near_y >= 0) & (near_y < CROSS_Y) & (near_z >= 0) & (near_z < CROSS_Z)
        near_device = jnp.clip(near_x, 0, devices * PLANES - 1) // PLANES
        near_place = jnp.clip(near_x, 0, devices * PLANES - 1) % PLANES * cross_cells + jnp.clip(near_y, 0, CROSS_Y - 1) * CROSS_Z + jnp.clip(near_z, 0, CROSS_Z - 1)
        lookup = jnp.clip(near_device * positions + near_place, 0, devices * positions - 1)
        near_slot = flat_slots[lookup]
        located = inside & slot_used & (near_slot >= 0)
        columns.append(jnp.where(located, near_device * LEAF_DEV + near_slot, -1))
    return jnp.stack(columns, axis=-1).reshape(SLOTS, 26).astype(jnp.int32)


def draw_mask_words(key, part):
    slot_of, place_of_slot, slot_used = leaf_layout(key)
    drawn = jax.random.randint(jax.random.fold_in(key, 29), (SLOTS, MASK_WORDS * 30), 0, 5)
    bit_values = (drawn < 3).astype(jnp.int32)
    within = (jnp.arange(MASK_WORDS * 30, dtype=jnp.int32) < VOXELS).astype(jnp.int32)
    bit_values = bit_values * within[None, :] * slot_used.reshape(SLOTS, 1).astype(jnp.int32)
    place_values = jnp.left_shift(jnp.ones((30,), jnp.int32), jnp.arange(30, dtype=jnp.int32))
    return jnp.sum(bit_values.reshape(SLOTS, MASK_WORDS, 30) * place_values[None, None, :], axis=2).astype(jnp.int32)


def shard_levels(rng, dims, cuts, low, high):
    def one(axis_at, parts):
        steps = jax.random.uniform(jax.random.fold_in(jax.random.fold_in(rng, 6), axis_at), (parts,), jnp.float32, low / len(cuts), high / len(cuts))
        return jnp.repeat(jnp.exp(steps), dims[axis_at] // parts).reshape((-1,) + (1,) * (len(dims) - axis_at - 1))

    factor_of = one(*cuts[0])
    for cut in cuts[1:]:
        factor_of = factor_of * one(*cut)
    return factor_of


def bell_draw(rng, dims, deviation, limit, pieces=(), kind=jnp.bfloat16):
    values = jax.random.normal(rng, dims, jnp.float32) * deviation
    if len(pieces) > 0:
        values = shard_levels(rng, dims, pieces, -0.22, 0.18) * values
    return jnp.clip(values, min=-limit, max=limit).astype(kind)


def setup_inputs(seed: int = 0, part: int = 0) -> dict:
    arg_keys = jax.random.split(jax.random.key(seed), 6)
    own_keys = jax.random.split(jax.random.fold_in(arg_keys[5], part), 6)
    features = bell_draw(own_keys[0], (SLOTS, C, VOXELS), 1.0, 6.0, ((0, 8),))
    cotangent = bell_draw(own_keys[1], (SLOTS, C, VOXELS), 1.0, 6.0, ((0, 8),))
    weight = bell_draw(arg_keys[2], (27, C, C), (27 * C) ** -0.5, 0.15625)
    mask_words = draw_mask_words(jax.random.fold_in(jax.random.fold_in(arg_keys[5], part), 71), part)
    neighbors = draw_neighbors(jax.random.fold_in(jax.random.fold_in(arg_keys[5], part), 71), part)
    return {"features": features, "cotangent": cotangent, "weight": weight, "mask_words": mask_words, "neighbors": neighbors}


def unpack_voxels(mask_words, voxel_count):
    bit_place = jnp.arange(30, dtype=jnp.int32)
    bit_values = jnp.right_shift(mask_words[:, :, None], bit_place[None, None, :]) & 1
    return bit_values.reshape(mask_words.shape[0], -1)[:, :voxel_count]


def edge_range(shift_value, extent):
    if shift_value < 0:
        return slice(extent - 1, extent)
    if shift_value > 0:
        return slice(0, 1)
    return slice(0, extent)


def tap_offsets():
    return [(shift_x, shift_y, shift_z) for shift_x in (-1, 0, 1) for shift_y in (-1, 0, 1) for shift_z in (-1, 0, 1)]


def assemble(center, fetch_piece):
    x_slabs = []
    for shift_x in (-1, 0, 1):
        y_rows = []
        for shift_y in (-1, 0, 1):
            z_cells = []
            for shift_z in (-1, 0, 1):
                if shift_x == 0 and shift_y == 0 and shift_z == 0:
                    z_cells.append(center)
                else:
                    z_cells.append(fetch_piece(shift_x, shift_y, shift_z))
            y_rows.append(jnp.concatenate(z_cells, axis=4))
        x_slabs.append(jnp.concatenate(y_rows, axis=3))
    return jnp.concatenate(x_slabs, axis=2)


def window(padded, offset, direction):
    extent = padded.shape[2] - 2
    start_x = 1 + direction * offset[0]
    start_y = 1 + direction * offset[1]
    start_z = 1 + direction * offset[2]
    piece = padded[:, :, start_x:start_x + extent, start_y:start_y + extent, start_z:start_z + extent]
    return piece.reshape(padded.shape[0], padded.shape[1], extent ** 3)


def reference(features, cotangent, weight, mask_words, neighbors):
    slot_total, channels, voxel_count = features.shape
    edge_cells = LEAF
    occupancy = unpack_voxels(mask_words, voxel_count).astype(jnp.bfloat16)
    masked_x = features * occupancy[:, None, :]
    masked_dy = cotangent * occupancy[:, None, :]
    shape_five = (slot_total, channels, edge_cells, edge_cells, edge_cells)
    block_x = masked_x.reshape(shape_five)
    block_dy = masked_dy.reshape(shape_five)
    offsets = tap_offsets()

    def sliced(block_field):
        table_list = []
        for offset in offsets:
            if offset == (0, 0, 0):
                table_list.append(None)
            else:
                table_list.append(block_field[:, :, edge_range(offset[0], edge_cells), edge_range(offset[1], edge_cells), edge_range(offset[2], edge_cells)])
        return table_list

    table_x = sliced(block_x)
    table_dy = sliced(block_dy)
    weight_wide = weight.astype(jnp.float32)
    group_size = LEAF_DEV
    block_count = slot_total // group_size

    def block_terms(inputs):
        near_block, center_x, center_dy, flat_dy = inputs

        def padded(center, table_list):
            def fetch_piece(shift_x, shift_y, shift_z):
                tap_number = (shift_x + 1) * 9 + (shift_y + 1) * 3 + shift_z + 1
                column = tap_number if tap_number < 13 else tap_number - 1
                row_index = near_block[:, column]
                picked = jnp.take(table_list[tap_number], jnp.clip(row_index, 0, slot_total - 1), axis=0)
                return jnp.where((row_index >= 0)[:, None, None, None, None], picked, jnp.zeros((), picked.dtype))
            return assemble(center, fetch_piece).astype(jnp.float32)

        pad_x = padded(center_x, table_x)
        pad_dy = padded(center_dy, table_dy)
        dy_wide = flat_dy.astype(jnp.float32)
        out_sum = jnp.zeros((group_size, channels, voxel_count), jnp.float32)
        back_sum = jnp.zeros((group_size, channels, voxel_count), jnp.float32)
        tap_grads = []
        for tap_number, offset in enumerate(offsets):
            ahead_cells = window(pad_x, offset, 1)
            behind_cells = window(pad_dy, offset, -1)
            out_sum = out_sum + jnp.einsum("io,liv->lov", weight_wide[tap_number], ahead_cells, precision=lax.Precision.HIGHEST)
            back_sum = back_sum + jnp.einsum("io,lov->liv", weight_wide[tap_number], behind_cells, precision=lax.Precision.HIGHEST)
            tap_grads.append(jnp.einsum("liv,lov->io", ahead_cells, dy_wide, precision=lax.Precision.HIGHEST))
        return out_sum, back_sum, jnp.stack(tap_grads)

    def regroup(array):
        return array.reshape((block_count, group_size) + array.shape[1:])

    out_parts, back_parts, grad_parts = lax.map(block_terms, (regroup(neighbors), regroup(block_x), regroup(block_dy), regroup(masked_dy)))
    occupancy_wide = occupancy.astype(jnp.float32)[:, None, :]
    out_features = (out_parts.reshape(slot_total, channels, voxel_count) * occupancy_wide).astype(jnp.bfloat16)
    in_grad = (back_parts.reshape(slot_total, channels, voxel_count) * occupancy_wide).astype(jnp.bfloat16)
    grad_scale = float(slot_total * voxel_count) ** -0.5
    weight_grad = jnp.sum(grad_parts, axis=0) * grad_scale
    return (out_features, in_grad, weight_grad)
```

```python
import functools

import jax
import jax.numpy as jnp
from jax import lax
from jax.experimental import pallas as pl
from jax.experimental.pallas import tpu as pltpu
from jax.sharding import PartitionSpec as P

BITS = 30
EDGE = 8
FACE = EDGE * EDGE
TILE = 128
CH = 64
GROUP = 8
KROWS = 9 * CH
VMEM_LIMIT = 48 * 1024 * 1024
BF = jnp.bfloat16
F32 = jnp.float32


def column_of(p, q, r):
    tap = (p + 1) * 9 + (q + 1) * 3 + r + 1
    return tap if tap < 13 else tap - 1


SHIFTS = [(p, q) for p in (-1, 0, 1) for q in (-1, 0)] + [(p, 1) for p in (-1, 0, 1)]


def lane_ids(rows):
    return lax.broadcasted_iota(jnp.int32, (rows, TILE), 1)


def occupancy_tile(words, tile):
    lane = lane_ids(words.shape[0]) + tile * TILE
    first, last = (tile * TILE) // BITS, (tile * TILE + TILE - 1) // BITS
    word = jnp.broadcast_to(words[:, first : first + 1], lane.shape)
    place = lane - first * BITS
    for w in range(first + 1, last + 1):
        past = lane >= w * BITS
        word = jnp.where(past, jnp.broadcast_to(words[:, w : w + 1], lane.shape), word)
        place = jnp.where(past, lane - w * BITS, place)
    return (jnp.right_shift(word, place) & 1).astype(F32)


def spread(occ, leaf):
    return jnp.broadcast_to(occ[leaf : leaf + 1, :], (CH, TILE)).astype(BF)


def roll(value, amount):
    return pltpu.roll(value, amount % TILE, 1)


def edges_kernel(words_ref, x_lo, x_hi, d_lo, d_hi, up_ref, down_ref):
    words = words_ref[...]
    occ_lo = occupancy_tile(words, 0)
    occ_hi = occupancy_tile(words, 3)
    left = lane_ids(CH) < FACE
    for leaf in range(x_lo.shape[0]):
        low, high = spread(occ_lo, leaf), spread(occ_hi, leaf)
        up_ref[leaf] = jnp.where(left, roll(d_hi[leaf] * high, FACE), x_hi[leaf] * high)
        down_ref[leaf] = jnp.where(left, x_lo[leaf] * low, roll(d_lo[leaf] * low, FACE))


def edges(words, x, dy):
    leaves = x.shape[0]
    block = (leaves, CH, TILE)
    lo = pl.BlockSpec(block, lambda i: (0, 0, 0))
    hi = pl.BlockSpec(block, lambda i: (0, 0, 3))
    shape = jax.ShapeDtypeStruct(block, BF)
    return pl.pallas_call(
        edges_kernel,
        grid=(1,),
        out_shape=(shape, shape),
        in_specs=[pl.BlockSpec(words.shape, lambda i: (0, 0)), lo, hi, lo, hi],
        out_specs=(lo, lo),
        cost_estimate=pl.CostEstimate(flops=10**6, bytes_accessed=10**6, transcendentals=0),
        compiler_params=pltpu.CompilerParams(vmem_limit_bytes=VMEM_LIMIT),
        name="edges",
    )(words, x, x, dy, dy)


def fill(store, field_ref, occ, below_ref, above_ref, turned):
    leaves = field_ref.shape[0]
    for leaf in range(leaves):
        for k in range(4):
            at = slice(k * TILE, (k + 1) * TILE)
            store[leaf, :, at] = field_ref[leaf, :, at] * spread(occ[k], leaf)
    for leaf in range(leaves):
        low, high = above_ref[leaf], below_ref[leaf]
        store[leaves + leaf, :, 0:TILE] = roll(low, FACE) if turned else low
        store[leaves + leaf, :, 3 * TILE : 4 * TILE] = roll(high, FACE) if turned else high
    store[2 * leaves] = jnp.zeros(store.shape[1:], BF)


def stacked(store, near_ref, leaf, z, device, leaves):
    def place(p, q):
        if (p, q, z) == (0, 0, 0):
            return leaf
        ident = near_ref[leaf, column_of(p, q, z)]
        owner = ident // leaves
        slot = ident - owner * leaves
        slot = jnp.where(owner == device, slot, slot + leaves)
        return jnp.where(ident < 0, 2 * leaves, slot)

    lane = lane_ids(CH)
    left = lane < FACE
    row_b = (lane // EDGE) % EDGE
    first, last = row_b == 0, row_b == EDGE - 1
    tiles = {}
    for q in (-1, 0, 1):
        mid = place(0, q)
        tiles[q] = [store[mid, :, k * TILE : (k + 1) * TILE] for k in range(4)]
        after = store[place(1, q), :, 0:TILE]
        before = store[place(-1, q), :, 3 * TILE : 4 * TILE]
        tiles[q].append(jnp.where(left, after, before))
    moved = {
        -1: [
            jnp.where(first, roll(m, FACE + EDGE), roll(c, EDGE))
            for m, c in zip(tiles[-1], tiles[0])
        ],
        0: tiles[0],
        1: [
            jnp.where(last, roll(m, -FACE - EDGE), roll(c, -EDGE))
            for m, c in zip(tiles[1], tiles[0])
        ],
    }
    swapped = {q: [roll(t, FACE) for t in moved[q]] for q in (-1, 0, 1)}

    def piece(p, q):
        if p == 0:
            parts = moved[q][:4]
        elif p == 1:
            parts = [jnp.where(left, swapped[q][k], swapped[q][k + 1]) for k in range(4)]
        else:
            parts = [jnp.where(left, swapped[q][(k - 1) % 5], swapped[q][k]) for k in range(4)]
        return jnp.concatenate(parts, axis=1)

    return jnp.concatenate([piece(p, q) for p, q in SHIFTS], axis=0)


def c_index():
    return lane_ids(CH) % EDGE


def shift_c(value, r, fill_from=None):
    if r == 0:
        return value
    edge = c_index() == (EDGE - 1 if r > 0 else 0)
    zero = jnp.zeros((CH, TILE), value.dtype)
    parts = [
        jnp.where(edge, zero, roll(value[:, k * TILE : (k + 1) * TILE], -r)) for k in range(4)
    ]
    return jnp.concatenate(parts, axis=1)


def across_c(value, z):
    edge = c_index() == (EDGE - 1 if z > 0 else 0)
    zero = jnp.zeros((CH, TILE), value.dtype)
    parts = [
        jnp.where(edge, roll(value[:, k * TILE : (k + 1) * TILE], z * (EDGE - 1)), zero)
        for k in range(4)
    ]
    return jnp.concatenate(parts, axis=1)


def listed(near_ref, leaf, z):
    found = jnp.int32(-1)
    for p in (-1, 0, 1):
        for q in (-1, 0, 1):
            found = jnp.maximum(found, near_ref[leaf, column_of(p, q, z)])
    return found >= 0


def grad_kernel(
    near_ref, words_ref, x_ref, d_ref, below_ref, above_ref, keep_ref, send_ref, store, total, packed
):
    leaves = x_ref.shape[0]
    device = lax.axis_index("dom")
    words = words_ref[...]
    occ = [occupancy_tile(words, k) for k in range(4)]
    fill(store, d_ref, occ, below_ref, above_ref, True)

    def masked_x(leaf):
        return jnp.concatenate(
            [x_ref[leaf, :, k * TILE : (k + 1) * TILE] * spread(occ[k], leaf) for k in range(4)],
            axis=1,
        )

    contract = (((1,), (1,)), ((), ()))
    for leaf in range(leaves):
        near_dy = stacked(store, near_ref, leaf, 0, device, leaves)
        center = masked_x(leaf)
        wide = jnp.concatenate([shift_c(center, r) for r in (-1, 0, 1)], axis=0)
        term = lax.dot_general(wide, near_dy, contract, preferred_element_type=F32)
        if leaf == 0:
            total[...] = term
        else:
            total[...] += term

    for z in (-1, 1):
        for leaf in range(leaves):

            @pl.when(listed(near_ref, leaf, z))
            def _():
                near_dy = stacked(store, near_ref, leaf, z, device, leaves)
                edge = across_c(masked_x(leaf), -z)
                rows = pl.ds((-z + 1) * CH, CH)
                total[rows, :] += lax.dot_general(
                    edge, near_dy, contract, preferred_element_type=F32
                )

    for k in range(4):
        packed[k * 3 * CH : (k + 1) * 3 * CH, :] = total[:, k * TILE : (k + 1) * TILE]
    half = 3 * CH // 2
    packed[12 * CH : 12 * CH + half, 0:CH] = total[0:half, 4 * TILE :]
    packed[12 * CH : 12 * CH + half, CH:] = total[half:, 4 * TILE :]
    packed[12 * CH + half :, :] = jnp.zeros((packed.shape[0] - 12 * CH - half, TILE), F32)
    core = lax.rem(device, 2)
    rows = packed.shape[0] // 2
    keep_ref[...] = packed[pl.ds(pl.multiple_of(core * rows, 8), rows), :]
    send_ref[...] = packed[pl.ds(pl.multiple_of((1 - core) * rows, 8), rows), :]


def grad_terms(near, words, x, dy, below, above):
    leaves = x.shape[0]
    rows = 14 * CH
    vmem = pl.BlockSpec(memory_space=pltpu.VMEM)
    smem = pl.BlockSpec(memory_space=pltpu.SMEM)
    shape = jax.ShapeDtypeStruct((rows // 2, TILE), F32)
    return pl.pallas_call(
        grad_kernel,
        out_shape=(shape, shape),
        in_specs=[smem, vmem, vmem, vmem, vmem, vmem],
        out_specs=(vmem, vmem),
        scratch_shapes=[
            pltpu.VMEM((2 * leaves + 1, CH, 4 * TILE), BF),
            pltpu.VMEM((3 * CH, KROWS), F32),
            pltpu.VMEM((rows, TILE), F32),
        ],
        cost_estimate=pl.CostEstimate(flops=10**9, bytes_accessed=2 * 10**6, transcendentals=0),
        compiler_params=pltpu.CompilerParams(vmem_limit_bytes=VMEM_LIMIT),
        name="grad_terms",
    )(near, words, x, dy, below, above)


def conv_kernel(turned, near_ref, words_ref, x_ref, below_ref, above_ref, w_ref, out_ref, store):
    leaves = x_ref.shape[0]
    device = lax.axis_index("dom")
    words = words_ref[...]
    occ = [occupancy_tile(words, k) for k in range(4)]
    fill(store, x_ref, occ, below_ref, above_ref, turned)
    taps = w_ref[...]

    def masked(leaf, value):
        return jnp.concatenate(
            [
                value[:, k * TILE : (k + 1) * TILE]
                * jnp.broadcast_to(occ[k][leaf : leaf + 1, :], (CH, TILE))
                for k in range(4)
            ],
            axis=1,
        )

    for leaf in range(leaves):
        near_x = stacked(store, near_ref, leaf, 0, device, leaves)
        wide = jnp.dot(taps, near_x, preferred_element_type=F32)
        total = wide[CH : 2 * CH]
        for r in (-1, 1):
            total = total + shift_c(wide[(r + 1) * CH : (r + 2) * CH], r)
        out_ref[leaf] = masked(leaf, total).astype(BF)

    for leaf in range(leaves):

        @pl.when(listed(near_ref, leaf, -1) | listed(near_ref, leaf, 1))
        def _():
            near_x = stacked(store, near_ref, leaf, 0, device, leaves)
            wide = jnp.dot(taps, near_x, preferred_element_type=F32)
            total = wide[CH : 2 * CH]
            for r in (-1, 1):
                total = total + shift_c(wide[(r + 1) * CH : (r + 2) * CH], r)
            for z in (-1, 1):
                near_z = stacked(store, near_ref, leaf, z, device, leaves)
                part = jnp.dot(
                    taps[(z + 1) * CH : (z + 2) * CH], near_z, preferred_element_type=F32
                )
                total = total + across_c(part, z)
            out_ref[leaf] = masked(leaf, total).astype(BF)


def conv(near, words, x, below, above, taps, turned):
    leaves = x.shape[0]
    vmem = pl.BlockSpec(memory_space=pltpu.VMEM)
    smem = pl.BlockSpec(memory_space=pltpu.SMEM)
    return pl.pallas_call(
        functools.partial(conv_kernel, turned),
        out_shape=jax.ShapeDtypeStruct(x.shape, BF),
        in_specs=[smem, vmem, vmem, vmem, vmem, vmem],
        out_specs=vmem,
        scratch_shapes=[pltpu.VMEM((2 * leaves + 1, CH, 4 * TILE), BF)],
        cost_estimate=pl.CostEstimate(flops=2 * 10**9, bytes_accessed=2 * 10**6, transcendentals=0),
        compiler_params=pltpu.CompilerParams(vmem_limit_bytes=VMEM_LIMIT),
        name="in_grad_conv" if turned else "out_conv",
    )(near, words, x, below, above, taps)


def unpack_kernel(scale, halves_ref, out_ref):
    core = lax.rem(lax.axis_index("dom"), 2)
    own, other = halves_ref[0], halves_ref[1]
    first = jnp.where(core == 0, own, other)
    second = jnp.where(core == 0, other, own)
    total = jnp.concatenate([first, second], axis=0) * scale
    for index, (p, q) in enumerate(SHIFTS):
        for r in (-1, 0, 1):
            tap = (-p + 1) * 9 + (-q + 1) * 3 + r + 1
            if index < 8:
                row = (index // 2) * 3 * CH + (r + 1) * CH
                side = index % 2
                out_ref[tap] = total[row : row + CH, side * CH : (side + 1) * CH]
            else:
                base, half = 12 * CH, 3 * CH // 2
                start = (r + 1) * CH
                parts = []
                for begin in range(start, start + CH, CH // 2):
                    side, row = begin // half, base + begin % half
                    parts.append(total[row : row + CH // 2, side * CH : (side + 1) * CH])
                out_ref[tap] = jnp.concatenate(parts, axis=0)


def unpack(halves, scale):
    vmem = pl.BlockSpec(memory_space=pltpu.VMEM)
    return pl.pallas_call(
        functools.partial(unpack_kernel, scale),
        out_shape=jax.ShapeDtypeStruct((27, CH, CH), F32),
        in_specs=[vmem],
        out_specs=vmem,
        cost_estimate=pl.CostEstimate(flops=10**6, bytes_accessed=10**6, transcendentals=0),
        compiler_params=pltpu.CompilerParams(vmem_limit_bytes=VMEM_LIMIT),
        name="unpack_grad",
    )(halves)


def exchange(array, mask, size):
    return lax.ppermute(array, "dom", [(i, i ^ mask) for i in range(size)])


def shards(features, cotangent, weight, mask_words, neighbors):
    leaves, channels, voxels = features.shape
    size = lax.axis_size("dom")
    device = lax.axis_index("dom")
    up = [(i, i + 1) for i in range(size - 1)]
    down = [(i + 1, i) for i in range(size - 1)]
    to_above, to_below = edges(mask_words, features, cotangent)
    below = lax.ppermute(to_above, "dom", up)
    above = lax.ppermute(to_below, "dom", down)

    cube = weight.reshape(3, 3, 3, channels, channels)
    order = lambda c: jnp.concatenate([c[:, :2].reshape(6, *c.shape[2:]), c[:, 2]], axis=0)
    taps_out = order(cube).transpose(1, 3, 0, 2).reshape(3 * channels, KROWS)
    taps_back = order(cube[::-1, ::-1, ::-1]).transpose(1, 2, 0, 3).reshape(3 * channels, KROWS)

    keep, send = grad_terms(neighbors, mask_words, features, cotangent, below, above)
    keep = keep + exchange(send, 1, size)
    rows = keep.shape[0] // 4
    lane = (device // 2) % 4
    chunk = lambda index: lax.dynamic_slice_in_dim(keep, index * rows, rows, axis=0)
    got = [exchange(chunk(lane ^ m), 2 * m, size) for m in (1, 2, 3)]
    out_features = conv(neighbors, mask_words, features, below, above, taps_out, False)
    own = chunk(lane) + got[0] + got[1] + got[2]
    if size > GROUP:
        groups = [[j * GROUP + i for j in range(size // GROUP)] for i in range(GROUP)]
        own = lax.psum(own, "dom", axis_index_groups=groups)
    back = [exchange(own, 2 * m, size) for m in (1, 2, 3)]
    in_grad = conv(neighbors, mask_words, cotangent, below, above, taps_back, True)
    half = jnp.zeros((4, rows, TILE), F32)
    for m, part in zip((0, 1, 2, 3), [own] + back):
        half = lax.dynamic_update_slice_in_dim(half, part[None], lane ^ m, axis=0)
    half = half.reshape(4 * rows, TILE)
    other = exchange(half, 1, size)
    scale = float(size * leaves * voxels) ** -0.5
    weight_grad = unpack(jnp.stack([half, other]), scale)
    return (out_features, in_grad, weight_grad)


def solution(mesh):
    split = P(("scene", "dom"), None, None)
    flat = P(("scene", "dom"), None)
    return jax.shard_map(
        shards,
        mesh=mesh,
        in_specs=(split, split, P(), flat, flat),
        out_specs=(split, split, P("scene", None, None)),
        check_vma=False,
    )
```

```python
import functools

import jax
import jax.numpy as jnp
from jax import lax
from jax.experimental import pallas as pl
from jax.experimental.pallas import tpu as pltpu
from jax.sharding import PartitionSpec as P

BITS = 30
EDGE = 8
FACE = EDGE * EDGE
TILE = 128
CH = 64
GROUP = 8
KROWS = 9 * CH
SPLIT = 5 * CH
VMEM_LIMIT = 40 * 1024 * 1024
EDGES_VMEM = 60 * 1024 * 1024
BF = jnp.bfloat16
F32 = jnp.float32


def column_of(p, q, r):
    tap = (p + 1) * 9 + (q + 1) * 3 + r + 1
    return tap if tap < 13 else tap - 1


SHIFTS = [(p, q) for p in (-1, 0, 1) for q in (-1, 0)] + [(p, 1) for p in (-1, 0, 1)]


def lane_ids(rows):
    return lax.broadcasted_iota(jnp.int32, (rows, TILE), 1)


def occupancy_tile(words, tile):
    lane = lane_ids(words.shape[0]) + tile * TILE
    first, last = (tile * TILE) // BITS, (tile * TILE + TILE - 1) // BITS
    word = jnp.broadcast_to(words[:, first : first + 1], lane.shape)
    place = lane - first * BITS
    for w in range(first + 1, last + 1):
        past = lane >= w * BITS
        word = jnp.where(past, jnp.broadcast_to(words[:, w : w + 1], lane.shape), word)
        place = jnp.where(past, lane - w * BITS, place)
    return (jnp.right_shift(word, place) & 1).astype(F32)


def spread(occ, leaf):
    return jnp.broadcast_to(occ[leaf : leaf + 1, :], (CH, TILE)).astype(BF)


def roll(value, amount):
    return pltpu.roll(value, amount % TILE, 1)


def edges_kernel(words_ref, x_lo, x_hi, d_lo, d_hi, cross_ref, chip_ref):
    words = words_ref[...]
    occ_lo = occupancy_tile(words, 0)
    occ_hi = occupancy_tile(words, 3)
    left = lane_ids(CH) < FACE
    first_core = lax.rem(lax.axis_index("dom"), 2) == 0
    for leaf in range(x_lo.shape[0]):
        low, high = spread(occ_lo, leaf), spread(occ_hi, leaf)
        up = jnp.where(left, roll(d_hi[leaf] * high, FACE), x_hi[leaf] * high)
        down = jnp.where(left, x_lo[leaf] * low, roll(d_lo[leaf] * low, FACE))

        @pl.when(first_core)
        def _():
            cross_ref[leaf] = down
            chip_ref[leaf] = up

        @pl.when(jnp.logical_not(first_core))
        def _():
            cross_ref[leaf] = up
            chip_ref[leaf] = down


def edges(words, x, dy):
    leaves = x.shape[0]
    block = (leaves, CH, TILE)
    lo = pl.BlockSpec(block, lambda i: (0, 0, 0))
    hi = pl.BlockSpec(block, lambda i: (0, 0, 3))
    shape = jax.ShapeDtypeStruct(block, BF)
    return pl.pallas_call(
        edges_kernel,
        grid=(1,),
        out_shape=(shape, shape),
        in_specs=[pl.BlockSpec(words.shape, lambda i: (0, 0)), lo, hi, lo, hi],
        out_specs=(lo, lo),
        cost_estimate=pl.CostEstimate(flops=10**6, bytes_accessed=10**6, transcendentals=0),
        compiler_params=pltpu.CompilerParams(vmem_limit_bytes=EDGES_VMEM),
        name="edges",
    )(words, x, x, dy, dy)


def fill(store, field_ref, occ, cross_ref, chip_ref, turned):
    leaves = field_ref.shape[0]
    first_core = lax.rem(lax.axis_index("dom"), 2) == 0
    for leaf in range(leaves):
        for k in range(4):
            at = slice(k * TILE, (k + 1) * TILE)
            store[leaf, :, at] = field_ref[leaf, :, at] * spread(occ[k], leaf)

    def far(above_ref, below_ref):
        for leaf in range(leaves):
            low, high = above_ref[leaf], below_ref[leaf]
            store[leaves + leaf, :, 0:TILE] = roll(low, FACE) if turned else low
            store[leaves + leaf, :, 3 * TILE : 4 * TILE] = roll(high, FACE) if turned else high

    pl.when(first_core)(lambda: far(chip_ref, cross_ref))
    pl.when(jnp.logical_not(first_core))(lambda: far(cross_ref, chip_ref))
    store[2 * leaves] = jnp.zeros(store.shape[1:], BF)


def stacked(store, near_ref, leaf, z, device, leaves):
    def place(p, q):
        if (p, q, z) == (0, 0, 0):
            return leaf
        ident = near_ref[leaf, column_of(p, q, z)]
        owner = ident // leaves
        slot = ident - owner * leaves
        slot = jnp.where(owner == device, slot, slot + leaves)
        return jnp.where(ident < 0, 2 * leaves, slot)

    lane = lane_ids(CH)
    left = lane < FACE
    row_b = (lane // EDGE) % EDGE
    first, last = row_b == 0, row_b == EDGE - 1
    tiles = {}
    for q in (-1, 0, 1):
        mid = place(0, q)
        tiles[q] = [store[mid, :, k * TILE : (k + 1) * TILE] for k in range(4)]
        after = store[place(1, q), :, 0:TILE]
        before = store[place(-1, q), :, 3 * TILE : 4 * TILE]
        tiles[q].append(jnp.where(left, after, before))
    moved = {
        -1: [
            jnp.where(first, roll(m, FACE + EDGE), roll(c, EDGE))
            for m, c in zip(tiles[-1], tiles[0])
        ],
        0: tiles[0],
        1: [
            jnp.where(last, roll(m, -FACE - EDGE), roll(c, -EDGE))
            for m, c in zip(tiles[1], tiles[0])
        ],
    }
    swapped = {q: [roll(t, FACE) for t in moved[q]] for q in (-1, 0, 1)}

    def piece(p, q):
        if p == 0:
            parts = moved[q][:4]
        elif p == 1:
            parts = [jnp.where(left, swapped[q][k], swapped[q][k + 1]) for k in range(4)]
        else:
            parts = [jnp.where(left, swapped[q][(k - 1) % 5], swapped[q][k]) for k in range(4)]
        return jnp.concatenate(parts, axis=1)

    return jnp.concatenate([piece(p, q) for p, q in SHIFTS], axis=0)


def c_index():
    return lane_ids(CH) % EDGE


def shift_c(value, r):
    if r == 0:
        return value
    edge = c_index() == (EDGE - 1 if r > 0 else 0)
    zero = jnp.zeros((CH, TILE), value.dtype)
    parts = [
        jnp.where(edge, zero, roll(value[:, k * TILE : (k + 1) * TILE], -r)) for k in range(4)
    ]
    return jnp.concatenate(parts, axis=1)


def across_c(value, z):
    edge = c_index() == (EDGE - 1 if z > 0 else 0)
    zero = jnp.zeros((CH, TILE), value.dtype)
    parts = [
        jnp.where(edge, roll(value[:, k * TILE : (k + 1) * TILE], z * (EDGE - 1)), zero)
        for k in range(4)
    ]
    return jnp.concatenate(parts, axis=1)


def listed(near_ref, leaf, z):
    found = jnp.int32(-1)
    for p in (-1, 0, 1):
        for q in (-1, 0, 1):
            found = jnp.maximum(found, near_ref[leaf, column_of(p, q, z)])
    return found >= 0


def grad_kernel(
    near_ref, words_ref, x_ref, d_ref, cross_ref, chip_ref, keep_ref, send_ref, store, total, packed
):
    leaves = x_ref.shape[0]
    device = lax.axis_index("dom")
    words = words_ref[...]
    occ = [occupancy_tile(words, k) for k in range(4)]
    fill(store, x_ref, occ, cross_ref, chip_ref, False)

    def masked_dy(leaf):
        return jnp.concatenate(
            [d_ref[leaf, :, k * TILE : (k + 1) * TILE] * spread(occ[k], leaf) for k in range(4)],
            axis=1,
        )

    contract = (((1,), (1,)), ((), ()))
    for leaf in range(leaves):
        near_x = stacked(store, near_ref, leaf, 0, device, leaves)
        center = masked_dy(leaf)
        wide = jnp.concatenate([shift_c(center, -r) for r in (-1, 0, 1)], axis=0)
        term = lax.dot_general(near_x, wide, contract, preferred_element_type=F32)
        if leaf == 0:
            total[...] = term
        else:
            total[...] += term

    for z in (-1, 1):
        for leaf in range(leaves):

            @pl.when(listed(near_ref, leaf, z))
            def _():
                near_x = stacked(store, near_ref, leaf, z, device, leaves)
                edge = across_c(masked_dy(leaf), -z)
                at = slice((z + 1) * CH, (z + 2) * CH)
                total[:, at] += lax.dot_general(
                    near_x, edge, contract, preferred_element_type=F32
                )

    packed[0:KROWS, :] = total[:, 0:TILE]
    packed[KROWS:, 0:CH] = total[0:SPLIT, TILE:]
    packed[KROWS : 2 * KROWS - SPLIT, CH:] = total[SPLIT:, TILE:]
    packed[2 * KROWS - SPLIT :, CH:] = jnp.zeros((2 * SPLIT - KROWS, CH), F32)
    core = lax.rem(device, 2)
    rows = packed.shape[0] // 2
    keep_ref[...] = packed[pl.ds(pl.multiple_of(core * rows, 8), rows), :]
    send_ref[...] = packed[pl.ds(pl.multiple_of((1 - core) * rows, 8), rows), :]


def vmem_spec():
    return pl.BlockSpec(memory_space=pltpu.VMEM)


def any_spec():
    return pl.BlockSpec(memory_space=pl.ANY)


def smem_spec():
    return pl.BlockSpec(memory_space=pltpu.SMEM)


def params():
    return pltpu.CompilerParams(vmem_limit_bytes=VMEM_LIMIT)


def cost(flops, bytes_accessed):
    return pl.CostEstimate(flops=flops, bytes_accessed=bytes_accessed, transcendentals=0)


def grad_terms(near, words, x, dy, cross, chip):
    leaves = x.shape[0]
    rows = KROWS + SPLIT
    shape = jax.ShapeDtypeStruct((rows // 2, TILE), F32)
    return pl.pallas_call(
        grad_kernel,
        out_shape=(shape, shape),
        in_specs=[smem_spec()] + [vmem_spec()] * 5,
        out_specs=(vmem_spec(), vmem_spec()),
        scratch_shapes=[
            pltpu.VMEM((2 * leaves + 1, CH, 4 * TILE), BF),
            pltpu.VMEM((KROWS, 3 * CH), F32),
            pltpu.VMEM((rows, TILE), F32),
        ],
        cost_estimate=cost(10**9, 2 * 10**6),
        compiler_params=params(),
        name="grad_terms",
    )(near, words, x, dy, cross, chip)


def conv_kernel(
    turned, near_ref, words_ref, x_ref, cross_ref, chip_ref, w_ref, _, out_ref, done_ref, store, taps_ref
):
    leaves = x_ref.shape[0]
    device = lax.axis_index("dom")
    words = words_ref[...]
    occ = [occupancy_tile(words, k) for k in range(4)]
    fill(store, x_ref, occ, cross_ref, chip_ref, turned)
    for index, (p, q) in enumerate(SHIFTS):
        for r in (-1, 0, 1):
            tap = (p + 1) * 9 + (q + 1) * 3 + r + 1
            block = w_ref[26 - tap] if turned else w_ref[tap].T
            taps_ref[(r + 1) * CH : (r + 2) * CH, index * CH : (index + 1) * CH] = block
    taps = taps_ref[...]
    done_ref[...] = jnp.zeros(done_ref.shape, F32)

    def masked(leaf, value):
        return jnp.concatenate(
            [
                value[:, k * TILE : (k + 1) * TILE]
                * jnp.broadcast_to(occ[k][leaf : leaf + 1, :], (CH, TILE))
                for k in range(4)
            ],
            axis=1,
        )

    for leaf in range(leaves):
        near_x = stacked(store, near_ref, leaf, 0, device, leaves)
        wide = jnp.dot(taps, near_x, preferred_element_type=F32)
        total = wide[CH : 2 * CH]
        for r in (-1, 1):
            total = total + shift_c(wide[(r + 1) * CH : (r + 2) * CH], r)
        out_ref[leaf] = masked(leaf, total).astype(BF)

    for leaf in range(leaves):

        @pl.when(listed(near_ref, leaf, -1) | listed(near_ref, leaf, 1))
        def _():
            near_x = stacked(store, near_ref, leaf, 0, device, leaves)
            wide = jnp.dot(taps, near_x, preferred_element_type=F32)
            total = wide[CH : 2 * CH]
            for r in (-1, 1):
                total = total + shift_c(wide[(r + 1) * CH : (r + 2) * CH], r)
            for z in (-1, 1):
                near_z = stacked(store, near_ref, leaf, z, device, leaves)
                part = jnp.dot(
                    taps[(z + 1) * CH : (z + 2) * CH], near_z, preferred_element_type=F32
                )
                total = total + across_c(part, z)
            out_ref[leaf] = masked(leaf, total).astype(BF)


def conv(near, words, x, cross, chip, weight, after, turned):
    leaves = x.shape[0]
    return pl.pallas_call(
        functools.partial(conv_kernel, turned),
        out_shape=(jax.ShapeDtypeStruct(x.shape, BF), jax.ShapeDtypeStruct((8, TILE), F32)),
        in_specs=[smem_spec()] + [vmem_spec()] * 5 + [any_spec()],
        out_specs=(vmem_spec(), vmem_spec()),
        scratch_shapes=[
            pltpu.VMEM((2 * leaves + 1, CH, 4 * TILE), BF),
            pltpu.VMEM((3 * CH, KROWS), BF),
        ],
        cost_estimate=cost(2 * 10**9, 2 * 10**6),
        compiler_params=params(),
        name="in_grad_conv" if turned else "out_conv",
    )(near, words, x, cross, chip, weight, after)


def sum_kernel(own_ref, *refs):
    *got_refs, _, out_ref = refs
    total = own_ref[...]
    for got_ref in got_refs:
        total = total + got_ref[...]
    out_ref[...] = total


def sum_chunks(own, got, after):
    return pl.pallas_call(
        sum_kernel,
        out_shape=jax.ShapeDtypeStruct(own.shape, F32),
        in_specs=[vmem_spec()] * (1 + len(got)) + [any_spec()],
        out_specs=vmem_spec(),
        cost_estimate=cost(10**5, 3 * 10**5),
        compiler_params=params(),
        name="sum_chunks",
    )(own, *got, after)


def join_kernel(*refs):
    *parts, _, out_ref = refs
    lane = lax.rem(lax.axis_index("dom") // 2, 4)
    rows = parts[0].shape[0]
    for mask, part in enumerate(parts):
        at = pl.multiple_of(jnp.bitwise_xor(lane, mask) * rows, 8)
        out_ref[pl.ds(at, rows), :] = part[...]


def join_chunks(parts, after):
    rows = parts[0].shape[0]
    return pl.pallas_call(
        join_kernel,
        out_shape=jax.ShapeDtypeStruct((len(parts) * rows, TILE), F32),
        in_specs=[vmem_spec()] * len(parts) + [any_spec()],
        out_specs=vmem_spec(),
        cost_estimate=cost(10**5, 5 * 10**5),
        compiler_params=params(),
        name="join_chunks",
    )(*parts, after)


def unpack_kernel(scale, own_ref, other_ref, out_ref, total):
    core = lax.rem(lax.axis_index("dom"), 2)
    rows = own_ref.shape[0]
    total[pl.ds(pl.multiple_of(core * rows, 8), rows), :] = own_ref[...] * scale
    total[pl.ds(pl.multiple_of((1 - core) * rows, 8), rows), :] = other_ref[...] * scale
    for index, (p, q) in enumerate(SHIFTS):
        for r in (-1, 0, 1):
            tap = (p + 1) * 9 + (q + 1) * 3 + r + 1
            row, side = index * CH, r + 1
            if r == 1:
                row, side = (KROWS + row, 0) if row < SPLIT else (KROWS + row - SPLIT, 1)
            out_ref[tap] = total[row : row + CH, side * CH : (side + 1) * CH]


def unpack(own, other, scale):
    return pl.pallas_call(
        functools.partial(unpack_kernel, scale),
        out_shape=jax.ShapeDtypeStruct((27, CH, CH), F32),
        in_specs=[vmem_spec(), vmem_spec()],
        out_specs=vmem_spec(),
        scratch_shapes=[pltpu.VMEM((2 * own.shape[0], TILE), F32)],
        cost_estimate=cost(10**6, 10**6),
        compiler_params=params(),
        name="unpack_grad",
    )(own, other)


def exchange(array, mask, size):
    return lax.ppermute(array, "dom", [(i, i ^ mask) for i in range(size)])


def shards(features, cotangent, weight, mask_words, neighbors):
    leaves, channels, voxels = features.shape
    size = lax.axis_size("dom")
    device = lax.axis_index("dom")
    to_cross, to_chip = edges(mask_words, features, cotangent)
    between = [(i, i + 1) for i in range(1, size - 1, 2)]
    cross = lax.ppermute(to_cross, "dom", between + [(j, i) for i, j in between])
    chip = exchange(to_chip, 1, size)

    keep, send = grad_terms(neighbors, mask_words, features, cotangent, cross, chip)
    keep = keep + exchange(send, 1, size)
    rows = keep.shape[0] // 4
    lane = (device // 2) % 4
    chunk = lambda index: lax.dynamic_slice_in_dim(keep, index * rows, rows, axis=0)
    to_send = [chunk(lane ^ m) for m in (1, 2, 3)]
    own = chunk(lane)
    got = [exchange(part, 2 * m, size) for m, part in zip((1, 2, 3), to_send)]
    out_features, out_done = conv(
        neighbors, mask_words, features, cross, chip, weight, to_send[2], False
    )
    own = sum_chunks(own, got, out_done)
    if size > GROUP:
        groups = [[j * GROUP + i for j in range(size // GROUP)] for i in range(GROUP)]
        own = lax.psum(own, "dom", axis_index_groups=groups)
    back = [exchange(own, 2 * m, size) for m in (1, 2, 3)]
    in_grad, in_done = conv(neighbors, mask_words, cotangent, cross, chip, weight, own, True)
    half = join_chunks([own] + back, in_done)
    other = exchange(half, 1, size)
    scale = float(size * leaves * voxels) ** -0.5
    return (out_features, in_grad, unpack(half, other, scale))


def solution(mesh):
    split = P(("scene", "dom"), None, None)
    flat = P(("scene", "dom"), None)
    return jax.shard_map(
        shards,
        mesh=mesh,
        in_specs=(split, split, P(), flat, flat),
        out_specs=(split, split, P("scene", None, None)),
        check_vma=False,
    )
```

```python
import functools

import jax
import jax.numpy as jnp
from jax import lax
from jax.experimental import pallas as pl
from jax.experimental.pallas import tpu as pltpu
from jax.sharding import PartitionSpec as P

BITS = 30
EDGE = 8
FACE = EDGE * EDGE
TILE = 128
CH = 64
GROUP = 8
KROWS = 9 * CH
SPLIT = 5 * CH
VMEM_LIMIT = 40 * 1024 * 1024
EDGES_VMEM = 63000000
BF = jnp.bfloat16
F32 = jnp.float32


def column_of(p, q, r):
    tap = (p + 1) * 9 + (q + 1) * 3 + r + 1
    return tap if tap < 13 else tap - 1


SHIFTS = [(p, q) for p in (-1, 0, 1) for q in (-1, 0)] + [(p, 1) for p in (-1, 0, 1)]


def lane_ids(rows):
    return lax.broadcasted_iota(jnp.int32, (rows, TILE), 1)


def occupancy_tile(words, tile):
    lane = lane_ids(words.shape[0]) + tile * TILE
    first, last = (tile * TILE) // BITS, (tile * TILE + TILE - 1) // BITS
    word = jnp.broadcast_to(words[:, first : first + 1], lane.shape)
    place = lane - first * BITS
    for w in range(first + 1, last + 1):
        past = lane >= w * BITS
        word = jnp.where(past, jnp.broadcast_to(words[:, w : w + 1], lane.shape), word)
        place = jnp.where(past, lane - w * BITS, place)
    return (jnp.right_shift(word, place) & 1).astype(F32)


def spread(occ, leaf):
    return jnp.broadcast_to(occ[leaf : leaf + 1, :], (CH, TILE)).astype(BF)


def roll(value, amount):
    return pltpu.roll(value, amount % TILE, 1)


def edges_kernel(words_hbm, x_hbm, d_hbm, cross_ref, chip_ref, words_ref, tiles, sems):
    leaves = x_hbm.shape[0]
    copies = [pltpu.make_async_copy(words_hbm, words_ref, sems.at[4])]
    for i, (field, k) in enumerate(((x_hbm, 0), (x_hbm, 3), (d_hbm, 0), (d_hbm, 3))):
        source = field.at[:, :, pl.ds(k * TILE, TILE)]
        copies.append(pltpu.make_async_copy(source, tiles.at[i], sems.at[i]))
    for copy in copies:
        copy.start()
    left = lane_ids(CH) < FACE
    first_core = lax.rem(lax.axis_index("dom"), 2) == 0
    for copy in copies:
        copy.wait()
    words = words_ref[...]
    occ_lo = occupancy_tile(words, 0)
    occ_hi = occupancy_tile(words, 3)
    for leaf in range(leaves):
        low, high = spread(occ_lo, leaf), spread(occ_hi, leaf)
        up = jnp.where(left, roll(tiles[3, leaf] * high, FACE), tiles[1, leaf] * high)
        down = jnp.where(left, tiles[0, leaf] * low, roll(tiles[2, leaf] * low, FACE))
        cross_ref[leaf] = jnp.where(first_core, down, up)
        chip_ref[leaf] = jnp.where(first_core, up, down)


def edges(words, x, dy):
    leaves = x.shape[0]
    shape = jax.ShapeDtypeStruct((leaves, CH, TILE), BF)
    return pl.pallas_call(
        edges_kernel,
        out_shape=(shape, shape),
        in_specs=[pl.BlockSpec(memory_space=pltpu.HBM)] * 3,
        out_specs=(vmem_spec(), vmem_spec()),
        scratch_shapes=[
            pltpu.VMEM(words.shape, jnp.int32),
            pltpu.VMEM((4, leaves, CH, TILE), BF),
            pltpu.SemaphoreType.DMA((5,)),
        ],
        cost_estimate=cost(10**6, 10**6),
        compiler_params=pltpu.CompilerParams(vmem_limit_bytes=EDGES_VMEM),
        name="edges",
    )(words, x, dy)


def fill(store, field_ref, occ, halo, turned):
    leaves = field_ref.shape[0]
    for leaf in range(leaves):
        for k in range(4):
            at = slice(k * TILE, (k + 1) * TILE)
            store[leaf, :, at] = field_ref[leaf, :, at] * spread(occ[k], leaf)
    if halo:
        cross_ref, chip_ref = halo
        first_core = lax.rem(lax.axis_index("dom"), 2) == 0
        for leaf in range(leaves):
            low = jnp.where(first_core, chip_ref[leaf], cross_ref[leaf])
            high = jnp.where(first_core, cross_ref[leaf], chip_ref[leaf])
            store[leaves + leaf, :, 0:TILE] = roll(low, FACE) if turned else low
            store[leaves + leaf, :, 3 * TILE : 4 * TILE] = roll(high, FACE) if turned else high
    store[store.shape[0] - 1] = jnp.zeros(store.shape[1:], BF)


def place(near_ref, leaf, p, q, z, device, leaves, which):
    if (p, q, z) == (0, 0, 0):
        return leaf
    ident = near_ref[leaf, column_of(p, q, z)]
    owner = ident // leaves
    slot = ident - owner * leaves
    absent = ident < 0
    if which == "all":
        slot = jnp.where(owner == device, slot, slot + leaves)
        return jnp.where(absent, 2 * leaves, slot)
    here = owner == device
    if which == "far":
        here = jnp.logical_not(here)
    return jnp.where(jnp.logical_and(here, jnp.logical_not(absent)), slot, leaves)


def moved_tiles(tiles):
    row_b = (lane_ids(CH) // EDGE) % EDGE
    first, last = row_b == 0, row_b == EDGE - 1
    return {
        -1: [
            jnp.where(first, roll(m, FACE + EDGE), roll(c, EDGE))
            for m, c in zip(tiles[-1], tiles[0])
        ],
        0: tiles[0],
        1: [
            jnp.where(last, roll(m, -FACE - EDGE), roll(c, -EDGE))
            for m, c in zip(tiles[1], tiles[0])
        ],
    }


def stacked(store, near_ref, leaf, z, device, leaves, which="all"):
    where = lambda p, q: place(near_ref, leaf, p, q, z, device, leaves, which)
    left = lane_ids(CH) < FACE
    tiles = {}
    for q in (-1, 0, 1):
        mid = where(0, q)
        tiles[q] = [store[mid, :, k * TILE : (k + 1) * TILE] for k in range(4)]
        after = store[where(1, q), :, 0:TILE]
        before = store[where(-1, q), :, 3 * TILE : 4 * TILE]
        tiles[q].append(jnp.where(left, after, before))
    moved = moved_tiles(tiles)
    swapped = {q: [roll(t, FACE) for t in moved[q]] for q in (-1, 0, 1)}

    def piece(p, q):
        if p == 0:
            parts = moved[q][:4]
        elif p == 1:
            parts = [jnp.where(left, swapped[q][k], swapped[q][k + 1]) for k in range(4)]
        else:
            parts = [jnp.where(left, swapped[q][(k - 1) % 5], swapped[q][k]) for k in range(4)]
        return jnp.concatenate(parts, axis=1)

    return jnp.concatenate([piece(p, q) for p, q in SHIFTS], axis=0)


def c_index():
    return lane_ids(CH) % EDGE


def shift_c(value, r):
    if r == 0:
        return value
    edge = c_index() == (EDGE - 1 if r > 0 else 0)
    zero = jnp.zeros((CH, TILE), value.dtype)
    parts = [
        jnp.where(edge, zero, roll(value[:, k * TILE : (k + 1) * TILE], -r)) for k in range(4)
    ]
    return jnp.concatenate(parts, axis=1)


def across_c(value, z):
    edge = c_index() == (EDGE - 1 if z > 0 else 0)
    zero = jnp.zeros((CH, TILE), value.dtype)
    parts = [
        jnp.where(edge, roll(value[:, k * TILE : (k + 1) * TILE], z * (EDGE - 1)), zero)
        for k in range(4)
    ]
    return jnp.concatenate(parts, axis=1)


def listed(near_ref, leaf, z):
    found = jnp.int32(-1)
    for p in (-1, 0, 1):
        for q in (-1, 0, 1):
            found = jnp.maximum(found, near_ref[leaf, column_of(p, q, z)])
    return found >= 0


def masked_field(field_ref, occ, leaf):
    return jnp.concatenate(
        [field_ref[leaf, :, k * TILE : (k + 1) * TILE] * spread(occ[k], leaf) for k in range(4)],
        axis=1,
    )


CONTRACT_LANES = (((1,), (1,)), ((), ()))


def dot_lanes(a, b):
    return lax.dot_general(a, b, CONTRACT_LANES, preferred_element_type=F32)


def grad_kernel(near_ref, words_ref, x_ref, d_ref, total, store):
    leaves = x_ref.shape[0]
    device = lax.axis_index("dom")
    words = words_ref[...]
    occ = [occupancy_tile(words, k) for k in range(4)]
    fill(store, x_ref, occ, None, False)
    for leaf in range(leaves):
        near_x = stacked(store, near_ref, leaf, 0, device, leaves, "near")
        center = masked_field(d_ref, occ, leaf)
        wide = jnp.concatenate([shift_c(center, -r) for r in (-1, 0, 1)], axis=0)
        term = dot_lanes(near_x, wide)
        if leaf == 0:
            total[...] = term
        else:
            total[...] += term

    for z in (-1, 1):
        for leaf in range(leaves):

            @pl.when(listed(near_ref, leaf, z))
            def _():
                near_x = stacked(store, near_ref, leaf, z, device, leaves, "near")
                edge = across_c(masked_field(d_ref, occ, leaf), -z)
                total[:, (z + 1) * CH : (z + 2) * CH] += dot_lanes(near_x, edge)


def grad_terms(near, words, x, dy):
    leaves = x.shape[0]
    return pl.pallas_call(
        grad_kernel,
        out_shape=jax.ShapeDtypeStruct((KROWS, 3 * CH), F32),
        in_specs=[smem_spec()] + [vmem_spec()] * 3,
        out_specs=vmem_spec(),
        scratch_shapes=[pltpu.VMEM((leaves + 1, CH, 4 * TILE), BF)],
        cost_estimate=cost(10**9, 2 * 10**6),
        compiler_params=params(),
        name="grad_terms",
    )(near, words, x, dy)


def grad_far_kernel(
    near_ref, words_ref, d_ref, cross_ref, chip_ref, near_total, keep_ref, send_ref, store, total, packed
):
    leaves = d_ref.shape[0]
    device = lax.axis_index("dom")
    first_core = lax.rem(device, 2) == 0
    words = words_ref[...]
    occ_lo, occ_hi = occupancy_tile(words, 0), occupancy_tile(words, 3)
    left = lane_ids(CH) < FACE
    zero = jnp.zeros((CH, TILE), BF)
    for leaf in range(leaves):
        low = jnp.where(first_core, chip_ref[leaf], cross_ref[leaf])
        high = jnp.where(first_core, cross_ref[leaf], chip_ref[leaf])
        store[leaf] = jnp.where(left, low, high)
    store[leaves] = zero

    def far_rows(leaf, z):
        where = lambda p, q: place(near_ref, leaf, p, q, z, device, leaves, "far")
        tiles = {q: [jnp.where(left, store[where(1, q)], store[where(-1, q)])] for q in (-1, 0, 1)}
        moved = moved_tiles(tiles)
        after = [jnp.where(left, moved[q][0], zero) for q in (-1, 0, 1)]
        before = [jnp.where(left, zero, moved[q][0]) for q in (-1, 0, 1)]
        return jnp.concatenate(after + before, axis=0)

    def end_planes(leaf):
        low = d_ref[leaf, :, 0:TILE] * spread(occ_lo, leaf)
        high = d_ref[leaf, :, 3 * TILE : 4 * TILE] * spread(occ_hi, leaf)
        return roll(jnp.where(left, low, high), FACE)

    def wide(leaf):
        plane = end_planes(leaf)
        cell = c_index()
        last = jnp.where(cell == EDGE - 1, zero, roll(plane, -1))
        first = jnp.where(cell == 0, zero, roll(plane, 1))
        return jnp.concatenate([last, plane, first], axis=0)

    rows = jnp.concatenate([far_rows(leaf, 0) for leaf in range(leaves)], axis=1)
    columns = jnp.concatenate([wide(leaf) for leaf in range(leaves)], axis=1)
    term = dot_lanes(rows, columns)
    total[...] = near_total[...]

    def add(part, at):
        for i, (p, q) in enumerate([(p, q) for p in (1, -1) for q in (-1, 0, 1)]):
            row = SHIFTS.index((p, q)) * CH
            total[row : row + CH, at] += part[i * CH : (i + 1) * CH, :]

    add(term, slice(0, 3 * CH))
    for z in (-1, 1):
        for leaf in range(leaves):

            @pl.when(listed(near_ref, leaf, z))
            def _():
                plane = end_planes(leaf)
                edge = c_index() == (0 if z > 0 else EDGE - 1)
                edge = jnp.where(edge, roll(plane, -z * (EDGE - 1)), zero)
                add(dot_lanes(far_rows(leaf, z), edge), slice((z + 1) * CH, (z + 2) * CH))

    packed[0:KROWS, :] = total[:, 0:TILE]
    packed[KROWS:, 0:CH] = total[0:SPLIT, TILE:]
    packed[KROWS : 2 * KROWS - SPLIT, CH:] = total[SPLIT:, TILE:]
    packed[2 * KROWS - SPLIT :, CH:] = jnp.zeros((2 * SPLIT - KROWS, CH), F32)
    core = lax.rem(device, 2)
    rows = packed.shape[0] // 2
    keep_ref[...] = packed[pl.ds(pl.multiple_of(core * rows, 8), rows), :]
    send_ref[...] = packed[pl.ds(pl.multiple_of((1 - core) * rows, 8), rows), :]


def grad_far(near, words, dy, cross, chip, total):
    leaves = dy.shape[0]
    rows = KROWS + SPLIT
    shape = jax.ShapeDtypeStruct((rows // 2, TILE), F32)
    return pl.pallas_call(
        grad_far_kernel,
        out_shape=(shape, shape),
        in_specs=[smem_spec()] + [vmem_spec()] * 5,
        out_specs=(vmem_spec(), vmem_spec()),
        scratch_shapes=[
            pltpu.VMEM((leaves + 1, CH, TILE), BF),
            pltpu.VMEM((KROWS, 3 * CH), F32),
            pltpu.VMEM((rows, TILE), F32),
        ],
        cost_estimate=cost(10**8, 2 * 10**6),
        compiler_params=params(),
        name="grad_far",
    )(near, words, dy, cross, chip, total)


def vmem_spec():
    return pl.BlockSpec(memory_space=pltpu.VMEM)


def any_spec():
    return pl.BlockSpec(memory_space=pl.ANY)


def smem_spec():
    return pl.BlockSpec(memory_space=pltpu.SMEM)


def params():
    return pltpu.CompilerParams(vmem_limit_bytes=VMEM_LIMIT)


def cost(flops, bytes_accessed):
    return pl.CostEstimate(flops=flops, bytes_accessed=bytes_accessed, transcendentals=0)


def conv_kernel(
    turned, near_ref, words_ref, x_ref, cross_ref, chip_ref, w_ref, _, out_ref, done_ref, store
):
    leaves = x_ref.shape[0]
    device = lax.axis_index("dom")
    words = words_ref[...]
    occ = [occupancy_tile(words, k) for k in range(4)]
    fill(store, x_ref, occ, (cross_ref, chip_ref), turned)

    def tap(index, r):
        p, q = SHIFTS[index]
        return (p + 1) * 9 + (q + 1) * 3 + r + 1

    if turned:
        taps = jnp.concatenate(
            [
                jnp.concatenate([w_ref[26 - tap(index, r)] for index in range(9)], axis=1)
                for r in (-1, 0, 1)
            ],
            axis=0,
        )
    else:
        taps = jnp.concatenate(
            [
                jnp.concatenate([w_ref[tap(index, r)] for r in (-1, 0, 1)], axis=1)
                for index in range(9)
            ],
            axis=0,
        ).T
    done_ref[...] = jnp.zeros(done_ref.shape, F32)

    def masked(leaf, value):
        return jnp.concatenate(
            [
                value[:, k * TILE : (k + 1) * TILE]
                * jnp.broadcast_to(occ[k][leaf : leaf + 1, :], (CH, TILE))
                for k in range(4)
            ],
            axis=1,
        )

    for leaf in range(leaves):
        near_x = stacked(store, near_ref, leaf, 0, device, leaves)
        wide = jnp.dot(taps, near_x, preferred_element_type=F32)
        total = wide[CH : 2 * CH]
        for r in (-1, 1):
            total = total + shift_c(wide[(r + 1) * CH : (r + 2) * CH], r)
        out_ref[leaf] = masked(leaf, total).astype(BF)

    for leaf in range(leaves):

        @pl.when(listed(near_ref, leaf, -1) | listed(near_ref, leaf, 1))
        def _():
            near_x = stacked(store, near_ref, leaf, 0, device, leaves)
            wide = jnp.dot(taps, near_x, preferred_element_type=F32)
            total = wide[CH : 2 * CH]
            for r in (-1, 1):
                total = total + shift_c(wide[(r + 1) * CH : (r + 2) * CH], r)
            for z in (-1, 1):
                near_z = stacked(store, near_ref, leaf, z, device, leaves)
                part = jnp.dot(
                    taps[(z + 1) * CH : (z + 2) * CH], near_z, preferred_element_type=F32
                )
                total = total + across_c(part, z)
            out_ref[leaf] = masked(leaf, total).astype(BF)


def conv(near, words, x, cross, chip, weight, after, turned):
    leaves = x.shape[0]
    return pl.pallas_call(
        functools.partial(conv_kernel, turned),
        out_shape=(jax.ShapeDtypeStruct(x.shape, BF), jax.ShapeDtypeStruct((8, TILE), F32)),
        in_specs=[smem_spec()] + [vmem_spec()] * 5 + [any_spec()],
        out_specs=(vmem_spec(), vmem_spec()),
        scratch_shapes=[pltpu.VMEM((2 * leaves + 1, CH, 4 * TILE), BF)],
        cost_estimate=cost(2 * 10**9, 2 * 10**6),
        compiler_params=params(),
        name="in_grad_conv" if turned else "out_conv",
    )(near, words, x, cross, chip, weight, after)


def sum_kernel(parts_ref, _, out_ref):
    parts = parts_ref.shape[0]
    total = parts_ref[0]
    for i in range(1, parts):
        total = total + parts_ref[i]
    for i in range(parts):
        out_ref[i] = total


def sum_chunks(parts, after):
    return pl.pallas_call(
        sum_kernel,
        out_shape=jax.ShapeDtypeStruct(parts.shape, F32),
        in_specs=[vmem_spec(), any_spec()],
        out_specs=vmem_spec(),
        cost_estimate=cost(10**5, 5 * 10**5),
        compiler_params=params(),
        name="sum_chunks",
    )(parts, after)


def unpack_kernel(scale, own_ref, other_ref, out_ref, total):
    core = lax.rem(lax.axis_index("dom"), 2)
    rows = own_ref.shape[0]
    total[pl.ds(pl.multiple_of(core * rows, 8), rows), :] = own_ref[...] * scale
    total[pl.ds(pl.multiple_of((1 - core) * rows, 8), rows), :] = other_ref[...] * scale
    for index, (p, q) in enumerate(SHIFTS):
        for r in (-1, 0, 1):
            tap = (p + 1) * 9 + (q + 1) * 3 + r + 1
            row, side = index * CH, r + 1
            if r == 1:
                row, side = (KROWS + row, 0) if row < SPLIT else (KROWS + row - SPLIT, 1)
            out_ref[tap] = total[row : row + CH, side * CH : (side + 1) * CH]


def unpack(own, other, scale):
    return pl.pallas_call(
        functools.partial(unpack_kernel, scale),
        out_shape=jax.ShapeDtypeStruct((27, CH, CH), F32),
        in_specs=[vmem_spec(), vmem_spec()],
        out_specs=vmem_spec(),
        scratch_shapes=[pltpu.VMEM((2 * own.shape[0], TILE), F32)],
        cost_estimate=cost(10**6, 10**6),
        compiler_params=params(),
        name="unpack_grad",
    )(own, other)


def exchange(array, mask, size):
    return lax.ppermute(array, "dom", [(i, i ^ mask) for i in range(size)])


def shards(features, cotangent, weight, mask_words, neighbors):
    leaves, channels, voxels = features.shape
    size = lax.axis_size("dom")
    device = lax.axis_index("dom")
    to_cross, to_chip = edges(mask_words, features, cotangent)
    between = [(i, i + 1) for i in range(1, size - 1, 2)]
    cross = lax.ppermute(to_cross, "dom", between + [(j, i) for i, j in between])
    chip = exchange(to_chip, 1, size)

    total = grad_terms(neighbors, mask_words, features, cotangent)
    keep, send = grad_far(neighbors, mask_words, cotangent, cross, chip, total)
    keep = (keep + exchange(send, 1, size)).reshape(4, -1, TILE)
    line = [
        [b + c + 2 * j for j in range(4)] for b in range(0, size, GROUP) for c in range(2)
    ]
    swap = lambda parts: lax.all_to_all(parts, "dom", 0, 0, axis_index_groups=line)
    got = swap(keep)
    out_features, out_done = conv(
        neighbors, mask_words, features, cross, chip, weight, keep, False
    )
    own = sum_chunks(got, out_done)
    if size > GROUP:
        groups = [[j * GROUP + i for j in range(size // GROUP)] for i in range(GROUP)]
        own = lax.psum(own, "dom", axis_index_groups=groups)
    back = swap(own)
    in_grad, in_done = conv(neighbors, mask_words, cotangent, cross, chip, weight, own, True)
    half = back.reshape(-1, TILE) + in_done[:1]
    other = exchange(half, 1, size)
    scale = float(size * leaves * voxels) ** -0.5
    return (out_features, in_grad, unpack(half, other, scale))


def solution(mesh):
    split = P(("scene", "dom"), None, None)
    flat = P(("scene", "dom"), None)
    return jax.shard_map(
        shards,
        mesh=mesh,
        in_specs=(split, split, P(), flat, flat),
        out_specs=(split, split, P("scene", None, None)),
        check_vma=False,
    )
```

```python
import functools

import jax
import jax.numpy as jnp
from jax import lax
from jax.experimental import pallas as pl
from jax.experimental.pallas import tpu as pltpu
from jax.sharding import PartitionSpec as P

BITS = 30
EDGE = 8
FACE = EDGE * EDGE
TILE = 128
CH = 64
GROUP = 8
KROWS = 9 * CH
SPLIT = 5 * CH
VMEM_LIMIT = 40 * 1024 * 1024
EDGES_VMEM = 63000000
BF = jnp.bfloat16
F32 = jnp.float32


def column_of(p, q, r):
    tap = (p + 1) * 9 + (q + 1) * 3 + r + 1
    return tap if tap < 13 else tap - 1


SHIFTS = [(p, q) for p in (-1, 0, 1) for q in (-1, 0)] + [(p, 1) for p in (-1, 0, 1)]


def lane_ids(rows):
    return lax.broadcasted_iota(jnp.int32, (rows, TILE), 1)


def occupancy_tile(words, tile):
    lane = lane_ids(words.shape[0]) + tile * TILE
    first, last = (tile * TILE) // BITS, (tile * TILE + TILE - 1) // BITS
    word = jnp.broadcast_to(words[:, first : first + 1], lane.shape)
    place = lane - first * BITS
    for w in range(first + 1, last + 1):
        past = lane >= w * BITS
        word = jnp.where(past, jnp.broadcast_to(words[:, w : w + 1], lane.shape), word)
        place = jnp.where(past, lane - w * BITS, place)
    return (jnp.right_shift(word, place) & 1).astype(F32)


def spread(occ, leaf):
    return jnp.broadcast_to(occ[leaf : leaf + 1, :], (CH, TILE)).astype(BF)


def roll(value, amount):
    return pltpu.roll(value, amount % TILE, 1)


def edges_kernel(words_hbm, x_hbm, d_hbm, cross_ref, chip_ref, words_ref, tiles, sems):
    leaves = x_hbm.shape[0]
    copies = [pltpu.make_async_copy(words_hbm, words_ref, sems.at[4])]
    for i, (field, k) in enumerate(((x_hbm, 0), (x_hbm, 3), (d_hbm, 0), (d_hbm, 3))):
        source = field.at[:, :, pl.ds(k * TILE, TILE)]
        copies.append(pltpu.make_async_copy(source, tiles.at[i], sems.at[i]))
    for copy in copies:
        copy.start()
    left = lane_ids(CH) < FACE
    first_core = lax.rem(lax.axis_index("dom"), 2) == 0
    for copy in copies:
        copy.wait()
    words = words_ref[...]
    occ_lo = occupancy_tile(words, 0)
    occ_hi = occupancy_tile(words, 3)
    for leaf in range(leaves):
        low, high = spread(occ_lo, leaf), spread(occ_hi, leaf)
        up = jnp.where(left, roll(tiles[3, leaf] * high, FACE), tiles[1, leaf] * high)
        down = jnp.where(left, tiles[0, leaf] * low, roll(tiles[2, leaf] * low, FACE))
        cross_ref[leaf] = jnp.where(first_core, down, up)
        chip_ref[leaf] = jnp.where(first_core, up, down)


def edges(words, x, dy):
    leaves = x.shape[0]
    shape = jax.ShapeDtypeStruct((leaves, CH, TILE), BF)
    return pl.pallas_call(
        edges_kernel,
        out_shape=(shape, shape),
        in_specs=[pl.BlockSpec(memory_space=pltpu.HBM)] * 3,
        out_specs=(vmem_spec(), vmem_spec()),
        scratch_shapes=[
            pltpu.VMEM(words.shape, jnp.int32),
            pltpu.VMEM((4, leaves, CH, TILE), BF),
            pltpu.SemaphoreType.DMA((5,)),
        ],
        cost_estimate=cost(10**6, 10**6),
        compiler_params=pltpu.CompilerParams(vmem_limit_bytes=EDGES_VMEM),
        name="edges",
    )(words, x, dy)


def fill(store, field_ref, occ, halo, turned):
    leaves = field_ref.shape[0]
    for leaf in range(leaves):
        for k in range(4):
            at = slice(k * TILE, (k + 1) * TILE)
            store[leaf, :, at] = field_ref[leaf, :, at] * spread(occ[k], leaf)
    if halo:
        cross_ref, chip_ref = halo
        first_core = lax.rem(lax.axis_index("dom"), 2) == 0
        for leaf in range(leaves):
            low = jnp.where(first_core, chip_ref[leaf], cross_ref[leaf])
            high = jnp.where(first_core, cross_ref[leaf], chip_ref[leaf])
            store[leaves + leaf, :, 0:TILE] = roll(low, FACE) if turned else low
            store[leaves + leaf, :, 3 * TILE : 4 * TILE] = roll(high, FACE) if turned else high
    store[store.shape[0] - 1] = jnp.zeros(store.shape[1:], BF)


def place(near_ref, leaf, p, q, z, device, leaves, which):
    if (p, q, z) == (0, 0, 0):
        return leaf
    ident = near_ref[leaf, column_of(p, q, z)]
    owner = ident // leaves
    slot = ident - owner * leaves
    absent = ident < 0
    if which == "all":
        slot = jnp.where(owner == device, slot, slot + leaves)
        return jnp.where(absent, 2 * leaves, slot)
    here = owner == device
    if which == "far":
        here = jnp.logical_not(here)
    return jnp.where(jnp.logical_and(here, jnp.logical_not(absent)), slot, leaves)


def moved_tiles(tiles):
    row_b = (lane_ids(CH) // EDGE) % EDGE
    first, last = row_b == 0, row_b == EDGE - 1
    return {
        -1: [
            jnp.where(first, roll(m, FACE + EDGE), roll(c, EDGE))
            for m, c in zip(tiles[-1], tiles[0])
        ],
        0: tiles[0],
        1: [
            jnp.where(last, roll(m, -FACE - EDGE), roll(c, -EDGE))
            for m, c in zip(tiles[1], tiles[0])
        ],
    }


def stacked(store, near_ref, leaf, z, device, leaves, which="all"):
    where = lambda p, q: place(near_ref, leaf, p, q, z, device, leaves, which)
    left = lane_ids(CH) < FACE
    tiles = {}
    for q in (-1, 0, 1):
        mid = where(0, q)
        tiles[q] = [store[mid, :, k * TILE : (k + 1) * TILE] for k in range(4)]
        after = store[where(1, q), :, 0:TILE]
        before = store[where(-1, q), :, 3 * TILE : 4 * TILE]
        tiles[q].append(jnp.where(left, after, before))
    moved = moved_tiles(tiles)
    swapped = {q: [roll(t, FACE) for t in moved[q]] for q in (-1, 0, 1)}

    def piece(p, q):
        if p == 0:
            parts = moved[q][:4]
        elif p == 1:
            parts = [jnp.where(left, swapped[q][k], swapped[q][k + 1]) for k in range(4)]
        else:
            parts = [jnp.where(left, swapped[q][(k - 1) % 5], swapped[q][k]) for k in range(4)]
        return jnp.concatenate(parts, axis=1)

    return jnp.concatenate([piece(p, q) for p, q in SHIFTS], axis=0)


def c_index():
    return lane_ids(CH) % EDGE


def shift_c(value, r):
    if r == 0:
        return value
    edge = c_index() == (EDGE - 1 if r > 0 else 0)
    zero = jnp.zeros((CH, TILE), value.dtype)
    parts = [
        jnp.where(edge, zero, roll(value[:, k * TILE : (k + 1) * TILE], -r)) for k in range(4)
    ]
    return jnp.concatenate(parts, axis=1)


def across_c(value, z):
    edge = c_index() == (EDGE - 1 if z > 0 else 0)
    zero = jnp.zeros((CH, TILE), value.dtype)
    parts = [
        jnp.where(edge, roll(value[:, k * TILE : (k + 1) * TILE], z * (EDGE - 1)), zero)
        for k in range(4)
    ]
    return jnp.concatenate(parts, axis=1)


def listed(near_ref, leaf, z):
    found = jnp.int32(-1)
    for p in (-1, 0, 1):
        for q in (-1, 0, 1):
            found = jnp.maximum(found, near_ref[leaf, column_of(p, q, z)])
    return found >= 0


def masked_field(field_ref, occ, leaf):
    return jnp.concatenate(
        [field_ref[leaf, :, k * TILE : (k + 1) * TILE] * spread(occ[k], leaf) for k in range(4)],
        axis=1,
    )


CONTRACT_LANES = (((1,), (1,)), ((), ()))


def dot_lanes(a, b):
    return lax.dot_general(a, b, CONTRACT_LANES, preferred_element_type=F32)


def grad_kernel(near_ref, words_ref, x_ref, d_ref, total, stack_ref, store):
    leaves = x_ref.shape[0]
    device = lax.axis_index("dom")
    words = words_ref[...]
    occ = [occupancy_tile(words, k) for k in range(4)]
    fill(store, x_ref, occ, None, False)
    for leaf in range(leaves):
        near_x = stacked(store, near_ref, leaf, 0, device, leaves, "near")
        stack_ref[leaf] = near_x
        center = masked_field(d_ref, occ, leaf)
        wide = jnp.concatenate([shift_c(center, -r) for r in (-1, 0, 1)], axis=0)
        term = dot_lanes(near_x, wide)
        if leaf == 0:
            total[...] = term
        else:
            total[...] += term

    for z in (-1, 1):
        for leaf in range(leaves):

            @pl.when(listed(near_ref, leaf, z))
            def _():
                near_x = stacked(store, near_ref, leaf, z, device, leaves, "near")
                edge = across_c(masked_field(d_ref, occ, leaf), -z)
                total[:, (z + 1) * CH : (z + 2) * CH] += dot_lanes(near_x, edge)


def grad_terms(near, words, x, dy):
    leaves = x.shape[0]
    return pl.pallas_call(
        grad_kernel,
        out_shape=(
            jax.ShapeDtypeStruct((KROWS, 3 * CH), F32),
            jax.ShapeDtypeStruct((leaves, KROWS, 4 * TILE), BF),
        ),
        in_specs=[smem_spec()] + [vmem_spec()] * 3,
        out_specs=(vmem_spec(), vmem_spec()),
        scratch_shapes=[pltpu.VMEM((leaves + 1, CH, 4 * TILE), BF)],
        cost_estimate=cost(10**9, 2 * 10**6),
        compiler_params=params(),
        name="grad_terms",
    )(near, words, x, dy)


def split_far(cross_ref, chip_ref, leaf):
    first_core = lax.rem(lax.axis_index("dom"), 2) == 0
    low = jnp.where(first_core, chip_ref[leaf], cross_ref[leaf])
    high = jnp.where(first_core, cross_ref[leaf], chip_ref[leaf])
    return low, high


def grad_far_kernel(
    near_ref, words_ref, d_ref, cross_ref, chip_ref, near_total, keep_ref, send_ref, store, packed
):
    leaves = d_ref.shape[0]
    device = lax.axis_index("dom")
    words = words_ref[...]
    occ_lo, occ_hi = occupancy_tile(words, 0), occupancy_tile(words, 3)
    left = lane_ids(CH) < FACE
    zero = jnp.zeros((CH, TILE), BF)
    for leaf in range(leaves):
        low, high = split_far(cross_ref, chip_ref, leaf)
        store[0, leaf], store[1, leaf] = low, high
        store[2, leaf], store[3, leaf] = roll(low, FACE), roll(high, FACE)
    for i in range(4):
        store[i, leaves] = zero

    def far_rows(p, one, two, z):
        at = lambda leaf, q: place(near_ref, leaf, p, q, z, device, leaves, "far")
        first, second = (0, 2) if p > 0 else (3, 1)
        tiles = {
            q: [jnp.where(left, store[first, at(one, q)], store[second, at(two, q)])]
            for q in (-1, 0, 1)
        }
        moved = moved_tiles(tiles)
        return jnp.concatenate([moved[q][0] for q in (-1, 0, 1)], axis=0)

    def end_plane(p, one, two):
        if p > 0:
            a, b = [d_ref[l, :, 3 * TILE :] * spread(occ_hi, l) for l in (one, two)]
            return jnp.where(left, roll(a, FACE), b)
        a, b = [d_ref[l, :, 0:TILE] * spread(occ_lo, l) for l in (one, two)]
        return jnp.where(left, a, roll(b, FACE))

    def wide(plane):
        cell = c_index()
        last = jnp.where(cell == EDGE - 1, zero, roll(plane, -1))
        first = jnp.where(cell == 0, zero, roll(plane, 1))
        return jnp.concatenate([last, plane, first], axis=0)

    pairs = [(leaf, leaf + 1) for leaf in range(0, leaves, 2)]
    for index, (p, q) in enumerate(SHIFTS):
        if p == 0:
            row = index * CH
            packed[row : row + CH, :] = near_total[row : row + CH, 0:TILE]
            far, side = (KROWS + row, 0) if row < SPLIT else (KROWS + row - SPLIT, 1)
            packed[far : far + CH, side * CH : (side + 1) * CH] = near_total[row : row + CH, TILE:]
    for p in (-1, 1):
        rows = jnp.concatenate([far_rows(p, a, b, 0) for a, b in pairs], axis=1)
        columns = jnp.concatenate([wide(end_plane(p, a, b)) for a, b in pairs], axis=1)
        term = dot_lanes(rows, columns)
        for q in (-1, 0, 1):
            row = SHIFTS.index((p, q)) * CH
            block = near_total[row : row + CH, :] + term[(q + 1) * CH : (q + 2) * CH, :]
            packed[row : row + CH, :] = block[:, 0:TILE]
            far, side = (KROWS + row, 0) if row < SPLIT else (KROWS + row - SPLIT, 1)
            packed[far : far + CH, side * CH : (side + 1) * CH] = block[:, TILE:]
    packed[2 * KROWS - SPLIT :, CH:] = jnp.zeros((2 * SPLIT - KROWS, CH), F32)

    for z in (-1, 1):
        for leaf in range(leaves):

            @pl.when(listed(near_ref, leaf, z))
            def _():
                edge = c_index() == (0 if z > 0 else EDGE - 1)
                for p in (-1, 1):
                    plane = jnp.where(left, end_plane(p, leaf, leaf), zero)
                    plane = jnp.where(edge, roll(plane, -z * (EDGE - 1)), zero)
                    term = dot_lanes(far_rows(p, leaf, leaf, z), plane)
                    for q in (-1, 0, 1):
                        row, side = SHIFTS.index((p, q)) * CH, 0
                        if z > 0:
                            row, side = (
                                (KROWS + row, 0) if row < SPLIT else (KROWS + row - SPLIT, 1)
                            )
                        packed[row : row + CH, side * CH : (side + 1) * CH] += term[
                            (q + 1) * CH : (q + 2) * CH, :
                        ]

    core = lax.rem(device, 2)
    rows = packed.shape[0] // 2
    keep_ref[...] = packed[pl.ds(pl.multiple_of(core * rows, 8), rows), :]
    send_ref[...] = packed[pl.ds(pl.multiple_of((1 - core) * rows, 8), rows), :]


def grad_far(near, words, dy, cross, chip, total):
    leaves = dy.shape[0]
    rows = KROWS + SPLIT
    shape = jax.ShapeDtypeStruct((rows // 2, TILE), F32)
    return pl.pallas_call(
        grad_far_kernel,
        out_shape=(shape, shape),
        in_specs=[smem_spec()] + [vmem_spec()] * 5,
        out_specs=(vmem_spec(), vmem_spec()),
        scratch_shapes=[
            pltpu.VMEM((4, leaves + 1, CH, TILE), BF),
            pltpu.VMEM((rows, TILE), F32),
        ],
        cost_estimate=cost(10**8, 2 * 10**6),
        compiler_params=params(),
        name="grad_far",
    )(near, words, dy, cross, chip, total)


def vmem_spec():
    return pl.BlockSpec(memory_space=pltpu.VMEM)


def any_spec():
    return pl.BlockSpec(memory_space=pl.ANY)


def smem_spec():
    return pl.BlockSpec(memory_space=pltpu.SMEM)


def params():
    return pltpu.CompilerParams(vmem_limit_bytes=VMEM_LIMIT)


def cost(flops, bytes_accessed):
    return pl.CostEstimate(flops=flops, bytes_accessed=bytes_accessed, transcendentals=0)


def ordered_taps(w_ref, turned):
    def tap(index, r):
        p, q = SHIFTS[index]
        return (p + 1) * 9 + (q + 1) * 3 + r + 1

    if turned:
        return jnp.concatenate(
            [
                jnp.concatenate([w_ref[26 - tap(index, r)] for index in range(9)], axis=1)
                for r in (-1, 0, 1)
            ],
            axis=0,
        )
    return jnp.concatenate(
        [
            jnp.concatenate([w_ref[tap(index, r)] for r in (-1, 0, 1)], axis=1)
            for index in range(9)
        ],
        axis=0,
    ).T


def masked_sum(occ, leaf, value):
    return jnp.concatenate(
        [
            value[:, k * TILE : (k + 1) * TILE]
            * jnp.broadcast_to(occ[k][leaf : leaf + 1, :], (CH, TILE))
            for k in range(4)
        ],
        axis=1,
    ).astype(BF)


def leaf_sum(taps, near_x):
    wide = jnp.dot(taps, near_x, preferred_element_type=F32)
    total = wide[CH : 2 * CH]
    for r in (-1, 1):
        total = total + shift_c(wide[(r + 1) * CH : (r + 2) * CH], r)
    return total


def third_dimension(near_ref, taps, occ, x_ref, cross_ref, chip_ref, turned, out_ref, store):
    leaves = x_ref.shape[0]
    device = lax.axis_index("dom")
    found = [listed(near_ref, leaf, -1) | listed(near_ref, leaf, 1) for leaf in range(leaves)]

    @pl.when(functools.reduce(jnp.logical_or, found))
    def _():
        fill(store, x_ref, occ, (cross_ref, chip_ref), turned)

        def one(leaf, carry):
            near_x = stacked(store, near_ref, leaf, 0, device, leaves)
            total = leaf_sum(taps, near_x)
            for z in (-1, 1):
                near_z = stacked(store, near_ref, leaf, z, device, leaves)
                part = jnp.dot(
                    taps[(z + 1) * CH : (z + 2) * CH], near_z, preferred_element_type=F32
                )
                total = total + across_c(part, z)
            out_ref[leaf] = masked_sum(occ, leaf, total)
            return carry

        for leaf in range(leaves):
            one(leaf, 0)


def out_kernel(
    near_ref, words_ref, x_ref, d_ref, cross_ref, chip_ref, w_ref, stack_ref, _,
    out_ref, stack_dy_ref, done_ref, store, far,
):
    leaves = x_ref.shape[0]
    device = lax.axis_index("dom")
    words = words_ref[...]
    occ = [occupancy_tile(words, k) for k in range(4)]
    done_ref[...] = jnp.zeros(done_ref.shape, F32)
    left = lane_ids(CH) < FACE
    zero = jnp.zeros((CH, TILE), BF)
    taps = ordered_taps(w_ref, False)
    fill(store, d_ref, occ, (cross_ref, chip_ref), True)
    for leaf in range(leaves):
        low, high = split_far(cross_ref, chip_ref, leaf)
        far[leaf] = jnp.where(left, low, high)
    far[leaves] = zero

    def far_planes(leaf):
        at = lambda p, q: place(near_ref, leaf, p, q, 0, device, leaves, "far")
        tiles = {q: [jnp.where(left, far[at(1, q)], far[at(-1, q)])] for q in (-1, 0, 1)}
        moved = moved_tiles(tiles)
        return {q: roll(moved[q][0], FACE) for q in (-1, 0, 1)}

    for leaf in range(leaves):
        stack_dy_ref[leaf] = stacked(store, near_ref, leaf, 0, device, leaves)
        planes = far_planes(leaf)
        pieces = []
        for index, (p, q) in enumerate(SHIFTS):
            piece = stack_ref[leaf, index * CH : (index + 1) * CH, :]
            parts = [piece[:, k * TILE : (k + 1) * TILE] for k in range(4)]
            if p > 0:
                parts[3] = parts[3] + jnp.where(left, zero, planes[q])
            elif p < 0:
                parts[0] = parts[0] + jnp.where(left, planes[q], zero)
            pieces.append(jnp.concatenate(parts, axis=1))
        total = leaf_sum(taps, jnp.concatenate(pieces, axis=0))
        out_ref[leaf] = masked_sum(occ, leaf, total)
    third_dimension(near_ref, taps, occ, x_ref, cross_ref, chip_ref, False, out_ref, store)


def out_conv(near, words, x, dy, cross, chip, weight, stack, after):
    leaves = x.shape[0]
    return pl.pallas_call(
        out_kernel,
        out_shape=(
            jax.ShapeDtypeStruct(x.shape, BF),
            jax.ShapeDtypeStruct(stack.shape, BF),
            jax.ShapeDtypeStruct((8, TILE), F32),
        ),
        in_specs=[smem_spec()] + [vmem_spec()] * 7 + [any_spec()],
        out_specs=(vmem_spec(),) * 3,
        scratch_shapes=[
            pltpu.VMEM((2 * leaves + 1, CH, 4 * TILE), BF),
            pltpu.VMEM((leaves + 1, CH, TILE), BF),
        ],
        cost_estimate=cost(10**9, 2 * 10**6),
        compiler_params=params(),
        name="out_conv",
    )(near, words, x, dy, cross, chip, weight, stack, after)


def in_grad_kernel(
    near_ref, words_ref, d_ref, cross_ref, chip_ref, w_ref, stack_ref, _, out_ref, done_ref, store
):
    leaves = d_ref.shape[0]
    words = words_ref[...]
    occ = [occupancy_tile(words, k) for k in range(4)]
    done_ref[...] = jnp.zeros(done_ref.shape, F32)
    taps = ordered_taps(w_ref, True)
    for leaf in range(leaves):
        out_ref[leaf] = masked_sum(occ, leaf, leaf_sum(taps, stack_ref[leaf]))
    third_dimension(near_ref, taps, occ, d_ref, cross_ref, chip_ref, True, out_ref, store)


def in_grad_conv(near, words, dy, cross, chip, weight, stack, after):
    leaves = dy.shape[0]
    return pl.pallas_call(
        in_grad_kernel,
        out_shape=(jax.ShapeDtypeStruct(dy.shape, BF), jax.ShapeDtypeStruct((8, TILE), F32)),
        in_specs=[smem_spec()] + [vmem_spec()] * 6 + [any_spec()],
        out_specs=(vmem_spec(),) * 2,
        scratch_shapes=[pltpu.VMEM((2 * leaves + 1, CH, 4 * TILE), BF)],
        cost_estimate=cost(10**9, 2 * 10**6),
        compiler_params=params(),
        name="in_grad_conv",
    )(near, words, dy, cross, chip, weight, stack, after)


def sum_kernel(own_ref, *refs):
    *got_refs, _, out_ref = refs
    total = own_ref[...]
    for got_ref in got_refs:
        total = total + got_ref[...]
    out_ref[...] = total


def sum_chunks(own, got, after):
    return pl.pallas_call(
        sum_kernel,
        out_shape=jax.ShapeDtypeStruct(own.shape, F32),
        in_specs=[vmem_spec()] * (1 + len(got)) + [any_spec()],
        out_specs=vmem_spec(),
        cost_estimate=cost(10**5, 3 * 10**5),
        compiler_params=params(),
        name="sum_chunks",
    )(own, *got, after)


def join_kernel(*refs):
    *parts, _, out_ref = refs
    lane = lax.rem(lax.axis_index("dom") // 2, 4)
    rows = parts[0].shape[0]
    for mask, part in enumerate(parts):
        at = pl.multiple_of(jnp.bitwise_xor(lane, mask) * rows, 8)
        out_ref[pl.ds(at, rows), :] = part[...]


def join_chunks(parts, after):
    rows = parts[0].shape[0]
    return pl.pallas_call(
        join_kernel,
        out_shape=jax.ShapeDtypeStruct((len(parts) * rows, TILE), F32),
        in_specs=[vmem_spec()] * len(parts) + [any_spec()],
        out_specs=vmem_spec(),
        cost_estimate=cost(10**5, 5 * 10**5),
        compiler_params=params(),
        name="join_chunks",
    )(*parts, after)


def unpack_kernel(scale, own_ref, other_ref, out_ref, total):
    core = lax.rem(lax.axis_index("dom"), 2)
    rows = own_ref.shape[0]
    total[pl.ds(pl.multiple_of(core * rows, 8), rows), :] = own_ref[...] * scale
    total[pl.ds(pl.multiple_of((1 - core) * rows, 8), rows), :] = other_ref[...] * scale
    for index, (p, q) in enumerate(SHIFTS):
        for r in (-1, 0, 1):
            tap = (p + 1) * 9 + (q + 1) * 3 + r + 1
            row, side = index * CH, r + 1
            if r == 1:
                row, side = (KROWS + row, 0) if row < SPLIT else (KROWS + row - SPLIT, 1)
            out_ref[tap] = total[row : row + CH, side * CH : (side + 1) * CH]


def unpack(own, other, scale):
    return pl.pallas_call(
        functools.partial(unpack_kernel, scale),
        out_shape=jax.ShapeDtypeStruct((27, CH, CH), F32),
        in_specs=[vmem_spec(), vmem_spec()],
        out_specs=vmem_spec(),
        scratch_shapes=[pltpu.VMEM((2 * own.shape[0], TILE), F32)],
        cost_estimate=cost(10**6, 10**6),
        compiler_params=params(),
        name="unpack_grad",
    )(own, other)


def exchange(array, mask, size):
    return lax.ppermute(array, "dom", [(i, i ^ mask) for i in range(size)])


def shards(features, cotangent, weight, mask_words, neighbors):
    leaves, channels, voxels = features.shape
    size = lax.axis_size("dom")
    device = lax.axis_index("dom")
    to_cross, to_chip = edges(mask_words, features, cotangent)
    between = [(i, i + 1) for i in range(1, size - 1, 2)]
    cross = lax.ppermute(to_cross, "dom", between + [(j, i) for i, j in between])
    chip = exchange(to_chip, 1, size)

    total, stack = grad_terms(neighbors, mask_words, features, cotangent)
    keep, send = grad_far(neighbors, mask_words, cotangent, cross, chip, total)
    keep = keep + exchange(send, 1, size)
    rows = keep.shape[0] // 4
    lane = (device // 2) % 4
    chunk = lambda index: lax.dynamic_slice_in_dim(keep, index * rows, rows, axis=0)
    to_send = [chunk(lane ^ m) for m in (1, 2, 3)]
    own = chunk(lane)
    got = [exchange(part, 2 * m, size) for m, part in zip((1, 2, 3), to_send)]
    out_features, stack_dy, out_done = out_conv(
        neighbors, mask_words, features, cotangent, cross, chip, weight, stack, to_send[2]
    )
    own = sum_chunks(own, got, out_done)
    if size > GROUP:
        groups = [[j * GROUP + i for j in range(size // GROUP)] for i in range(GROUP)]
        own = lax.psum(own, "dom", axis_index_groups=groups)
    back = [exchange(own, 2 * m, size) for m in (1, 2, 3)]
    in_grad, in_done = in_grad_conv(
        neighbors, mask_words, cotangent, cross, chip, weight, stack_dy, own
    )
    half = join_chunks([own] + back, in_done)
    other = exchange(half, 1, size)
    scale = float(size * leaves * voxels) ** -0.5
    return (out_features, in_grad, unpack(half, other, scale))


def solution(mesh):
    split = P(("scene", "dom"), None, None)
    flat = P(("scene", "dom"), None)
    return jax.shard_map(
        shards,
        mesh=mesh,
        in_specs=(split, split, P(), flat, flat),
        out_specs=(split, split, P("scene", None, None)),
        check_vma=False,
    )
```

```python
import functools

import jax
import jax.numpy as jnp
from jax import lax
from jax.experimental import pallas as pl
from jax.experimental.pallas import tpu as pltpu
from jax.sharding import PartitionSpec as P

BITS = 30
WORDS = 18
EDGE = 8
FACE = EDGE * EDGE
TILE = 128
CH = 64
GROUP = 8
KROWS = 9 * CH
SPLIT = 5 * CH
STACK = (3 * CH, 6 * TILE)
VMEM_LIMIT = 16 * 1024 * 1024
BF = jnp.bfloat16
F32 = jnp.float32

SHIFTS = [(p, q) for p in (-1, 0, 1) for q in (-1, 0, 1)]


def column_of(p, q, r):
    tap = (p + 1) * 9 + (q + 1) * 3 + r + 1
    return tap if tap < 13 else tap - 1


def lane_ids(rows):
    return lax.broadcasted_iota(jnp.int32, (rows, TILE), 1)


def pick(test, a, b):
    rows = 16 if a.dtype == BF else 8
    mask = test(lane_ids(rows))
    return jnp.concatenate(
        [
            jnp.where(mask, a[i : i + rows], b[i : i + rows])
            for i in range(0, a.shape[0], rows)
        ],
        axis=0,
    )


def left(lane):
    return lane < FACE


def row_first(lane):
    return (lane // EDGE) % EDGE == 0


def row_last(lane):
    return (lane // EDGE) % EDGE == EDGE - 1


def cell_first(lane):
    return lane % EDGE == 0


def cell_last(lane):
    return lane % EDGE == EDGE - 1


def roll(value, amount):
    return pltpu.roll(value, amount % TILE, 1)


def swap(value):
    return roll(value, FACE)


def tile_of(value, k):
    return value[:, k * TILE : (k + 1) * TILE]


def occupancy_tile(words, tile):
    lane = lane_ids(words.shape[0]) + tile * TILE
    first, last = (tile * TILE) // BITS, (tile * TILE + TILE - 1) // BITS
    word = jnp.broadcast_to(words[:, first : first + 1], lane.shape)
    place = lane - first * BITS
    for w in range(first + 1, last + 1):
        past = lane >= w * BITS
        word = jnp.where(past, jnp.broadcast_to(words[:, w : w + 1], lane.shape), word)
        place = jnp.where(past, lane - w * BITS, place)
    return (jnp.right_shift(word, place) & 1).astype(F32)


def spread(occ, leaf):
    part = jnp.broadcast_to(occ[leaf : leaf + 1, :], (16, TILE)).astype(BF)
    return jnp.concatenate([part] * (CH // 16), axis=0)


def masked_tiles(field_ref, occ, leaf):
    return [
        field_ref[leaf, :, k * TILE : (k + 1) * TILE] * spread(occ[k], leaf) for k in range(4)
    ]


def reorder(tiles):
    n0, n1, n2, n3 = tiles
    r0, r1, r2, r3 = [swap(t) for t in tiles]
    order = [pick(left, n0, r2), pick(left, r0, n2), pick(left, n1, r3), pick(left, r1, n3)]
    flipped = [pick(left, n2, r0), pick(left, r2, n0), pick(left, n3, r1), pick(left, r3, n1)]
    return order, flipped


def restore(t0, t1, t2, t3):
    return [
        pick(left, t0, swap(t1)),
        pick(left, t2, swap(t3)),
        pick(left, swap(t0), t1),
        pick(left, swap(t2), t3),
    ]


def shift_q(center, flipped, q):
    test = row_last if q < 0 else row_first
    return [roll(pick(test, m, c), -q * EDGE) for m, c in zip(flipped, center)]


def edges_kernel(meta_ref, x_ref, d_ref, cross_ref, chip_ref):
    words = meta_ref[:, 0:WORDS]
    occ_lo = occupancy_tile(words, 0)
    occ_hi = occupancy_tile(words, 3)
    first_core = lax.rem(lax.axis_index("dom"), 2) == 0
    for leaf in range(x_ref.shape[0]):
        low, high = spread(occ_lo, leaf), spread(occ_hi, leaf)
        x_lo, x_hi = x_ref[leaf, :, 0:TILE] * low, x_ref[leaf, :, 3 * TILE :] * high
        d_lo, d_hi = d_ref[leaf, :, 0:TILE] * low, d_ref[leaf, :, 3 * TILE :] * high
        up = pick(left, swap(d_hi), x_hi)
        down = pick(left, x_lo, swap(d_lo))
        cross_ref[leaf] = jnp.where(first_core, down, up)
        chip_ref[leaf] = jnp.where(first_core, up, down)


def edges(meta, x, dy):
    shape = jax.ShapeDtypeStruct((x.shape[0], CH, TILE), BF)
    return pl.pallas_call(
        edges_kernel,
        out_shape=(shape, shape),
        in_specs=[vmem_spec()] * 3,
        out_specs=(vmem_spec(), vmem_spec()),
        cost_estimate=cost(10**6, 10**6),
        compiler_params=params(),
        name="edges",
    )(meta, x, dy)


def split_far(cross_ref, chip_ref, leaf):
    first_core = lax.rem(lax.axis_index("dom"), 2) == 0
    low = jnp.where(first_core, chip_ref[leaf], cross_ref[leaf])
    high = jnp.where(first_core, cross_ref[leaf], chip_ref[leaf])
    return low, high


def fill(store, flip, field_ref, occ, halo, turned):
    leaves = field_ref.shape[0]
    for leaf in range(leaves):
        order, flipped = reorder(masked_tiles(field_ref, occ, leaf))
        store[leaf] = jnp.concatenate(order, axis=1)
        flip[leaf] = jnp.concatenate(flipped, axis=1)
    if halo:
        for leaf in range(leaves):
            low, high = split_far(*halo, leaf)
            store[leaves + leaf, :, 0:TILE] = swap(low) if turned else low
            store[leaves + leaf, :, 3 * TILE :] = swap(high) if turned else high
    store[store.shape[0] - 1] = jnp.zeros(store.shape[1:], BF)
    flip[leaves] = jnp.zeros(flip.shape[1:], BF)


def place(near_ref, leaf, p, q, z, device, leaves, which):
    if (p, q, z) == (0, 0, 0):
        return leaf
    ident = near_ref[leaf, WORDS + column_of(p, q, z)]
    owner = ident // leaves
    slot = ident - owner * leaves
    absent = ident < 0
    if which == "all":
        slot = jnp.where(owner == device, slot, slot + leaves)
        return jnp.where(absent, 2 * leaves, slot)
    here = owner == device
    if which == "far":
        here = jnp.logical_not(here)
    return jnp.where(jnp.logical_and(here, jnp.logical_not(absent)), slot, leaves)


def stacked(store, flip, near_ref, leaf, z, device, leaves, which="all"):
    rows = {}
    center = None
    for q in (0, -1, 1):
        mid = place(near_ref, leaf, 0, q, z, device, leaves, which)
        after = place(near_ref, leaf, 1, q, z, device, leaves, which)
        before = place(near_ref, leaf, -1, q, z, device, leaves, which)
        mine = store[mid]
        past = pick(left, store[after, :, 0:TILE], tile_of(mine, 0))
        ahead = pick(left, tile_of(mine, 3), store[before, :, 3 * TILE :])
        if q == 0:
            center = [swap(ahead)] + [tile_of(mine, k) for k in range(4)] + [swap(past)]
            rows[q] = center
        else:
            other = flip[jnp.minimum(mid, leaves)]
            flipped = [ahead] + [tile_of(other, k) for k in range(4)] + [past]
            rows[q] = shift_q(center, flipped, q)
    return jnp.concatenate([jnp.concatenate(rows[q], axis=1) for q in (-1, 0, 1)], axis=0)


def unstack(stack):
    return jnp.concatenate([stack[:, i * TILE : (i + 4) * TILE] for i in range(3)], axis=0)


def shift_c(value, r):
    if r == 0:
        return value
    test = cell_last if r > 0 else cell_first
    tiles = [tile_of(value, k) for k in range(value.shape[1] // TILE)]
    return jnp.concatenate([pick(test, jnp.zeros_like(t), roll(t, -r)) for t in tiles], axis=1)


def across_c(value, z):
    test = cell_last if z > 0 else cell_first
    tiles = [tile_of(value, k) for k in range(value.shape[1] // TILE)]
    return jnp.concatenate(
        [pick(test, roll(t, z * (EDGE - 1)), jnp.zeros_like(t)) for t in tiles], axis=1
    )


def listed(near_ref, leaf, z):
    found = jnp.int32(-1)
    for p in (-1, 0, 1):
        for q in (-1, 0, 1):
            found = jnp.maximum(found, near_ref[leaf, WORDS + column_of(p, q, z)])
    return found >= 0


CONTRACT_LANES = (((1,), (1,)), ((), ()))


def dot_lanes(a, b):
    return lax.dot_general(a, b, CONTRACT_LANES, preferred_element_type=F32)


def grad_kernel(near_ref, meta_ref, x_ref, d_ref, total, stack_ref, store, flip):
    leaves = x_ref.shape[0]
    device = lax.axis_index("dom")
    words = meta_ref[:, 0:WORDS]
    occ = [occupancy_tile(words, k) for k in range(4)]
    fill(store, flip, x_ref, occ, None, False)

    def ordered_dy(leaf):
        return jnp.concatenate(reorder(masked_tiles(d_ref, occ, leaf))[0], axis=1)

    for leaf in range(leaves):
        stack = stacked(store, flip, near_ref, leaf, 0, device, leaves, "near")
        stack_ref[leaf] = stack
        center = ordered_dy(leaf)
        wide = jnp.concatenate([shift_c(center, -r) for r in (-1, 0, 1)], axis=0)
        term = dot_lanes(unstack(stack), wide)
        if leaf == 0:
            total[...] = term
        else:
            total[...] += term

    for z in (-1, 1):
        for leaf in range(leaves):

            @pl.when(listed(near_ref, leaf, z))
            def _():
                stack = stacked(store, flip, near_ref, leaf, z, device, leaves, "near")
                edge = across_c(ordered_dy(leaf), -z)
                total[:, (z + 1) * CH : (z + 2) * CH] += dot_lanes(unstack(stack), edge)


def grad_terms(meta, x, dy):
    leaves = x.shape[0]
    return pl.pallas_call(
        grad_kernel,
        out_shape=(
            jax.ShapeDtypeStruct((KROWS, 3 * CH), F32),
            jax.ShapeDtypeStruct((leaves,) + STACK, BF),
        ),
        in_specs=[smem_spec()] + [vmem_spec()] * 3,
        out_specs=(vmem_spec(), vmem_spec()),
        scratch_shapes=[pltpu.VMEM((leaves + 1, CH, 4 * TILE), BF)] * 2,
        cost_estimate=cost(10**9, 2 * 10**6),
        compiler_params=params(),
        name="grad_terms",
    )(meta, meta, x, dy)


def third_part(row):
    return (KROWS + row, 0) if row < SPLIT else (KROWS + row - SPLIT, 1)


def grad_far_kernel(
    near_ref, meta_ref, d_ref, cross_ref, chip_ref, near_total, keep_ref, send_ref, store, packed
):
    leaves = d_ref.shape[0]
    device = lax.axis_index("dom")
    words = meta_ref[:, 0:WORDS]
    occ_lo, occ_hi = occupancy_tile(words, 0), occupancy_tile(words, 3)
    for leaf in range(leaves):
        low, high = split_far(cross_ref, chip_ref, leaf)
        store[0, leaf], store[1, leaf] = low, high
        store[2, leaf], store[3, leaf] = swap(low), swap(high)
    for i in range(4):
        store[i, leaves] = jnp.zeros((CH, TILE), BF)

    def far_rows(p, one, two, z):
        at = lambda leaf, q: place(near_ref, leaf, p, q, z, device, leaves, "far")
        first, second = (0, 2) if p > 0 else (3, 1)
        pair = lambda a, b, q: pick(left, store[first, at(a, q)], store[second, at(b, q)])
        center = pair(one, two, 0)
        sides = [shift_q([center], [pair(two, one, q)], q)[0] for q in (-1, 1)]
        return jnp.concatenate([sides[0], center, sides[1]], axis=0)

    def end_plane(p, one, two):
        if p > 0:
            a, b = [d_ref[l, :, 3 * TILE :] * spread(occ_hi, l) for l in (one, two)]
            return pick(left, swap(a), b)
        a, b = [d_ref[l, :, 0:TILE] * spread(occ_lo, l) for l in (one, two)]
        return pick(left, a, swap(b))

    pairs = [(leaf, leaf + 1) for leaf in range(0, leaves, 2)]
    for p in (-1, 0, 1):
        term = None
        if p != 0:
            rows = jnp.concatenate([far_rows(p, a, b, 0) for a, b in pairs], axis=1)
            planes = jnp.concatenate([end_plane(p, a, b) for a, b in pairs], axis=1)
            wide = jnp.concatenate([shift_c(planes, -r) for r in (-1, 0, 1)], axis=0)
            term = dot_lanes(rows, wide)
        for q in (-1, 0, 1):
            row = SHIFTS.index((p, q)) * CH
            block = near_total[row : row + CH, :]
            if p != 0:
                block = block + term[(q + 1) * CH : (q + 2) * CH, :]
            packed[row : row + CH, :] = block[:, 0:TILE]
            low, side = third_part(row)
            packed[low : low + CH, side * CH : (side + 1) * CH] = block[:, TILE:]
    packed[2 * KROWS - SPLIT :, CH:] = jnp.zeros((2 * SPLIT - KROWS, CH), F32)

    for z in (-1, 1):
        for leaf in range(leaves):

            @pl.when(listed(near_ref, leaf, z))
            def _():
                for p in (-1, 1):
                    plane = end_plane(p, leaf, leaf)
                    plane = across_c(pick(left, plane, jnp.zeros_like(plane)), -z)
                    term = dot_lanes(far_rows(p, leaf, leaf, z), plane)
                    for q in (-1, 0, 1):
                        row, side = SHIFTS.index((p, q)) * CH, 0
                        if z > 0:
                            row, side = third_part(row)
                        packed[row : row + CH, side * CH : (side + 1) * CH] += term[
                            (q + 1) * CH : (q + 2) * CH, :
                        ]

    core = lax.rem(device, 2)
    rows = packed.shape[0] // 2
    keep_ref[...] = packed[pl.ds(pl.multiple_of(core * rows, 8), rows), :]
    send_ref[...] = packed[pl.ds(pl.multiple_of((1 - core) * rows, 8), rows), :]


def grad_far(meta, dy, cross, chip, total):
    leaves = dy.shape[0]
    rows = KROWS + SPLIT
    shape = jax.ShapeDtypeStruct((rows // 2, TILE), F32)
    return pl.pallas_call(
        grad_far_kernel,
        out_shape=(shape, shape),
        in_specs=[smem_spec()] + [vmem_spec()] * 5,
        out_specs=(vmem_spec(), vmem_spec()),
        scratch_shapes=[
            pltpu.VMEM((4, leaves + 1, CH, TILE), BF),
            pltpu.VMEM((rows, TILE), F32),
        ],
        cost_estimate=cost(10**8, 2 * 10**6),
        compiler_params=params(),
        name="grad_far",
    )(meta, meta, dy, cross, chip, total)


def vmem_spec():
    return pl.BlockSpec(memory_space=pltpu.VMEM)


def any_spec():
    return pl.BlockSpec(memory_space=pl.ANY)


def smem_spec():
    return pl.BlockSpec(memory_space=pltpu.SMEM)


def params():
    return pltpu.CompilerParams(vmem_limit_bytes=VMEM_LIMIT)


def cost(flops, bytes_accessed):
    return pl.CostEstimate(flops=flops, bytes_accessed=bytes_accessed, transcendentals=0)


def ordered_taps(w_ref, turned):
    def tap(index, r):
        p, q = SHIFTS[index]
        return (p + 1) * 9 + (q + 1) * 3 + r + 1

    if turned:
        return jnp.concatenate(
            [
                jnp.concatenate([w_ref[26 - tap(index, r)] for index in range(9)], axis=1)
                for r in (-1, 0, 1)
            ],
            axis=0,
        )
    return jnp.concatenate(
        [
            jnp.concatenate([w_ref[tap(index, r)] for r in (-1, 0, 1)], axis=1)
            for index in range(9)
        ],
        axis=0,
    ).T


def finish(occ, leaf, total):
    rounded = total.astype(BF)
    tiles = restore(*[tile_of(rounded, k) for k in range(4)])
    return jnp.concatenate([t * spread(occ[k], leaf) for k, t in enumerate(tiles)], axis=1)


def leaf_sum(taps, near_x):
    wide = jnp.dot(taps, near_x, preferred_element_type=F32)
    total = wide[CH : 2 * CH]
    for r in (-1, 1):
        total = total + shift_c(wide[(r + 1) * CH : (r + 2) * CH], r)
    return total


def third_dimension(near_ref, taps, occ, x_ref, cross_ref, chip_ref, turned, out_ref, store, flip):
    leaves = x_ref.shape[0]
    device = lax.axis_index("dom")
    found = [listed(near_ref, leaf, -1) | listed(near_ref, leaf, 1) for leaf in range(leaves)]

    @pl.when(functools.reduce(jnp.logical_or, found))
    def _():
        fill(store, flip, x_ref, occ, (cross_ref, chip_ref), turned)
        for leaf in range(leaves):
            stack = stacked(store, flip, near_ref, leaf, 0, device, leaves)
            total = leaf_sum(taps, unstack(stack))
            for z in (-1, 1):
                stack = stacked(store, flip, near_ref, leaf, z, device, leaves)
                part = jnp.dot(
                    taps[(z + 1) * CH : (z + 2) * CH], unstack(stack), preferred_element_type=F32
                )
                total = total + across_c(part, z)
            out_ref[leaf] = finish(occ, leaf, total)


def out_kernel(
    near_ref, meta_ref, x_ref, d_ref, cross_ref, chip_ref, w_ref, stack_ref, _,
    out_ref, stack_dy_ref, done_ref, store, flip, far,
):
    leaves = x_ref.shape[0]
    device = lax.axis_index("dom")
    words = meta_ref[:, 0:WORDS]
    occ = [occupancy_tile(words, k) for k in range(4)]
    done_ref[...] = jnp.zeros(done_ref.shape, F32)
    taps = ordered_taps(w_ref, False)
    fill(store, flip, d_ref, occ, (cross_ref, chip_ref), True)
    for leaf in range(leaves):
        low, high = split_far(cross_ref, chip_ref, leaf)
        both = pick(left, low, high)
        far[0, leaf], far[1, leaf] = both, swap(both)
    far[0, leaves] = far[1, leaves] = jnp.zeros((CH, TILE), BF)

    def far_tiles(leaf):
        at = lambda p, q: place(near_ref, leaf, p, q, 0, device, leaves, "far")
        center = pick(left, far[1, at(-1, 0)], far[1, at(1, 0)])
        flipped = {q: pick(left, far[0, at(1, q)], far[0, at(-1, q)]) for q in (-1, 1)}
        sides = [shift_q([center], [flipped[q]], q)[0] for q in (-1, 1)]
        return jnp.concatenate([sides[0], center, sides[1]], axis=0)

    for leaf in range(leaves):
        stack_dy_ref[leaf] = stacked(store, flip, near_ref, leaf, 0, device, leaves)
        planes = far_tiles(leaf)
        zero = jnp.zeros_like(planes)
        stack = stack_ref[leaf]
        stack = jnp.concatenate(
            [
                tile_of(stack, 0) + pick(left, planes, zero),
                stack[:, TILE : 5 * TILE],
                tile_of(stack, 5) + pick(left, zero, planes),
            ],
            axis=1,
        )
        out_ref[leaf] = finish(occ, leaf, leaf_sum(taps, unstack(stack)))
    third_dimension(
        near_ref, taps, occ, x_ref, cross_ref, chip_ref, False, out_ref, store, flip
    )


def out_conv(meta, x, dy, cross, chip, weight, stack, after):
    leaves = x.shape[0]
    return pl.pallas_call(
        out_kernel,
        out_shape=(
            jax.ShapeDtypeStruct(x.shape, BF),
            jax.ShapeDtypeStruct(stack.shape, BF),
            jax.ShapeDtypeStruct((8, TILE), F32),
        ),
        in_specs=[smem_spec()] + [vmem_spec()] * 7 + [any_spec()],
        out_specs=(vmem_spec(),) * 3,
        scratch_shapes=[
            pltpu.VMEM((2 * leaves + 1, CH, 4 * TILE), BF),
            pltpu.VMEM((leaves + 1, CH, 4 * TILE), BF),
            pltpu.VMEM((2, leaves + 1, CH, TILE), BF),
        ],
        cost_estimate=cost(10**9, 2 * 10**6),
        compiler_params=params(),
        name="out_conv",
    )(meta, meta, x, dy, cross, chip, weight, stack, after)


def in_grad_kernel(
    near_ref, meta_ref, d_ref, cross_ref, chip_ref, w_ref, stack_ref, _,
    out_ref, done_ref, store, flip,
):
    leaves = d_ref.shape[0]
    words = meta_ref[:, 0:WORDS]
    occ = [occupancy_tile(words, k) for k in range(4)]
    done_ref[...] = jnp.zeros(done_ref.shape, F32)
    taps = ordered_taps(w_ref, True)
    for leaf in range(leaves):
        out_ref[leaf] = finish(occ, leaf, leaf_sum(taps, unstack(stack_ref[leaf])))
    third_dimension(near_ref, taps, occ, d_ref, cross_ref, chip_ref, True, out_ref, store, flip)


def in_grad_conv(meta, dy, cross, chip, weight, stack, after):
    leaves = dy.shape[0]
    return pl.pallas_call(
        in_grad_kernel,
        out_shape=(jax.ShapeDtypeStruct(dy.shape, BF), jax.ShapeDtypeStruct((8, TILE), F32)),
        in_specs=[smem_spec()] + [vmem_spec()] * 6 + [any_spec()],
        out_specs=(vmem_spec(),) * 2,
        scratch_shapes=[
            pltpu.VMEM((2 * leaves + 1, CH, 4 * TILE), BF),
            pltpu.VMEM((leaves + 1, CH, 4 * TILE), BF),
        ],
        cost_estimate=cost(10**9, 2 * 10**6),
        compiler_params=params(),
        name="in_grad_conv",
    )(meta, meta, dy, cross, chip, weight, stack, after)


def sum_kernel(own_ref, *refs):
    *got_refs, _, out_ref = refs
    total = own_ref[...]
    for got_ref in got_refs:
        total = total + got_ref[...]
    out_ref[...] = total


def sum_chunks(own, got, after):
    return pl.pallas_call(
        sum_kernel,
        out_shape=jax.ShapeDtypeStruct(own.shape, F32),
        in_specs=[vmem_spec()] * (1 + len(got)) + [any_spec()],
        out_specs=vmem_spec(),
        cost_estimate=cost(10**5, 3 * 10**5),
        compiler_params=params(),
        name="sum_chunks",
    )(own, *got, after)


def join_kernel(*refs):
    *parts, _, out_ref = refs
    lane = lax.rem(lax.axis_index("dom") // 2, 4)
    rows = parts[0].shape[0]
    for mask, part in enumerate(parts):
        at = pl.multiple_of(jnp.bitwise_xor(lane, mask) * rows, 8)
        out_ref[pl.ds(at, rows), :] = part[...]


def join_chunks(parts, after):
    rows = parts[0].shape[0]
    return pl.pallas_call(
        join_kernel,
        out_shape=jax.ShapeDtypeStruct((len(parts) * rows, TILE), F32),
        in_specs=[vmem_spec()] * len(parts) + [any_spec()],
        out_specs=vmem_spec(),
        cost_estimate=cost(10**5, 5 * 10**5),
        compiler_params=params(),
        name="join_chunks",
    )(*parts, after)


def unpack_kernel(scale, own_ref, other_ref, out_ref, total):
    core = lax.rem(lax.axis_index("dom"), 2)
    rows = own_ref.shape[0]
    total[pl.ds(pl.multiple_of(core * rows, 8), rows), :] = own_ref[...] * scale
    total[pl.ds(pl.multiple_of((1 - core) * rows, 8), rows), :] = other_ref[...] * scale
    for index, (p, q) in enumerate(SHIFTS):
        for r in (-1, 0, 1):
            tap = (p + 1) * 9 + (q + 1) * 3 + r + 1
            row, side = index * CH, r + 1
            if r == 1:
                row, side = third_part(row)
            out_ref[tap] = total[row : row + CH, side * CH : (side + 1) * CH]


def unpack(own, other, scale):
    return pl.pallas_call(
        functools.partial(unpack_kernel, scale),
        out_shape=jax.ShapeDtypeStruct((27, CH, CH), F32),
        in_specs=[vmem_spec(), vmem_spec()],
        out_specs=vmem_spec(),
        scratch_shapes=[pltpu.VMEM((2 * own.shape[0], TILE), F32)],
        cost_estimate=cost(10**6, 10**6),
        compiler_params=params(),
        name="unpack_grad",
    )(own, other)


def exchange(array, mask, size):
    return lax.ppermute(array, "dom", [(i, i ^ mask) for i in range(size)])


def shards(features, cotangent, weight, mask_words, neighbors):
    leaves, channels, voxels = features.shape
    size = lax.axis_size("dom")
    device = lax.axis_index("dom")
    meta = jnp.concatenate([mask_words, neighbors], axis=1)
    to_cross, to_chip = edges(meta, features, cotangent)
    between = [(i, i + 1) for i in range(1, size - 1, 2)]
    cross = lax.ppermute(to_cross, "dom", between + [(j, i) for i, j in between])
    chip = exchange(to_chip, 1, size)

    total, stack = grad_terms(meta, features, cotangent)
    keep, send = grad_far(meta, cotangent, cross, chip, total)
    keep = keep + exchange(send, 1, size)
    rows = keep.shape[0] // 4
    lane = (device // 2) % 4
    chunk = lambda index: lax.dynamic_slice_in_dim(keep, index * rows, rows, axis=0)
    to_send = [chunk(lane ^ m) for m in (1, 2, 3)]
    own = chunk(lane)
    got = [exchange(part, 2 * m, size) for m, part in zip((1, 2, 3), to_send)]
    out_features, stack_dy, out_done = out_conv(
        meta, features, cotangent, cross, chip, weight, stack, to_send[2]
    )
    own = sum_chunks(own, got, out_done)
    if size > GROUP:
        groups = [[j * GROUP + i for j in range(size // GROUP)] for i in range(GROUP)]
        own = lax.psum(own, "dom", axis_index_groups=groups)
    back = [exchange(own, 2 * m, size) for m in (1, 2, 3)]
    in_grad, in_done = in_grad_conv(meta, cotangent, cross, chip, weight, stack_dy, own)
    half = join_chunks([own] + back, in_done)
    other = exchange(half, 1, size)
    scale = float(size * leaves * voxels) ** -0.5
    return (out_features, in_grad, unpack(half, other, scale))


def solution(mesh):
    split = P(("scene", "dom"), None, None)
    flat = P(("scene", "dom"), None)
    return jax.shard_map(
        shards,
        mesh=mesh,
        in_specs=(split, split, P(), flat, flat),
        out_specs=(split, split, P("scene", None, None)),
        check_vma=False,
    )
```

```python
import functools

import jax
import jax.numpy as jnp
from jax import lax
from jax.experimental import pallas as pl
from jax.experimental.pallas import tpu as pltpu
from jax.sharding import PartitionSpec as P

BITS = 30
NEAR = 26
EDGE = 8
FACE = EDGE * EDGE
TILE = 128
CH = 64
GROUP = 8
KROWS = 9 * CH
SPLIT = 5 * CH
STACK = (3 * CH, 6 * TILE)
VMEM_LIMIT = 16 * 1024 * 1024
BF = jnp.bfloat16
F32 = jnp.float32

SHIFTS = [(p, q) for p in (-1, 0, 1) for q in (-1, 0, 1)]


def column_of(p, q, r):
    tap = (p + 1) * 9 + (q + 1) * 3 + r + 1
    return tap if tap < 13 else tap - 1


def lane_ids(rows):
    return lax.broadcasted_iota(jnp.int32, (rows, TILE), 1)


def pick(test, a, b):
    rows = 16 if a.dtype == BF else 8
    mask = test(lane_ids(rows))
    return jnp.concatenate(
        [
            jnp.where(mask, a[i : i + rows], b[i : i + rows])
            for i in range(0, a.shape[0], rows)
        ],
        axis=0,
    )


def left(lane):
    return lane < FACE


def row_first(lane):
    return (lane // EDGE) % EDGE == 0


def row_last(lane):
    return (lane // EDGE) % EDGE == EDGE - 1


def cell_first(lane):
    return lane % EDGE == 0


def cell_last(lane):
    return lane % EDGE == EDGE - 1


def roll(value, amount):
    return pltpu.roll(value, amount % TILE, 1)


def swap(value):
    return roll(value, FACE)


def tile_of(value, k):
    return value[:, k * TILE : (k + 1) * TILE]


def occupancy_tile(words, tile):
    lane = lane_ids(words.shape[0]) + tile * TILE
    first, last = (tile * TILE) // BITS, (tile * TILE + TILE - 1) // BITS
    word = jnp.broadcast_to(words[:, first : first + 1], lane.shape)
    place = lane - first * BITS
    for w in range(first + 1, last + 1):
        past = lane >= w * BITS
        word = jnp.where(past, jnp.broadcast_to(words[:, w : w + 1], lane.shape), word)
        place = jnp.where(past, lane - w * BITS, place)
    return (jnp.right_shift(word, place) & 1).astype(F32)


def spread(occ, leaf):
    part = jnp.broadcast_to(occ[leaf : leaf + 1, :], (16, TILE)).astype(BF)
    return jnp.concatenate([part] * (CH // 16), axis=0)


def masked_tiles(field_ref, occ, leaf):
    return [
        field_ref[leaf, :, k * TILE : (k + 1) * TILE] * spread(occ[k], leaf) for k in range(4)
    ]


def reorder(tiles):
    n0, n1, n2, n3 = tiles
    r0, r1, r2, r3 = [swap(t) for t in tiles]
    order = [pick(left, n0, r2), pick(left, r0, n2), pick(left, n1, r3), pick(left, r1, n3)]
    flipped = [pick(left, n2, r0), pick(left, r2, n0), pick(left, n3, r1), pick(left, r3, n1)]
    return order, flipped


def restore(t0, t1, t2, t3):
    return [
        pick(left, t0, swap(t1)),
        pick(left, t2, swap(t3)),
        pick(left, swap(t0), t1),
        pick(left, swap(t2), t3),
    ]


def shift_q(center, flipped, q):
    test = row_last if q < 0 else row_first
    return [roll(pick(test, m, c), -q * EDGE) for m, c in zip(flipped, center)]


def write_tables(near, all_ref, own_ref, far_ref, flags_ref):
    leaves = near.shape[0]
    first = lax.axis_index("dom") * leaves
    slot = near - first
    absent = near < 0
    here = (slot >= 0) & (slot < leaves) & jnp.logical_not(absent)
    other = jnp.where(slot < 0, slot + leaves, slot - leaves)
    own_ref[...] = jnp.where(here, slot, leaves)
    far_ref[...] = jnp.where(here | absent, leaves, other)
    all_ref[...] = jnp.where(absent, 2 * leaves, jnp.where(here, slot, other + leaves))
    column = lax.broadcasted_iota(jnp.int32, near.shape, 1)
    cell = lax.rem(jnp.where(column < 13, column, column + 1), 3)
    flags = [
        jnp.max(jnp.where(present, 1, 0).astype(F32), axis=1, keepdims=True)
        for present in (
            jnp.logical_not(absent) & (cell == 0),
            jnp.logical_not(absent) & (cell == 2),
        )
    ]
    some = jnp.max(jnp.maximum(*flags), axis=0, keepdims=True)
    lane = lane_ids(leaves)
    table = jnp.where(lane == 0, flags[0], jnp.where(lane == 1, flags[1], some))
    flags_ref[...] = table.astype(jnp.int32)


def prepare_kernel(
    meta_ref, x_ref, d_ref, cross_ref, chip_ref, store, flip, store_dy, flip_dy, occ_ref,
    all_ref, own_ref, far_ref, flags_ref,
):
    leaves = x_ref.shape[0]
    words = meta_ref[:, NEAR:]
    occ = [occupancy_tile(words, k) for k in range(4)]
    occ_ref[...] = jnp.concatenate(occ, axis=1)
    write_tables(meta_ref[:, 0:NEAR], all_ref, own_ref, far_ref, flags_ref)
    first_core = lax.rem(lax.axis_index("dom"), 2) == 0
    for leaf in range(leaves):
        x_tiles, d_tiles = masked_tiles(x_ref, occ, leaf), masked_tiles(d_ref, occ, leaf)
        up = pick(left, swap(d_tiles[3]), x_tiles[3])
        down = pick(left, x_tiles[0], swap(d_tiles[0]))
        cross_ref[leaf] = jnp.where(first_core, down, up)
        chip_ref[leaf] = jnp.where(first_core, up, down)
        for tiles, order_ref, flip_ref in ((x_tiles, store, flip), (d_tiles, store_dy, flip_dy)):
            order, flipped = reorder(tiles)
            order_ref[leaf] = jnp.concatenate(order, axis=1)
            flip_ref[leaf] = jnp.concatenate(flipped, axis=1)
    for ref in (store, flip, store_dy, flip_dy):
        ref[leaves] = jnp.zeros(ref.shape[1:], BF)


def prepare(meta, x, dy):
    leaves = x.shape[0]
    planes = jax.ShapeDtypeStruct((leaves, CH, TILE), BF)
    store = jax.ShapeDtypeStruct((leaves + 1,) + x.shape[1:], BF)
    table = jax.ShapeDtypeStruct((leaves, NEAR), jnp.int32)
    return pl.pallas_call(
        prepare_kernel,
        out_shape=(planes,) * 2
        + (store,) * 4
        + (jax.ShapeDtypeStruct((leaves, 4 * TILE), F32),)
        + (table,) * 3
        + (jax.ShapeDtypeStruct((leaves, TILE), jnp.int32),),
        in_specs=[vmem_spec()] * 3,
        out_specs=(vmem_spec(),) * 11,
        cost_estimate=cost(10**6, 4 * 10**6),
        compiler_params=params(),
        name="prepare",
    )(meta, x, dy)


def split_far(cross_ref, chip_ref, leaf):
    first_core = lax.rem(lax.axis_index("dom"), 2) == 0
    low = jnp.where(first_core, chip_ref[leaf], cross_ref[leaf])
    high = jnp.where(first_core, cross_ref[leaf], chip_ref[leaf])
    return low, high


def with_far(store, own, cross_ref, chip_ref, turned):
    leaves = own.shape[0] - 1
    for leaf in range(leaves):
        store[leaf] = own[leaf]
        low, high = split_far(cross_ref, chip_ref, leaf)
        store[leaves + leaf, :, 0:TILE] = swap(low) if turned else low
        store[leaves + leaf, :, 3 * TILE :] = swap(high) if turned else high
    store[2 * leaves] = own[leaves]


def place(table_ref, leaf, p, q, z):
    if (p, q, z) == (0, 0, 0):
        return leaf
    return table_ref[leaf, column_of(p, q, z)]


def third(flags_ref, leaf, z):
    return flags_ref[leaf, 0 if z < 0 else 1] > 0


def any_third(flags_ref):
    return flags_ref[0, 2] > 0


def stacked(store, flip, table_ref, leaf, z):
    rows = {}
    center = None
    for q in (0, -1, 1):
        mid = place(table_ref, leaf, 0, q, z)
        after = place(table_ref, leaf, 1, q, z)
        before = place(table_ref, leaf, -1, q, z)
        mine = store[mid]
        past = pick(left, store[after, :, 0:TILE], tile_of(mine, 0))
        ahead = pick(left, tile_of(mine, 3), store[before, :, 3 * TILE :])
        if q == 0:
            center = [swap(ahead)] + [tile_of(mine, k) for k in range(4)] + [swap(past)]
            rows[q] = center
        else:
            other = flip[jnp.minimum(mid, flip.shape[0] - 1)]
            flipped = [ahead] + [tile_of(other, k) for k in range(4)] + [past]
            rows[q] = shift_q(center, flipped, q)
    return jnp.concatenate([jnp.concatenate(rows[q], axis=1) for q in (-1, 0, 1)], axis=0)


def unstack(stack):
    return jnp.concatenate([stack[:, i * TILE : (i + 4) * TILE] for i in range(3)], axis=0)


def shift_c(value, r):
    if r == 0:
        return value
    test = cell_last if r > 0 else cell_first
    tiles = [tile_of(value, k) for k in range(value.shape[1] // TILE)]
    return jnp.concatenate([pick(test, jnp.zeros_like(t), roll(t, -r)) for t in tiles], axis=1)


def across_c(value, z):
    test = cell_last if z > 0 else cell_first
    tiles = [tile_of(value, k) for k in range(value.shape[1] // TILE)]
    return jnp.concatenate(
        [pick(test, roll(t, z * (EDGE - 1)), jnp.zeros_like(t)) for t in tiles], axis=1
    )


CONTRACT_LANES = (((1,), (1,)), ((), ()))


def dot_lanes(a, b):
    return lax.dot_general(a, b, CONTRACT_LANES, preferred_element_type=F32)


def grad_kernel(
    table_ref, flags_ref, store, flip, store_dy, flip_dy, total, stack_ref, stack_dy_ref
):
    leaves = stack_ref.shape[0]
    for leaf in range(leaves):
        stack = stacked(store, flip, table_ref, leaf, 0)
        stack_ref[leaf] = stack
        stack_dy_ref[leaf] = stacked(store_dy, flip_dy, table_ref, leaf, 0)
        wide = jnp.concatenate([shift_c(store_dy[leaf], -r) for r in (-1, 0, 1)], axis=0)
        term = dot_lanes(unstack(stack), wide)
        if leaf == 0:
            total[...] = term
        else:
            total[...] += term

    @pl.when(any_third(flags_ref))
    def _():
        for z in (-1, 1):
            for leaf in range(leaves):

                @pl.when(third(flags_ref, leaf, z))
                def _():
                    stack = stacked(store, flip, table_ref, leaf, z)
                    edge = across_c(store_dy[leaf], -z)
                    total[:, (z + 1) * CH : (z + 2) * CH] += dot_lanes(unstack(stack), edge)


def grad_terms(table, flags, store, flip, store_dy, flip_dy):
    leaves = store.shape[0] - 1
    stack = jax.ShapeDtypeStruct((leaves,) + STACK, BF)
    return pl.pallas_call(
        grad_kernel,
        out_shape=(jax.ShapeDtypeStruct((KROWS, 3 * CH), F32), stack, stack),
        in_specs=[smem_spec()] * 2 + [vmem_spec()] * 4,
        out_specs=(vmem_spec(),) * 3,
        cost_estimate=cost(10**9, 2 * 10**6),
        compiler_params=params(),
        name="grad_terms",
    )(table, flags, store, flip, store_dy, flip_dy)


def third_part(row):
    return (KROWS + row, 0) if row < SPLIT else (KROWS + row - SPLIT, 1)


def grad_far_kernel(
    table_ref, flags_ref, store_dy, cross_ref, chip_ref, near_total, keep_ref, send_ref,
    store, packed,
):
    leaves = store_dy.shape[0] - 1
    for leaf in range(leaves):
        low, high = split_far(cross_ref, chip_ref, leaf)
        store[0, leaf], store[1, leaf] = low, high
        store[2, leaf], store[3, leaf] = swap(low), swap(high)
    for i in range(4):
        store[i, leaves] = jnp.zeros((CH, TILE), BF)

    def far_rows(p, one, two, z):
        at = lambda leaf, q: place(table_ref, leaf, p, q, z)
        first, second = (0, 2) if p > 0 else (3, 1)
        pair = lambda a, b, q: pick(left, store[first, at(a, q)], store[second, at(b, q)])
        center = pair(one, two, 0)
        sides = [shift_q([center], [pair(two, one, q)], q)[0] for q in (-1, 1)]
        return jnp.concatenate([sides[0], center, sides[1]], axis=0)

    def end_plane(p, one, two):
        if p > 0:
            return pick(left, swap(store_dy[one, :, 3 * TILE :]), store_dy[two, :, 3 * TILE :])
        return pick(left, store_dy[one, :, 0:TILE], swap(store_dy[two, :, 0:TILE]))

    pairs = [(leaf, leaf + 1) for leaf in range(0, leaves, 2)]
    for p in (-1, 0, 1):
        term = None
        if p != 0:
            rows = jnp.concatenate([far_rows(p, a, b, 0) for a, b in pairs], axis=1)
            planes = jnp.concatenate([end_plane(p, a, b) for a, b in pairs], axis=1)
            wide = jnp.concatenate([shift_c(planes, -r) for r in (-1, 0, 1)], axis=0)
            term = dot_lanes(rows, wide)
        for q in (-1, 0, 1):
            row = SHIFTS.index((p, q)) * CH
            block = near_total[row : row + CH, :]
            if p != 0:
                block = block + term[(q + 1) * CH : (q + 2) * CH, :]
            packed[row : row + CH, :] = block[:, 0:TILE]
            low, side = third_part(row)
            packed[low : low + CH, side * CH : (side + 1) * CH] = block[:, TILE:]
    packed[2 * KROWS - SPLIT :, CH:] = jnp.zeros((2 * SPLIT - KROWS, CH), F32)

    @pl.when(any_third(flags_ref))
    def _():
        for z in (-1, 1):
            for leaf in range(leaves):

                @pl.when(third(flags_ref, leaf, z))
                def _():
                    for p in (-1, 1):
                        plane = end_plane(p, leaf, leaf)
                        plane = across_c(pick(left, plane, jnp.zeros_like(plane)), -z)
                        term = dot_lanes(far_rows(p, leaf, leaf, z), plane)
                        for q in (-1, 0, 1):
                            row, side = SHIFTS.index((p, q)) * CH, 0
                            if z > 0:
                                row, side = third_part(row)
                            packed[row : row + CH, side * CH : (side + 1) * CH] += term[
                                (q + 1) * CH : (q + 2) * CH, :
                            ]

    core = lax.rem(lax.axis_index("dom"), 2)
    rows = packed.shape[0] // 2
    keep_ref[...] = packed[pl.ds(pl.multiple_of(core * rows, 8), rows), :]
    send_ref[...] = packed[pl.ds(pl.multiple_of((1 - core) * rows, 8), rows), :]


def grad_far(table, flags, store_dy, cross, chip, total):
    leaves = store_dy.shape[0] - 1
    rows = KROWS + SPLIT
    shape = jax.ShapeDtypeStruct((rows // 2, TILE), F32)
    return pl.pallas_call(
        grad_far_kernel,
        out_shape=(shape, shape),
        in_specs=[smem_spec()] * 2 + [vmem_spec()] * 4,
        out_specs=(vmem_spec(), vmem_spec()),
        scratch_shapes=[
            pltpu.VMEM((4, leaves + 1, CH, TILE), BF),
            pltpu.VMEM((rows, TILE), F32),
        ],
        cost_estimate=cost(10**8, 2 * 10**6),
        compiler_params=params(),
        name="grad_far",
    )(table, flags, store_dy, cross, chip, total)


def vmem_spec():
    return pl.BlockSpec(memory_space=pltpu.VMEM)


def any_spec():
    return pl.BlockSpec(memory_space=pl.ANY)


def smem_spec():
    return pl.BlockSpec(memory_space=pltpu.SMEM)


def params():
    return pltpu.CompilerParams(vmem_limit_bytes=VMEM_LIMIT)


def cost(flops, bytes_accessed):
    return pl.CostEstimate(flops=flops, bytes_accessed=bytes_accessed, transcendentals=0)


def ordered_taps(w_ref, turned):
    def tap(index, r):
        p, q = SHIFTS[index]
        return (p + 1) * 9 + (q + 1) * 3 + r + 1

    if turned:
        return jnp.concatenate(
            [
                jnp.concatenate([w_ref[26 - tap(index, r)] for index in range(9)], axis=1)
                for r in (-1, 0, 1)
            ],
            axis=0,
        )
    return jnp.concatenate(
        [
            jnp.concatenate([w_ref[tap(index, r)] for r in (-1, 0, 1)], axis=1)
            for index in range(9)
        ],
        axis=0,
    ).T


def finish(occ, leaf, total):
    rounded = total.astype(BF)
    tiles = restore(*[tile_of(rounded, k) for k in range(4)])
    return jnp.concatenate([t * spread(occ[k], leaf) for k, t in enumerate(tiles)], axis=1)


def leaf_sum(taps, near_x):
    wide = jnp.dot(taps, near_x, preferred_element_type=F32)
    total = wide[CH : 2 * CH]
    for r in (-1, 1):
        total = total + shift_c(wide[(r + 1) * CH : (r + 2) * CH], r)
    return total


def far_tiles(far, table_ref, leaf):
    at = lambda p, q: place(table_ref, leaf, p, q, 0)
    center = pick(left, far[1, at(-1, 0)], far[1, at(1, 0)])
    flipped = {q: pick(left, far[0, at(1, q)], far[0, at(-1, q)]) for q in (-1, 1)}
    sides = [shift_q([center], [flipped[q]], q)[0] for q in (-1, 1)]
    return jnp.concatenate([sides[0], center, sides[1]], axis=0)


def conv_kernel(
    turned, far_table_ref, all_table_ref, flags_ref, occ_ref, own, flip, cross_ref, chip_ref, w_ref,
    stack_ref, _, out_ref, done_ref, far, store,
):
    leaves = out_ref.shape[0]
    occ = [tile_of(occ_ref[...], k) for k in range(4)]
    done_ref[...] = jnp.zeros(done_ref.shape, F32)
    taps = ordered_taps(w_ref, turned)
    for leaf in range(leaves):
        low, high = split_far(cross_ref, chip_ref, leaf)
        both = pick(left, high, low) if turned else pick(left, low, high)
        far[0, leaf], far[1, leaf] = (swap(both), both) if turned else (both, swap(both))
    far[0, leaves] = far[1, leaves] = jnp.zeros((CH, TILE), BF)
    for leaf in range(leaves):
        planes = far_tiles(far, far_table_ref, leaf)
        zero = jnp.zeros_like(planes)
        stack = stack_ref[leaf]
        stack = jnp.concatenate(
            [
                tile_of(stack, 0) + pick(left, planes, zero),
                stack[:, TILE : 5 * TILE],
                tile_of(stack, 5) + pick(left, zero, planes),
            ],
            axis=1,
        )
        out_ref[leaf] = finish(occ, leaf, leaf_sum(taps, unstack(stack)))

    @pl.when(any_third(flags_ref))
    def _():
        with_far(store, own, cross_ref, chip_ref, turned)
        for leaf in range(leaves):
            total = leaf_sum(taps, unstack(stacked(store, flip, all_table_ref, leaf, 0)))
            for z in (-1, 1):
                near_z = unstack(stacked(store, flip, all_table_ref, leaf, z))
                part = jnp.dot(
                    taps[(z + 1) * CH : (z + 2) * CH], near_z, preferred_element_type=F32
                )
                total = total + across_c(part, z)
            out_ref[leaf] = finish(occ, leaf, total)


def conv(far_table, all_table, flags, occ, own, flip, cross, chip, weight, stack, after, turned):
    leaves = stack.shape[0]
    return pl.pallas_call(
        functools.partial(conv_kernel, turned),
        out_shape=(
            jax.ShapeDtypeStruct((leaves, CH, 4 * TILE), BF),
            jax.ShapeDtypeStruct((8, TILE), F32),
        ),
        in_specs=[smem_spec()] * 3 + [vmem_spec()] * 7 + [any_spec()],
        out_specs=(vmem_spec(),) * 2,
        scratch_shapes=[
            pltpu.VMEM((2, leaves + 1, CH, TILE), BF),
            pltpu.VMEM((2 * leaves + 1, CH, 4 * TILE), BF),
        ],
        cost_estimate=cost(10**9, 2 * 10**6),
        compiler_params=params(),
        name="in_grad_conv" if turned else "out_conv",
    )(far_table, all_table, flags, occ, own, flip, cross, chip, weight, stack, after)


def split_kernel(keep_ref, got_ref, *refs):
    *out_refs, total = refs
    total[...] = keep_ref[...] + got_ref[...]
    lane = lax.rem(lax.axis_index("dom") // 2, 4)
    rows = out_refs[0].shape[0]
    for mask, out_ref in enumerate(out_refs):
        at = pl.multiple_of(jnp.bitwise_xor(lane, mask) * rows, 8)
        out_ref[...] = total[pl.ds(at, rows), :]


def split_chunks(keep, got):
    chunk = jax.ShapeDtypeStruct((keep.shape[0] // 4, TILE), F32)
    return pl.pallas_call(
        split_kernel,
        out_shape=(chunk,) * 4,
        in_specs=[vmem_spec()] * 2,
        out_specs=(vmem_spec(),) * 4,
        scratch_shapes=[pltpu.VMEM(keep.shape, F32)],
        cost_estimate=cost(10**5, 10**6),
        compiler_params=params(),
        name="split_chunks",
    )(keep, got)


def sum_kernel(own_ref, *refs):
    *got_refs, _, out_ref = refs
    total = own_ref[...]
    for got_ref in got_refs:
        total = total + got_ref[...]
    out_ref[...] = total


def sum_chunks(own, got, after):
    return pl.pallas_call(
        sum_kernel,
        out_shape=jax.ShapeDtypeStruct(own.shape, F32),
        in_specs=[vmem_spec()] * (1 + len(got)) + [any_spec()],
        out_specs=vmem_spec(),
        cost_estimate=cost(10**5, 3 * 10**5),
        compiler_params=params(),
        name="sum_chunks",
    )(own, *got, after)


def join_kernel(*refs):
    *parts, _, out_ref = refs
    lane = lax.rem(lax.axis_index("dom") // 2, 4)
    rows = parts[0].shape[0]
    for mask, part in enumerate(parts):
        at = pl.multiple_of(jnp.bitwise_xor(lane, mask) * rows, 8)
        out_ref[pl.ds(at, rows), :] = part[...]


def join_chunks(parts, after):
    rows = parts[0].shape[0]
    return pl.pallas_call(
        join_kernel,
        out_shape=jax.ShapeDtypeStruct((len(parts) * rows, TILE), F32),
        in_specs=[vmem_spec()] * len(parts) + [any_spec()],
        out_specs=vmem_spec(),
        cost_estimate=cost(10**5, 5 * 10**5),
        compiler_params=params(),
        name="join_chunks",
    )(*parts, after)


def unpack_kernel(scale, own_ref, other_ref, out_ref, total):
    core = lax.rem(lax.axis_index("dom"), 2)
    rows = own_ref.shape[0]
    total[pl.ds(pl.multiple_of(core * rows, 8), rows), :] = own_ref[...] * scale
    total[pl.ds(pl.multiple_of((1 - core) * rows, 8), rows), :] = other_ref[...] * scale
    for index, (p, q) in enumerate(SHIFTS):
        for r in (-1, 0, 1):
            tap = (p + 1) * 9 + (q + 1) * 3 + r + 1
            row, side = index * CH, r + 1
            if r == 1:
                row, side = third_part(row)
            out_ref[tap] = total[row : row + CH, side * CH : (side + 1) * CH]


def unpack(own, other, scale):
    return pl.pallas_call(
        functools.partial(unpack_kernel, scale),
        out_shape=jax.ShapeDtypeStruct((27, CH, CH), F32),
        in_specs=[vmem_spec(), vmem_spec()],
        out_specs=vmem_spec(),
        scratch_shapes=[pltpu.VMEM((2 * own.shape[0], TILE), F32)],
        cost_estimate=cost(10**6, 10**6),
        compiler_params=params(),
        name="unpack_grad",
    )(own, other)


def exchange(array, mask, size):
    return lax.ppermute(array, "dom", [(i, i ^ mask) for i in range(size)])


def shards(features, cotangent, weight, mask_words, neighbors):
    leaves, channels, voxels = features.shape
    size = lax.axis_size("dom")
    meta = jnp.concatenate([neighbors, mask_words], axis=1)
    to_cross, to_chip, *fields, occ, all_table, own_table, far_table, flags = prepare(
        meta, features, cotangent
    )
    store, flip, store_dy, flip_dy = fields
    between = [(i, i + 1) for i in range(1, size - 1, 2)]
    cross = lax.ppermute(to_cross, "dom", between + [(j, i) for i, j in between])
    chip = exchange(to_chip, 1, size)

    total, stack, stack_dy = grad_terms(own_table, flags, *fields)
    keep, send = grad_far(far_table, flags, store_dy, cross, chip, total)
    own, *to_send = split_chunks(keep, exchange(send, 1, size))
    got = [exchange(part, 2 * m, size) for m, part in zip((1, 2, 3), to_send)]
    out_features, out_done = conv(
        far_table, all_table, flags, occ, store, flip, cross, chip, weight, stack,
        to_send[2], False,
    )
    own = sum_chunks(own, got, out_done)
    if size > GROUP:
        groups = [[j * GROUP + i for j in range(size // GROUP)] for i in range(GROUP)]
        own = lax.psum(own, "dom", axis_index_groups=groups)
    back = [exchange(own, 2 * m, size) for m in (1, 2, 3)]
    in_grad, in_done = conv(
        far_table, all_table, flags, occ, store_dy, flip_dy, cross, chip, weight, stack_dy,
        own, True,
    )
    half = join_chunks([own] + back, in_done)
    other = exchange(half, 1, size)
    scale = float(size * leaves * voxels) ** -0.5
    return (out_features, in_grad, unpack(half, other, scale))


def solution(mesh):
    split = P(("scene", "dom"), None, None)
    flat = P(("scene", "dom"), None)
    return jax.shard_map(
        shards,
        mesh=mesh,
        in_specs=(split, split, P(), flat, flat),
        out_specs=(split, split, P("scene", None, None)),
        check_vma=False,
    )
```

```python
import functools

import jax
import jax.numpy as jnp
from jax import lax
from jax.experimental import pallas as pl
from jax.experimental.pallas import tpu as pltpu
from jax.sharding import PartitionSpec as P

BITS = 30
NEAR = 26
EDGE = 8
FACE = EDGE * EDGE
TILE = 128
CH = 64
GROUP = 8
KROWS = 9 * CH
SPLIT = 5 * CH
STACK = (3 * CH, 6 * TILE)
VMEM_LIMIT = 16 * 1024 * 1024
BF = jnp.bfloat16
F32 = jnp.float32

SHIFTS = [(p, q) for p in (-1, 0, 1) for q in (-1, 0, 1)]


def column_of(p, q, r):
    tap = (p + 1) * 9 + (q + 1) * 3 + r + 1
    return tap if tap < 13 else tap - 1


def lane_ids(rows):
    return lax.broadcasted_iota(jnp.int32, (rows, TILE), 1)


def pick(test, a, b):
    rows = 16 if a.dtype == BF else 8
    mask = test(lane_ids(rows))
    return jnp.concatenate(
        [
            jnp.where(mask, a[i : i + rows], b[i : i + rows])
            for i in range(0, a.shape[0], rows)
        ],
        axis=0,
    )


def left(lane):
    return lane < FACE


def row_first(lane):
    return (lane // EDGE) % EDGE == 0


def row_last(lane):
    return (lane // EDGE) % EDGE == EDGE - 1


def cell_first(lane):
    return lane % EDGE == 0


def cell_last(lane):
    return lane % EDGE == EDGE - 1


def roll(value, amount):
    return pltpu.roll(value, amount % TILE, 1)


def swap(value):
    return roll(value, FACE)


def tile_of(value, k):
    return value[:, k * TILE : (k + 1) * TILE]


def occupancy_tile(words, tile):
    lane = lane_ids(words.shape[0]) + tile * TILE
    first, last = (tile * TILE) // BITS, (tile * TILE + TILE - 1) // BITS
    word = jnp.broadcast_to(words[:, first : first + 1], lane.shape)
    place = lane - first * BITS
    for w in range(first + 1, last + 1):
        past = lane >= w * BITS
        word = jnp.where(past, jnp.broadcast_to(words[:, w : w + 1], lane.shape), word)
        place = jnp.where(past, lane - w * BITS, place)
    return (jnp.right_shift(word, place) & 1).astype(F32)


def spread(occ, leaf):
    part = jnp.broadcast_to(occ[leaf : leaf + 1, :], (16, TILE)).astype(BF)
    return jnp.concatenate([part] * (CH // 16), axis=0)


def masked_tiles(field_ref, occ, leaf):
    return [
        field_ref[leaf, :, k * TILE : (k + 1) * TILE] * spread(occ[k], leaf) for k in range(4)
    ]


def reorder(tiles):
    n0, n1, n2, n3 = tiles
    r0, r1, r2, r3 = [swap(t) for t in tiles]
    order = [pick(left, n0, r2), pick(left, r0, n2), pick(left, n1, r3), pick(left, r1, n3)]
    flipped = [pick(left, n2, r0), pick(left, r2, n0), pick(left, n3, r1), pick(left, r3, n1)]
    return order, flipped


def restore(t0, t1, t2, t3):
    return [
        pick(left, t0, swap(t1)),
        pick(left, t2, swap(t3)),
        pick(left, swap(t0), t1),
        pick(left, swap(t2), t3),
    ]


def shift_q(center, flipped, q):
    test = row_last if q < 0 else row_first
    return [roll(pick(test, m, c), -q * EDGE) for m, c in zip(flipped, center)]


def write_tables(near, all_ref, own_ref, far_ref, flags_ref):
    leaves = near.shape[0]
    first = lax.axis_index("dom") * leaves
    slot = near - first
    absent = near < 0
    here = (slot >= 0) & (slot < leaves) & jnp.logical_not(absent)
    other = jnp.where(slot < 0, slot + leaves, slot - leaves)
    own_ref[...] = jnp.where(here, slot, leaves)
    far_ref[...] = jnp.where(here | absent, leaves, other)
    all_ref[...] = jnp.where(absent, 2 * leaves, jnp.where(here, slot, other + leaves))
    column = lax.broadcasted_iota(jnp.int32, near.shape, 1)
    cell = lax.rem(jnp.where(column < 13, column, column + 1), 3)
    flags = [
        jnp.max(jnp.where(present, 1, 0).astype(F32), axis=1, keepdims=True)
        for present in (
            jnp.logical_not(absent) & (cell == 0),
            jnp.logical_not(absent) & (cell == 2),
        )
    ]
    some = jnp.max(jnp.maximum(*flags), axis=0, keepdims=True)
    lane = lane_ids(leaves)
    table = jnp.where(lane == 0, flags[0], jnp.where(lane == 1, flags[1], some))
    flags_ref[...] = table.astype(jnp.int32)


def prepare_kernel(
    meta_ref, x_ref, d_ref, cross_ref, chip_ref, store, flip, store_dy, flip_dy, occ_ref,
    all_ref, own_ref, far_ref, flags_ref,
):
    leaves = x_ref.shape[0]
    words = meta_ref[:, NEAR:]
    occ = [occupancy_tile(words, k) for k in range(4)]
    occ_ref[...] = jnp.concatenate(occ, axis=1)
    write_tables(meta_ref[:, 0:NEAR], all_ref, own_ref, far_ref, flags_ref)
    first_core = lax.rem(lax.axis_index("dom"), 2) == 0
    for leaf in range(leaves):
        x_tiles, d_tiles = masked_tiles(x_ref, occ, leaf), masked_tiles(d_ref, occ, leaf)
        up = pick(left, swap(d_tiles[3]), x_tiles[3])
        down = pick(left, x_tiles[0], swap(d_tiles[0]))
        cross_ref[leaf] = jnp.where(first_core, down, up)
        chip_ref[leaf] = jnp.where(first_core, up, down)
        for tiles, order_ref, flip_ref in ((x_tiles, store, flip), (d_tiles, store_dy, flip_dy)):
            order, flipped = reorder(tiles)
            order_ref[leaf] = jnp.concatenate(order, axis=1)
            flip_ref[leaf] = jnp.concatenate(flipped, axis=1)
    for ref in (store, flip, store_dy, flip_dy):
        ref[leaves] = jnp.zeros(ref.shape[1:], BF)


def prepare(meta, x, dy):
    leaves = x.shape[0]
    planes = jax.ShapeDtypeStruct((leaves, CH, TILE), BF)
    store = jax.ShapeDtypeStruct((leaves + 1,) + x.shape[1:], BF)
    table = jax.ShapeDtypeStruct((leaves, NEAR), jnp.int32)
    return pl.pallas_call(
        prepare_kernel,
        out_shape=(planes,) * 2
        + (store,) * 4
        + (jax.ShapeDtypeStruct((leaves, 4 * TILE), F32),)
        + (table,) * 3
        + (jax.ShapeDtypeStruct((leaves, TILE), jnp.int32),),
        in_specs=[vmem_spec()] * 3,
        out_specs=(vmem_spec(),) * 11,
        cost_estimate=cost(10**6, 4 * 10**6),
        compiler_params=params(),
        name="prepare",
    )(meta, x, dy)


def split_far(cross_ref, chip_ref, leaf):
    first_core = lax.rem(lax.axis_index("dom"), 2) == 0
    low = jnp.where(first_core, chip_ref[leaf], cross_ref[leaf])
    high = jnp.where(first_core, cross_ref[leaf], chip_ref[leaf])
    return low, high


def with_far(store, own, cross_ref, chip_ref, turned):
    leaves = own.shape[0] - 1
    for leaf in range(leaves):
        store[leaf] = own[leaf]
        low, high = split_far(cross_ref, chip_ref, leaf)
        store[leaves + leaf, :, 0:TILE] = swap(low) if turned else low
        store[leaves + leaf, :, 3 * TILE :] = swap(high) if turned else high
    store[2 * leaves] = own[leaves]


def place(table_ref, leaf, p, q, z):
    if (p, q, z) == (0, 0, 0):
        return leaf
    return table_ref[leaf, column_of(p, q, z)]


def third(flags_ref, leaf, z):
    return flags_ref[leaf, 0 if z < 0 else 1] > 0


def any_third(flags_ref):
    return flags_ref[0, 2] > 0


def stacked(store, flip, table_ref, leaf, z):
    rows = {}
    center = None
    for q in (0, -1, 1):
        mid = place(table_ref, leaf, 0, q, z)
        after = place(table_ref, leaf, 1, q, z)
        before = place(table_ref, leaf, -1, q, z)
        mine = store[mid]
        past = pick(left, store[after, :, 0:TILE], tile_of(mine, 0))
        ahead = pick(left, tile_of(mine, 3), store[before, :, 3 * TILE :])
        if q == 0:
            center = [swap(ahead)] + [tile_of(mine, k) for k in range(4)] + [swap(past)]
            rows[q] = center
        else:
            other = flip[jnp.minimum(mid, flip.shape[0] - 1)]
            flipped = [ahead] + [tile_of(other, k) for k in range(4)] + [past]
            rows[q] = shift_q(center, flipped, q)
    return jnp.concatenate([jnp.concatenate(rows[q], axis=1) for q in (-1, 0, 1)], axis=0)


def unstack(stack):
    return jnp.concatenate([stack[:, i * TILE : (i + 4) * TILE] for i in range(3)], axis=0)


def shift_c(value, r):
    if r == 0:
        return value
    test = cell_last if r > 0 else cell_first
    tiles = [tile_of(value, k) for k in range(value.shape[1] // TILE)]
    return jnp.concatenate([pick(test, jnp.zeros_like(t), roll(t, -r)) for t in tiles], axis=1)


def across_c(value, z):
    test = cell_last if z > 0 else cell_first
    tiles = [tile_of(value, k) for k in range(value.shape[1] // TILE)]
    return jnp.concatenate(
        [pick(test, roll(t, z * (EDGE - 1)), jnp.zeros_like(t)) for t in tiles], axis=1
    )


CONTRACT_LANES = (((1,), (1,)), ((), ()))


def dot_lanes(a, b):
    return lax.dot_general(a, b, CONTRACT_LANES, preferred_element_type=F32)


def grad_kernel(
    table_ref, flags_ref, store, flip, store_dy, flip_dy, total, stack_ref, stack_dy_ref
):
    leaves = stack_ref.shape[0]
    for leaf in range(leaves):
        stack = stacked(store, flip, table_ref, leaf, 0)
        stack_ref[leaf] = stack
        stack_dy_ref[leaf] = stacked(store_dy, flip_dy, table_ref, leaf, 0)
        wide = jnp.concatenate([shift_c(store_dy[leaf], -r) for r in (-1, 0, 1)], axis=0)
        term = dot_lanes(unstack(stack), wide)
        if leaf == 0:
            total[...] = term
        else:
            total[...] += term

    @pl.when(any_third(flags_ref))
    def _():
        for z in (-1, 1):
            for leaf in range(leaves):

                @pl.when(third(flags_ref, leaf, z))
                def _():
                    stack = stacked(store, flip, table_ref, leaf, z)
                    edge = across_c(store_dy[leaf], -z)
                    total[:, (z + 1) * CH : (z + 2) * CH] += dot_lanes(unstack(stack), edge)


def grad_terms(table, flags, store, flip, store_dy, flip_dy):
    leaves = store.shape[0] - 1
    stack = jax.ShapeDtypeStruct((leaves,) + STACK, BF)
    return pl.pallas_call(
        grad_kernel,
        out_shape=(jax.ShapeDtypeStruct((KROWS, 3 * CH), F32), stack, stack),
        in_specs=[smem_spec()] * 2 + [vmem_spec()] * 4,
        out_specs=(vmem_spec(),) * 3,
        cost_estimate=cost(10**9, 2 * 10**6),
        compiler_params=params(),
        name="grad_terms",
    )(table, flags, store, flip, store_dy, flip_dy)


def third_part(row):
    return (KROWS + row, 0) if row < SPLIT else (KROWS + row - SPLIT, 1)


def grad_far_kernel(
    table_ref, flags_ref, store_dy, cross_ref, chip_ref, near_total, keep_ref, send_ref,
    store, packed,
):
    leaves = store_dy.shape[0] - 1
    for leaf in range(leaves):
        low, high = split_far(cross_ref, chip_ref, leaf)
        store[0, leaf], store[1, leaf] = low, high
        store[2, leaf], store[3, leaf] = swap(low), swap(high)
    for i in range(4):
        store[i, leaves] = jnp.zeros((CH, TILE), BF)

    def far_rows(p, one, two, z):
        at = lambda leaf, q: place(table_ref, leaf, p, q, z)
        first, second = (0, 2) if p > 0 else (3, 1)
        pair = lambda a, b, q: pick(left, store[first, at(a, q)], store[second, at(b, q)])
        center = pair(one, two, 0)
        sides = [shift_q([center], [pair(two, one, q)], q)[0] for q in (-1, 1)]
        return jnp.concatenate([sides[0], center, sides[1]], axis=0)

    def end_plane(p, one, two):
        if p > 0:
            return pick(left, swap(store_dy[one, :, 3 * TILE :]), store_dy[two, :, 3 * TILE :])
        return pick(left, store_dy[one, :, 0:TILE], swap(store_dy[two, :, 0:TILE]))

    pairs = [(leaf, leaf + 1) for leaf in range(0, leaves, 2)]
    for p in (-1, 0, 1):
        term = None
        if p != 0:
            rows = jnp.concatenate([far_rows(p, a, b, 0) for a, b in pairs], axis=1)
            planes = jnp.concatenate([end_plane(p, a, b) for a, b in pairs], axis=1)
            wide = jnp.concatenate([shift_c(planes, -r) for r in (-1, 0, 1)], axis=0)
            term = dot_lanes(rows, wide)
        for q in (-1, 0, 1):
            row = SHIFTS.index((p, q)) * CH
            block = near_total[row : row + CH, :]
            if p != 0:
                block = block + term[(q + 1) * CH : (q + 2) * CH, :]
            packed[row : row + CH, :] = block[:, 0:TILE]
            low, side = third_part(row)
            packed[low : low + CH, side * CH : (side + 1) * CH] = block[:, TILE:]
    packed[2 * KROWS - SPLIT :, CH:] = jnp.zeros((2 * SPLIT - KROWS, CH), F32)

    @pl.when(any_third(flags_ref))
    def _():
        for z in (-1, 1):
            for leaf in range(leaves):

                @pl.when(third(flags_ref, leaf, z))
                def _():
                    for p in (-1, 1):
                        plane = end_plane(p, leaf, leaf)
                        plane = across_c(pick(left, plane, jnp.zeros_like(plane)), -z)
                        term = dot_lanes(far_rows(p, leaf, leaf, z), plane)
                        for q in (-1, 0, 1):
                            row, side = SHIFTS.index((p, q)) * CH, 0
                            if z > 0:
                                row, side = third_part(row)
                            packed[row : row + CH, side * CH : (side + 1) * CH] += term[
                                (q + 1) * CH : (q + 2) * CH, :
                            ]

    core = lax.rem(lax.axis_index("dom"), 2)
    rows = packed.shape[0] // 2
    keep_ref[...] = packed[pl.ds(pl.multiple_of(core * rows, 8), rows), :]
    send_ref[...] = packed[pl.ds(pl.multiple_of((1 - core) * rows, 8), rows), :]


def grad_far(table, flags, store_dy, cross, chip, total):
    leaves = store_dy.shape[0] - 1
    rows = KROWS + SPLIT
    shape = jax.ShapeDtypeStruct((rows // 2, TILE), F32)
    return pl.pallas_call(
        grad_far_kernel,
        out_shape=(shape, shape),
        in_specs=[smem_spec()] * 2 + [vmem_spec()] * 4,
        out_specs=(vmem_spec(), vmem_spec()),
        scratch_shapes=[
            pltpu.VMEM((4, leaves + 1, CH, TILE), BF),
            pltpu.VMEM((rows, TILE), F32),
        ],
        cost_estimate=cost(10**8, 2 * 10**6),
        compiler_params=params(),
        name="grad_far",
    )(table, flags, store_dy, cross, chip, total)


def vmem_spec():
    return pl.BlockSpec(memory_space=pltpu.VMEM)


def any_spec():
    return pl.BlockSpec(memory_space=pl.ANY)


def smem_spec():
    return pl.BlockSpec(memory_space=pltpu.SMEM)


def params():
    return pltpu.CompilerParams(vmem_limit_bytes=VMEM_LIMIT)


def cost(flops, bytes_accessed):
    return pl.CostEstimate(flops=flops, bytes_accessed=bytes_accessed, transcendentals=0)


def ordered_taps(w_ref, turned):
    def tap(index, r):
        p, q = SHIFTS[index]
        return (p + 1) * 9 + (q + 1) * 3 + r + 1

    if turned:
        return jnp.concatenate(
            [
                jnp.concatenate([w_ref[26 - tap(index, r)] for index in range(9)], axis=1)
                for r in (-1, 0, 1)
            ],
            axis=0,
        )
    return jnp.concatenate(
        [
            jnp.concatenate([w_ref[tap(index, r)] for r in (-1, 0, 1)], axis=1)
            for index in range(9)
        ],
        axis=0,
    ).T


def finish(occ, leaf, total):
    rounded = total.astype(BF)
    tiles = restore(*[tile_of(rounded, k) for k in range(4)])
    return jnp.concatenate([t * spread(occ[k], leaf) for k, t in enumerate(tiles)], axis=1)


def leaf_sum(taps, near_x):
    wide = jnp.dot(taps, near_x, preferred_element_type=F32)
    total = wide[CH : 2 * CH]
    for r in (-1, 1):
        total = total + shift_c(wide[(r + 1) * CH : (r + 2) * CH], r)
    return total


def far_tiles(far, table_ref, leaf):
    at = lambda p, q: place(table_ref, leaf, p, q, 0)
    center = pick(left, far[1, at(-1, 0)], far[1, at(1, 0)])
    flipped = {q: pick(left, far[0, at(1, q)], far[0, at(-1, q)]) for q in (-1, 1)}
    sides = [shift_q([center], [flipped[q]], q)[0] for q in (-1, 1)]
    return jnp.concatenate([sides[0], center, sides[1]], axis=0)


def conv_kernel(
    turned, far_table_ref, all_table_ref, flags_ref, occ_ref, own, flip, cross_ref, chip_ref, w_ref,
    stack_ref, _, out_ref, done_ref, far, store,
):
    leaves = out_ref.shape[0]
    occ = [tile_of(occ_ref[...], k) for k in range(4)]
    done_ref[...] = jnp.zeros(done_ref.shape, F32)
    taps = ordered_taps(w_ref, turned)
    for leaf in range(leaves):
        low, high = split_far(cross_ref, chip_ref, leaf)
        both = pick(left, high, low) if turned else pick(left, low, high)
        far[0, leaf], far[1, leaf] = (swap(both), both) if turned else (both, swap(both))
    far[0, leaves] = far[1, leaves] = jnp.zeros((CH, TILE), BF)
    for leaf in range(leaves):
        planes = far_tiles(far, far_table_ref, leaf)
        zero = jnp.zeros_like(planes)
        stack = stack_ref[leaf]
        stack = jnp.concatenate(
            [
                tile_of(stack, 0) + pick(left, planes, zero),
                stack[:, TILE : 5 * TILE],
                tile_of(stack, 5) + pick(left, zero, planes),
            ],
            axis=1,
        )
        out_ref[leaf] = finish(occ, leaf, leaf_sum(taps, unstack(stack)))

    @pl.when(any_third(flags_ref))
    def _():
        with_far(store, own, cross_ref, chip_ref, turned)
        for leaf in range(leaves):
            total = leaf_sum(taps, unstack(stacked(store, flip, all_table_ref, leaf, 0)))
            for z in (-1, 1):
                near_z = unstack(stacked(store, flip, all_table_ref, leaf, z))
                part = jnp.dot(
                    taps[(z + 1) * CH : (z + 2) * CH], near_z, preferred_element_type=F32
                )
                total = total + across_c(part, z)
            out_ref[leaf] = finish(occ, leaf, total)


def conv(far_table, all_table, flags, occ, own, flip, cross, chip, weight, stack, after, turned):
    leaves = stack.shape[0]
    return pl.pallas_call(
        functools.partial(conv_kernel, turned),
        out_shape=(
            jax.ShapeDtypeStruct((leaves, CH, 4 * TILE), BF),
            jax.ShapeDtypeStruct((8, TILE), F32),
        ),
        in_specs=[smem_spec()] * 3 + [vmem_spec()] * 7 + [any_spec()],
        out_specs=(vmem_spec(),) * 2,
        scratch_shapes=[
            pltpu.VMEM((2, leaves + 1, CH, TILE), BF),
            pltpu.VMEM((2 * leaves + 1, CH, 4 * TILE), BF),
        ],
        cost_estimate=cost(10**9, 2 * 10**6),
        compiler_params=params(),
        name="in_grad_conv" if turned else "out_conv",
    )(far_table, all_table, flags, occ, own, flip, cross, chip, weight, stack, after)


def split_kernel(keep_ref, got_ref, *refs):
    *out_refs, total = refs
    total[...] = keep_ref[...] + got_ref[...]
    lane = lax.rem(lax.axis_index("dom") // 2, 4)
    rows = out_refs[0].shape[0]
    for mask, out_ref in enumerate(out_refs):
        at = pl.multiple_of(jnp.bitwise_xor(lane, mask) * rows, 8)
        out_ref[...] = total[pl.ds(at, rows), :]


def split_chunks(keep, got):
    chunk = jax.ShapeDtypeStruct((keep.shape[0] // 4, TILE), F32)
    return pl.pallas_call(
        split_kernel,
        out_shape=(chunk,) * 4,
        in_specs=[vmem_spec()] * 2,
        out_specs=(vmem_spec(),) * 4,
        scratch_shapes=[pltpu.VMEM(keep.shape, F32)],
        cost_estimate=cost(10**5, 10**6),
        compiler_params=params(),
        name="split_chunks",
    )(keep, got)


def sum_kernel(own_ref, *refs):
    *got_refs, _, out_ref = refs
    total = own_ref[...]
    for got_ref in got_refs:
        total = total + got_ref[...]
    out_ref[...] = total


def sum_chunks(own, got, after):
    return pl.pallas_call(
        sum_kernel,
        out_shape=jax.ShapeDtypeStruct(own.shape, F32),
        in_specs=[vmem_spec()] * (1 + len(got)) + [any_spec()],
        out_specs=vmem_spec(),
        cost_estimate=cost(10**5, 3 * 10**5),
        compiler_params=params(),
        name="sum_chunks",
    )(own, *got, after)


def join_kernel(*refs):
    *parts, _, out_ref = refs
    lane = lax.rem(lax.axis_index("dom") // 2, 4)
    rows = parts[0].shape[0]
    for mask, part in enumerate(parts):
        at = pl.multiple_of(jnp.bitwise_xor(lane, mask) * rows, 8)
        out_ref[pl.ds(at, rows), :] = part[...]


def join_chunks(parts, after):
    rows = parts[0].shape[0]
    return pl.pallas_call(
        join_kernel,
        out_shape=jax.ShapeDtypeStruct((len(parts) * rows, TILE), F32),
        in_specs=[vmem_spec()] * len(parts) + [any_spec()],
        out_specs=vmem_spec(),
        cost_estimate=cost(10**5, 5 * 10**5),
        compiler_params=params(),
        name="join_chunks",
    )(*parts, after)


def half_taps(half):
    found = []
    for index, (p, q) in enumerate(SHIFTS):
        for r in (-1, 0, 1):
            row, side = index * CH, r + 1
            if r == 1:
                row, side = third_part(row)
            if row // (7 * CH) == half:
                found.append(((p + 1) * 9 + (q + 1) * 3 + r + 1, row - half * 7 * CH, side))
    return found


def unpack_kernel(scale, mine, half_ref, *refs):
    *_, out_ref, taps, sem = refs
    core = lax.rem(lax.axis_index("dom"), 2)

    def write(half):
        found = half_taps(half)
        for i, (tap, row, side) in enumerate(found):
            block = half_ref[row : row + CH, side * CH : (side + 1) * CH]
            taps[i] = block * scale
            pltpu.make_async_copy(taps.at[i], out_ref.at[tap], sem.at[i]).start()
        for i, (tap, row, side) in enumerate(found):
            pltpu.make_async_copy(taps.at[i], out_ref.at[tap], sem.at[i]).wait()

    first = core == 0 if mine else core == 1
    pl.when(first)(lambda: write(0))
    pl.when(jnp.logical_not(first))(lambda: write(1))


def unpack(half, scale, so_far=None):
    rest = [] if so_far is None else [so_far]
    hbm = pl.BlockSpec(memory_space=pltpu.HBM)
    return pl.pallas_call(
        functools.partial(unpack_kernel, scale, not rest),
        out_shape=jax.ShapeDtypeStruct((27, CH, CH), F32),
        in_specs=[vmem_spec()] + [hbm] * len(rest),
        out_specs=hbm,
        input_output_aliases={1: 0} if rest else {},
        scratch_shapes=[pltpu.VMEM((14, CH, CH), F32), pltpu.SemaphoreType.DMA((14,))],
        cost_estimate=cost(10**6, 10**6),
        compiler_params=params(),
        name="unpack_other" if rest else "unpack_own",
    )(half, *rest)


def exchange(array, mask, size):
    return lax.ppermute(array, "dom", [(i, i ^ mask) for i in range(size)])


def shards(features, cotangent, weight, mask_words, neighbors):
    leaves, channels, voxels = features.shape
    size = lax.axis_size("dom")
    meta = jnp.concatenate([neighbors, mask_words], axis=1)
    to_cross, to_chip, *fields, occ, all_table, own_table, far_table, flags = prepare(
        meta, features, cotangent
    )
    store, flip, store_dy, flip_dy = fields
    between = [(i, i + 1) for i in range(1, size - 1, 2)]
    chip = exchange(to_chip, 1, size)
    cross = lax.ppermute(to_cross, "dom", between + [(j, i) for i, j in between])

    total, stack, stack_dy = grad_terms(own_table, flags, *fields)
    keep, send = grad_far(far_table, flags, store_dy, cross, chip, total)
    own, *to_send = split_chunks(keep, exchange(send, 1, size))
    got = [exchange(to_send[m - 1], 2 * m, size) for m in (2, 3, 1)]
    out_features, out_done = conv(
        far_table, all_table, flags, occ, store, flip, cross, chip, weight, stack,
        to_send[2], False,
    )
    own = sum_chunks(own, got, out_done)
    if size > GROUP:
        groups = [[j * GROUP + i for j in range(size // GROUP)] for i in range(GROUP)]
        own = lax.psum(own, "dom", axis_index_groups=groups)
    back = [exchange(own, 2 * m, size) for m in (1, 2, 3)]
    in_grad, in_done = conv(
        far_table, all_table, flags, occ, store_dy, flip_dy, cross, chip, weight, stack_dy,
        own, True,
    )
    half = join_chunks([own] + back, in_done)
    other = exchange(half, 1, size)
    scale = float(size * leaves * voxels) ** -0.5
    weight_grad = unpack(other, scale, unpack(half, scale))
    return (out_features, in_grad, weight_grad)


def solution(mesh):
    split = P(("scene", "dom"), None, None)
    flat = P(("scene", "dom"), None)
    return jax.shard_map(
        shards,
        mesh=mesh,
        in_specs=(split, split, P(), flat, flat),
        out_specs=(split, split, P("scene", None, None)),
        check_vma=False,
    )
```

```python
import functools

import jax
import jax.numpy as jnp
from jax import lax
from jax.experimental import pallas as pl
from jax.experimental.pallas import tpu as pltpu
from jax.sharding import PartitionSpec as P

BITS = 30
NEAR = 26
EDGE = 8
FACE = EDGE * EDGE
TILE = 128
CH = 64
GROUP = 8
KROWS = 9 * CH
SPLIT = 5 * CH
STACK = (3 * CH, 6 * TILE)
VMEM_LIMIT = 16 * 1024 * 1024
BF = jnp.bfloat16
F32 = jnp.float32

SHIFTS = [(p, q) for p in (-1, 0, 1) for q in (-1, 0, 1)]


def column_of(p, q, r):
    tap = (p + 1) * 9 + (q + 1) * 3 + r + 1
    return tap if tap < 13 else tap - 1


def lane_ids(rows):
    return lax.broadcasted_iota(jnp.int32, (rows, TILE), 1)


def pick(test, a, b):
    rows = 16 if a.dtype == BF else 8
    mask = test(lane_ids(rows))
    return jnp.concatenate(
        [
            jnp.where(mask, a[i : i + rows], b[i : i + rows])
            for i in range(0, a.shape[0], rows)
        ],
        axis=0,
    )


def left(lane):
    return lane < FACE


def row_first(lane):
    return (lane // EDGE) % EDGE == 0


def row_last(lane):
    return (lane // EDGE) % EDGE == EDGE - 1


def cell_first(lane):
    return lane % EDGE == 0


def cell_last(lane):
    return lane % EDGE == EDGE - 1


def roll(value, amount):
    return pltpu.roll(value, amount % TILE, 1)


def swap(value):
    return roll(value, FACE)


def tile_of(value, k):
    return value[:, k * TILE : (k + 1) * TILE]


def occupancy_tile(words, tile):
    lane = lane_ids(words.shape[0]) + tile * TILE
    first, last = (tile * TILE) // BITS, (tile * TILE + TILE - 1) // BITS
    word = jnp.broadcast_to(words[:, first : first + 1], lane.shape)
    place = lane - first * BITS
    for w in range(first + 1, last + 1):
        past = lane >= w * BITS
        word = jnp.where(past, jnp.broadcast_to(words[:, w : w + 1], lane.shape), word)
        place = jnp.where(past, lane - w * BITS, place)
    return (jnp.right_shift(word, place) & 1).astype(F32)


def spread(occ, leaf):
    part = jnp.broadcast_to(occ[leaf : leaf + 1, :], (16, TILE)).astype(BF)
    return jnp.concatenate([part] * (CH // 16), axis=0)


def masked_tiles(field_ref, occ, leaf):
    return [
        field_ref[leaf, :, k * TILE : (k + 1) * TILE] * spread(occ[k], leaf) for k in range(4)
    ]


def reorder(tiles):
    n0, n1, n2, n3 = tiles
    r0, r1, r2, r3 = [swap(t) for t in tiles]
    order = [pick(left, n0, r2), pick(left, r0, n2), pick(left, n1, r3), pick(left, r1, n3)]
    flipped = [pick(left, n2, r0), pick(left, r2, n0), pick(left, n3, r1), pick(left, r3, n1)]
    return order, flipped


def restore(t0, t1, t2, t3):
    return [
        pick(left, t0, swap(t1)),
        pick(left, t2, swap(t3)),
        pick(left, swap(t0), t1),
        pick(left, swap(t2), t3),
    ]


def shift_q(center, flipped, q):
    test = row_last if q < 0 else row_first
    return [roll(pick(test, m, c), -q * EDGE) for m, c in zip(flipped, center)]


def write_tables(near, all_ref, own_ref, far_ref, flags_ref):
    leaves = near.shape[0]
    first = lax.axis_index("dom") * leaves
    slot = near - first
    absent = near < 0
    here = (slot >= 0) & (slot < leaves) & jnp.logical_not(absent)
    other = jnp.where(slot < 0, slot + leaves, slot - leaves)
    own_ref[...] = jnp.where(here, slot, leaves)
    far_ref[...] = jnp.where(here | absent, leaves, other)
    all_ref[...] = jnp.where(absent, 2 * leaves, jnp.where(here, slot, other + leaves))
    column = lax.broadcasted_iota(jnp.int32, near.shape, 1)
    cell = lax.rem(jnp.where(column < 13, column, column + 1), 3)
    flags = [
        jnp.max(jnp.where(present, 1, 0).astype(F32), axis=1, keepdims=True)
        for present in (
            jnp.logical_not(absent) & (cell == 0),
            jnp.logical_not(absent) & (cell == 2),
        )
    ]
    some = jnp.max(jnp.maximum(*flags), axis=0, keepdims=True)
    lane = lane_ids(leaves)
    table = jnp.where(lane == 0, flags[0], jnp.where(lane == 1, flags[1], some))
    flags_ref[...] = table.astype(jnp.int32)


def prepare_kernel(
    meta_ref, x_ref, d_ref, cross_ref, chip_ref, store, flip, store_dy, flip_dy, occ_ref,
    all_ref, own_ref, far_ref, flags_ref,
):
    leaves = x_ref.shape[0]
    words = meta_ref[:, NEAR:]
    occ = [occupancy_tile(words, k) for k in range(4)]
    occ_ref[...] = jnp.concatenate(occ, axis=1)
    write_tables(meta_ref[:, 0:NEAR], all_ref, own_ref, far_ref, flags_ref)
    first_core = lax.rem(lax.axis_index("dom"), 2) == 0
    for leaf in range(leaves):
        x_tiles, d_tiles = masked_tiles(x_ref, occ, leaf), masked_tiles(d_ref, occ, leaf)
        up = pick(left, swap(d_tiles[3]), x_tiles[3])
        down = pick(left, x_tiles[0], swap(d_tiles[0]))
        cross_ref[leaf] = jnp.where(first_core, down, up)
        chip_ref[leaf] = jnp.where(first_core, up, down)
        for tiles, order_ref, flip_ref in ((x_tiles, store, flip), (d_tiles, store_dy, flip_dy)):
            order, flipped = reorder(tiles)
            order_ref[leaf] = jnp.concatenate(order, axis=1)
            flip_ref[leaf] = jnp.concatenate(flipped, axis=1)
    for ref in (store, flip, store_dy, flip_dy):
        ref[leaves] = jnp.zeros(ref.shape[1:], BF)


def prepare(meta, x, dy):
    leaves = x.shape[0]
    planes = jax.ShapeDtypeStruct((leaves, CH, TILE), BF)
    store = jax.ShapeDtypeStruct((leaves + 1,) + x.shape[1:], BF)
    table = jax.ShapeDtypeStruct((leaves, NEAR), jnp.int32)
    return pl.pallas_call(
        prepare_kernel,
        out_shape=(planes,) * 2
        + (store,) * 4
        + (jax.ShapeDtypeStruct((leaves, 4 * TILE), F32),)
        + (table,) * 3
        + (jax.ShapeDtypeStruct((leaves, TILE), jnp.int32),),
        in_specs=[vmem_spec()] * 3,
        out_specs=(vmem_spec(),) * 11,
        cost_estimate=cost(10**6, 4 * 10**6),
        compiler_params=params(),
        name="prepare",
    )(meta, x, dy)


def split_far(cross_ref, chip_ref, leaf):
    first_core = lax.rem(lax.axis_index("dom"), 2) == 0
    low = jnp.where(first_core, chip_ref[leaf], cross_ref[leaf])
    high = jnp.where(first_core, cross_ref[leaf], chip_ref[leaf])
    return low, high


def with_far(store, own, cross_ref, chip_ref, turned):
    leaves = own.shape[0] - 1
    for leaf in range(leaves):
        store[leaf] = own[leaf]
        low, high = split_far(cross_ref, chip_ref, leaf)
        store[leaves + leaf, :, 0:TILE] = swap(low) if turned else low
        store[leaves + leaf, :, 3 * TILE :] = swap(high) if turned else high
    store[2 * leaves] = own[leaves]


def place(table_ref, leaf, p, q, z):
    if (p, q, z) == (0, 0, 0):
        return leaf
    return table_ref[leaf, column_of(p, q, z)]


def third(flags_ref, leaf, z):
    return flags_ref[leaf, 0 if z < 0 else 1] > 0


def any_third(flags_ref):
    return flags_ref[0, 2] > 0


def stacked(store, flip, table_ref, leaf, z):
    rows = {}
    center = None
    for q in (0, -1, 1):
        mid = place(table_ref, leaf, 0, q, z)
        after = place(table_ref, leaf, 1, q, z)
        before = place(table_ref, leaf, -1, q, z)
        mine = store[mid]
        past = pick(left, store[after, :, 0:TILE], tile_of(mine, 0))
        ahead = pick(left, tile_of(mine, 3), store[before, :, 3 * TILE :])
        if q == 0:
            center = [swap(ahead)] + [tile_of(mine, k) for k in range(4)] + [swap(past)]
            rows[q] = center
        else:
            other = flip[jnp.minimum(mid, flip.shape[0] - 1)]
            flipped = [ahead] + [tile_of(other, k) for k in range(4)] + [past]
            rows[q] = shift_q(center, flipped, q)
    return jnp.concatenate([jnp.concatenate(rows[q], axis=1) for q in (-1, 0, 1)], axis=0)


def unstack(stack):
    return jnp.concatenate([stack[:, i * TILE : (i + 4) * TILE] for i in range(3)], axis=0)


def shift_c(value, r):
    if r == 0:
        return value
    test = cell_last if r > 0 else cell_first
    tiles = [tile_of(value, k) for k in range(value.shape[1] // TILE)]
    return jnp.concatenate([pick(test, jnp.zeros_like(t), roll(t, -r)) for t in tiles], axis=1)


def across_c(value, z):
    test = cell_last if z > 0 else cell_first
    tiles = [tile_of(value, k) for k in range(value.shape[1] // TILE)]
    return jnp.concatenate(
        [pick(test, roll(t, z * (EDGE - 1)), jnp.zeros_like(t)) for t in tiles], axis=1
    )


CONTRACT_LANES = (((1,), (1,)), ((), ()))


def dot_lanes(a, b):
    return lax.dot_general(a, b, CONTRACT_LANES, preferred_element_type=F32)


def grad_kernel(
    table_ref, flags_ref, store, flip, store_dy, flip_dy, _, total, stack_ref, stack_dy_ref
):
    leaves = stack_ref.shape[0]
    for leaf in range(leaves):
        stack = stacked(store, flip, table_ref, leaf, 0)
        stack_ref[leaf] = stack
        stack_dy_ref[leaf] = stacked(store_dy, flip_dy, table_ref, leaf, 0)
        wide = jnp.concatenate([shift_c(store_dy[leaf], -r) for r in (-1, 0, 1)], axis=0)
        term = dot_lanes(unstack(stack), wide)
        if leaf == 0:
            total[...] = term
        else:
            total[...] += term

    @pl.when(any_third(flags_ref))
    def _():
        for z in (-1, 1):
            for leaf in range(leaves):

                @pl.when(third(flags_ref, leaf, z))
                def _():
                    stack = stacked(store, flip, table_ref, leaf, z)
                    edge = across_c(store_dy[leaf], -z)
                    total[:, (z + 1) * CH : (z + 2) * CH] += dot_lanes(unstack(stack), edge)


def grad_terms(table, flags, store, flip, store_dy, flip_dy, after):
    leaves = store.shape[0] - 1
    stack = jax.ShapeDtypeStruct((leaves,) + STACK, BF)
    return pl.pallas_call(
        grad_kernel,
        out_shape=(jax.ShapeDtypeStruct((KROWS, 3 * CH), F32), stack, stack),
        in_specs=[smem_spec()] * 2 + [vmem_spec()] * 4 + [any_spec()],
        out_specs=(vmem_spec(),) * 3,
        cost_estimate=cost(10**9, 2 * 10**6),
        compiler_params=params(),
        name="grad_terms",
    )(table, flags, store, flip, store_dy, flip_dy, after)


def third_part(row):
    return (KROWS + row, 0) if row < SPLIT else (KROWS + row - SPLIT, 1)


def grad_far_kernel(
    table_ref, flags_ref, store_dy, cross_ref, chip_ref, near_total, keep_ref, send_ref,
    store, packed,
):
    leaves = store_dy.shape[0] - 1
    for leaf in range(leaves):
        low, high = split_far(cross_ref, chip_ref, leaf)
        store[0, leaf], store[1, leaf] = low, high
        store[2, leaf], store[3, leaf] = swap(low), swap(high)
    for i in range(4):
        store[i, leaves] = jnp.zeros((CH, TILE), BF)

    def far_rows(p, one, two, z):
        at = lambda leaf, q: place(table_ref, leaf, p, q, z)
        first, second = (0, 2) if p > 0 else (3, 1)
        pair = lambda a, b, q: pick(left, store[first, at(a, q)], store[second, at(b, q)])
        center = pair(one, two, 0)
        sides = [shift_q([center], [pair(two, one, q)], q)[0] for q in (-1, 1)]
        return jnp.concatenate([sides[0], center, sides[1]], axis=0)

    def end_plane(p, one, two):
        if p > 0:
            return pick(left, swap(store_dy[one, :, 3 * TILE :]), store_dy[two, :, 3 * TILE :])
        return pick(left, store_dy[one, :, 0:TILE], swap(store_dy[two, :, 0:TILE]))

    pairs = [(leaf, leaf + 1) for leaf in range(0, leaves, 2)]
    for p in (-1, 0, 1):
        term = None
        if p != 0:
            rows = jnp.concatenate([far_rows(p, a, b, 0) for a, b in pairs], axis=1)
            planes = jnp.concatenate([end_plane(p, a, b) for a, b in pairs], axis=1)
            wide = jnp.concatenate([shift_c(planes, -r) for r in (-1, 0, 1)], axis=0)
            term = dot_lanes(rows, wide)
        for q in (-1, 0, 1):
            row = SHIFTS.index((p, q)) * CH
            block = near_total[row : row + CH, :]
            if p != 0:
                block = block + term[(q + 1) * CH : (q + 2) * CH, :]
            packed[row : row + CH, :] = block[:, 0:TILE]
            low, side = third_part(row)
            packed[low : low + CH, side * CH : (side + 1) * CH] = block[:, TILE:]
    packed[2 * KROWS - SPLIT :, CH:] = jnp.zeros((2 * SPLIT - KROWS, CH), F32)

    @pl.when(any_third(flags_ref))
    def _():
        for z in (-1, 1):
            for leaf in range(leaves):

                @pl.when(third(flags_ref, leaf, z))
                def _():
                    for p in (-1, 1):
                        plane = end_plane(p, leaf, leaf)
                        plane = across_c(pick(left, plane, jnp.zeros_like(plane)), -z)
                        term = dot_lanes(far_rows(p, leaf, leaf, z), plane)
                        for q in (-1, 0, 1):
                            row, side = SHIFTS.index((p, q)) * CH, 0
                            if z > 0:
                                row, side = third_part(row)
                            packed[row : row + CH, side * CH : (side + 1) * CH] += term[
                                (q + 1) * CH : (q + 2) * CH, :
                            ]

    core = lax.rem(lax.axis_index("dom"), 2)
    rows = packed.shape[0] // 2
    keep_ref[...] = packed[pl.ds(pl.multiple_of(core * rows, 8), rows), :]
    send_ref[...] = packed[pl.ds(pl.multiple_of((1 - core) * rows, 8), rows), :]


def grad_far(table, flags, store_dy, cross, chip, total):
    leaves = store_dy.shape[0] - 1
    rows = KROWS + SPLIT
    shape = jax.ShapeDtypeStruct((rows // 2, TILE), F32)
    return pl.pallas_call(
        grad_far_kernel,
        out_shape=(shape, shape),
        in_specs=[smem_spec()] * 2 + [vmem_spec()] * 4,
        out_specs=(vmem_spec(), vmem_spec()),
        scratch_shapes=[
            pltpu.VMEM((4, leaves + 1, CH, TILE), BF),
            pltpu.VMEM((rows, TILE), F32),
        ],
        cost_estimate=cost(10**8, 2 * 10**6),
        compiler_params=params(),
        name="grad_far",
    )(table, flags, store_dy, cross, chip, total)


def vmem_spec():
    return pl.BlockSpec(memory_space=pltpu.VMEM)


def any_spec():
    return pl.BlockSpec(memory_space=pl.ANY)


def smem_spec():
    return pl.BlockSpec(memory_space=pltpu.SMEM)


def params():
    return pltpu.CompilerParams(vmem_limit_bytes=VMEM_LIMIT)


def cost(flops, bytes_accessed):
    return pl.CostEstimate(flops=flops, bytes_accessed=bytes_accessed, transcendentals=0)


def ordered_taps(w_ref, turned):
    def tap(index, r):
        p, q = SHIFTS[index]
        return (p + 1) * 9 + (q + 1) * 3 + r + 1

    if turned:
        return jnp.concatenate(
            [
                jnp.concatenate([w_ref[26 - tap(index, r)] for index in range(9)], axis=1)
                for r in (-1, 0, 1)
            ],
            axis=0,
        )
    return jnp.concatenate(
        [
            jnp.concatenate([w_ref[tap(index, r)] for r in (-1, 0, 1)], axis=1)
            for index in range(9)
        ],
        axis=0,
    ).T


def finish(occ, leaf, total):
    rounded = total.astype(BF)
    tiles = restore(*[tile_of(rounded, k) for k in range(4)])
    return jnp.concatenate([t * spread(occ[k], leaf) for k, t in enumerate(tiles)], axis=1)


def leaf_sum(taps, near_x):
    wide = jnp.dot(taps, near_x, preferred_element_type=F32)
    total = wide[CH : 2 * CH]
    for r in (-1, 1):
        total = total + shift_c(wide[(r + 1) * CH : (r + 2) * CH], r)
    return total


def far_tiles(far, table_ref, leaf):
    at = lambda p, q: place(table_ref, leaf, p, q, 0)
    center = pick(left, far[1, at(-1, 0)], far[1, at(1, 0)])
    flipped = {q: pick(left, far[0, at(1, q)], far[0, at(-1, q)]) for q in (-1, 1)}
    sides = [shift_q([center], [flipped[q]], q)[0] for q in (-1, 1)]
    return jnp.concatenate([sides[0], center, sides[1]], axis=0)


def conv_kernel(
    turned, far_table_ref, all_table_ref, flags_ref, occ_ref, own, flip, cross_ref, chip_ref, w_ref,
    stack_ref, _, out_ref, done_ref, far, store,
):
    leaves = out_ref.shape[0]
    occ = [tile_of(occ_ref[...], k) for k in range(4)]
    done_ref[...] = jnp.zeros(done_ref.shape, F32)
    taps = ordered_taps(w_ref, turned)
    for leaf in range(leaves):
        low, high = split_far(cross_ref, chip_ref, leaf)
        both = pick(left, high, low) if turned else pick(left, low, high)
        far[0, leaf], far[1, leaf] = (swap(both), both) if turned else (both, swap(both))
    far[0, leaves] = far[1, leaves] = jnp.zeros((CH, TILE), BF)
    for leaf in range(leaves):
        planes = far_tiles(far, far_table_ref, leaf)
        zero = jnp.zeros_like(planes)
        stack = stack_ref[leaf]
        stack = jnp.concatenate(
            [
                tile_of(stack, 0) + pick(left, planes, zero),
                stack[:, TILE : 5 * TILE],
                tile_of(stack, 5) + pick(left, zero, planes),
            ],
            axis=1,
        )
        out_ref[leaf] = finish(occ, leaf, leaf_sum(taps, unstack(stack)))

    @pl.when(any_third(flags_ref))
    def _():
        with_far(store, own, cross_ref, chip_ref, turned)
        for leaf in range(leaves):
            total = leaf_sum(taps, unstack(stacked(store, flip, all_table_ref, leaf, 0)))
            for z in (-1, 1):
                near_z = unstack(stacked(store, flip, all_table_ref, leaf, z))
                part = jnp.dot(
                    taps[(z + 1) * CH : (z + 2) * CH], near_z, preferred_element_type=F32
                )
                total = total + across_c(part, z)
            out_ref[leaf] = finish(occ, leaf, total)


def conv(far_table, all_table, flags, occ, own, flip, cross, chip, weight, stack, after, turned):
    leaves = stack.shape[0]
    return pl.pallas_call(
        functools.partial(conv_kernel, turned),
        out_shape=(
            jax.ShapeDtypeStruct((leaves, CH, 4 * TILE), BF),
            jax.ShapeDtypeStruct((8, TILE), F32),
        ),
        in_specs=[smem_spec()] * 3 + [vmem_spec()] * 7 + [any_spec()],
        out_specs=(vmem_spec(),) * 2,
        scratch_shapes=[
            pltpu.VMEM((2, leaves + 1, CH, TILE), BF),
            pltpu.VMEM((2 * leaves + 1, CH, 4 * TILE), BF),
        ],
        cost_estimate=cost(10**9, 2 * 10**6),
        compiler_params=params(),
        name="in_grad_conv" if turned else "out_conv",
    )(far_table, all_table, flags, occ, own, flip, cross, chip, weight, stack, after)


def split_kernel(keep_ref, got_ref, *refs):
    *out_refs, total = refs
    total[...] = keep_ref[...] + got_ref[...]
    lane = lax.rem(lax.axis_index("dom") // 2, 4)
    rows = out_refs[0].shape[0]
    for mask, out_ref in enumerate(out_refs):
        at = pl.multiple_of(jnp.bitwise_xor(lane, mask) * rows, 8)
        out_ref[...] = total[pl.ds(at, rows), :]


def split_chunks(keep, got):
    chunk = jax.ShapeDtypeStruct((keep.shape[0] // 4, TILE), F32)
    return pl.pallas_call(
        split_kernel,
        out_shape=(chunk,) * 4,
        in_specs=[vmem_spec()] * 2,
        out_specs=(vmem_spec(),) * 4,
        scratch_shapes=[pltpu.VMEM(keep.shape, F32)],
        cost_estimate=cost(10**5, 10**6),
        compiler_params=params(),
        name="split_chunks",
    )(keep, got)


def sum_kernel(own_ref, *refs):
    *got_refs, _, out_ref = refs
    total = own_ref[...]
    for got_ref in got_refs:
        total = total + got_ref[...]
    out_ref[...] = total


def sum_chunks(own, got, after):
    return pl.pallas_call(
        sum_kernel,
        out_shape=jax.ShapeDtypeStruct(own.shape, F32),
        in_specs=[vmem_spec()] * (1 + len(got)) + [any_spec()],
        out_specs=vmem_spec(),
        cost_estimate=cost(10**5, 3 * 10**5),
        compiler_params=params(),
        name="sum_chunks",
    )(own, *got, after)


def join_kernel(*refs):
    *parts, _, out_ref = refs
    lane = lax.rem(lax.axis_index("dom") // 2, 4)
    rows = parts[0].shape[0]
    for mask, part in enumerate(parts):
        at = pl.multiple_of(jnp.bitwise_xor(lane, mask) * rows, 8)
        out_ref[pl.ds(at, rows), :] = part[...]


def join_chunks(parts, after):
    rows = parts[0].shape[0]
    return pl.pallas_call(
        join_kernel,
        out_shape=jax.ShapeDtypeStruct((len(parts) * rows, TILE), F32),
        in_specs=[vmem_spec()] * len(parts) + [any_spec()],
        out_specs=vmem_spec(),
        cost_estimate=cost(10**5, 5 * 10**5),
        compiler_params=params(),
        name="join_chunks",
    )(*parts, after)


def half_taps(half):
    found = []
    for index, (p, q) in enumerate(SHIFTS):
        for r in (-1, 0, 1):
            row, side = index * CH, r + 1
            if r == 1:
                row, side = third_part(row)
            if row // (7 * CH) == half:
                found.append(((p + 1) * 9 + (q + 1) * 3 + r + 1, row - half * 7 * CH, side))
    return found


def unpack_kernel(scale, mine, half_ref, *refs):
    *_, out_ref, taps, sem = refs
    core = lax.rem(lax.axis_index("dom"), 2)

    def write(half):
        found = half_taps(half)
        for i, (tap, row, side) in enumerate(found):
            block = half_ref[row : row + CH, side * CH : (side + 1) * CH]
            taps[i] = block * scale
            pltpu.make_async_copy(taps.at[i], out_ref.at[tap], sem.at[i]).start()
        for i, (tap, row, side) in enumerate(found):
            pltpu.make_async_copy(taps.at[i], out_ref.at[tap], sem.at[i]).wait()

    first = core == 0 if mine else core == 1
    pl.when(first)(lambda: write(0))
    pl.when(jnp.logical_not(first))(lambda: write(1))


def unpack(half, scale, so_far=None):
    rest = [] if so_far is None else [so_far]
    hbm = pl.BlockSpec(memory_space=pltpu.HBM)
    return pl.pallas_call(
        functools.partial(unpack_kernel, scale, not rest),
        out_shape=jax.ShapeDtypeStruct((27, CH, CH), F32),
        in_specs=[vmem_spec()] + [hbm] * len(rest),
        out_specs=hbm,
        input_output_aliases={1: 0} if rest else {},
        scratch_shapes=[pltpu.VMEM((14, CH, CH), F32), pltpu.SemaphoreType.DMA((14,))],
        cost_estimate=cost(10**6, 10**6),
        compiler_params=params(),
        name="unpack_other" if rest else "unpack_own",
    )(half, *rest)


def exchange(array, mask, size):
    return lax.ppermute(array, "dom", [(i, i ^ mask) for i in range(size)])


def shards(features, cotangent, weight, mask_words, neighbors):
    leaves, channels, voxels = features.shape
    size = lax.axis_size("dom")
    meta = jnp.concatenate([neighbors, mask_words], axis=1)
    to_cross, to_chip, *fields, occ, all_table, own_table, far_table, flags = prepare(
        meta, features, cotangent
    )
    store, flip, store_dy, flip_dy = fields
    between = [(i, i + 1) for i in range(1, size - 1, 2)]
    chip = exchange(to_chip, 1, size)
    cross = lax.ppermute(to_cross, "dom", between + [(j, i) for i, j in between])

    total, stack, stack_dy = grad_terms(own_table, flags, *fields, to_cross)
    keep, send = grad_far(far_table, flags, store_dy, cross, chip, total)
    own, *to_send = split_chunks(keep, exchange(send, 1, size))
    got = [exchange(to_send[m - 1], 2 * m, size) for m in (3, 2, 1)]
    out_features, out_done = conv(
        far_table, all_table, flags, occ, store, flip, cross, chip, weight, stack,
        to_send[0], False,
    )
    own = sum_chunks(own, got, out_done)
    if size > GROUP:
        groups = [[j * GROUP + i for j in range(size // GROUP)] for i in range(GROUP)]
        own = lax.psum(own, "dom", axis_index_groups=groups)
    back = [exchange(own, 2 * m, size) for m in (1, 2, 3)]
    in_grad, in_done = conv(
        far_table, all_table, flags, occ, store_dy, flip_dy, cross, chip, weight, stack_dy,
        own, True,
    )
    half = join_chunks([own] + back, in_done)
    other = exchange(half, 1, size)
    scale = float(size * leaves * voxels) ** -0.5
    weight_grad = unpack(other, scale, unpack(half, scale))
    return (out_features, in_grad, weight_grad)


def solution(mesh):
    split = P(("scene", "dom"), None, None)
    flat = P(("scene", "dom"), None)
    return jax.shard_map(
        shards,
        mesh=mesh,
        in_specs=(split, split, P(), flat, flat),
        out_specs=(split, split, P("scene", None, None)),
        check_vma=False,
    )
```

```python
import functools

import jax
import jax.numpy as jnp
from jax import lax
from jax.experimental import pallas as pl
from jax.experimental.pallas import tpu as pltpu
from jax.sharding import PartitionSpec as P

BITS = 30
NEAR = 26
EDGE = 8
FACE = EDGE * EDGE
TILE = 128
CH = 64
GROUP = 8
KROWS = 9 * CH
SPLIT = 5 * CH
STACK = (3 * CH, 6 * TILE)
VMEM_LIMIT = 16 * 1024 * 1024
BF = jnp.bfloat16
F32 = jnp.float32

SHIFTS = [(p, q) for p in (-1, 0, 1) for q in (-1, 0, 1)]


def column_of(p, q, r):
    tap = (p + 1) * 9 + (q + 1) * 3 + r + 1
    return tap if tap < 13 else tap - 1


def lane_ids(rows):
    return lax.broadcasted_iota(jnp.int32, (rows, TILE), 1)


def pick(test, a, b):
    rows = 16 if a.dtype == BF else 8
    mask = test(lane_ids(rows))
    return jnp.concatenate(
        [
            jnp.where(mask, a[i : i + rows], b[i : i + rows])
            for i in range(0, a.shape[0], rows)
        ],
        axis=0,
    )


def left(lane):
    return lane < FACE


def row_first(lane):
    return (lane // EDGE) % EDGE == 0


def row_last(lane):
    return (lane // EDGE) % EDGE == EDGE - 1


def cell_first(lane):
    return lane % EDGE == 0


def cell_last(lane):
    return lane % EDGE == EDGE - 1


def roll(value, amount):
    return pltpu.roll(value, amount % TILE, 1)


def swap(value):
    return roll(value, FACE)


def tile_of(value, k):
    return value[:, k * TILE : (k + 1) * TILE]


def occupancy_tile(words, tile):
    lane = lane_ids(words.shape[0]) + tile * TILE
    first, last = (tile * TILE) // BITS, (tile * TILE + TILE - 1) // BITS
    word = jnp.broadcast_to(words[:, first : first + 1], lane.shape)
    place = lane - first * BITS
    for w in range(first + 1, last + 1):
        past = lane >= w * BITS
        word = jnp.where(past, jnp.broadcast_to(words[:, w : w + 1], lane.shape), word)
        place = jnp.where(past, lane - w * BITS, place)
    return (jnp.right_shift(word, place) & 1).astype(F32)


def spread(occ, leaf):
    part = jnp.broadcast_to(occ[leaf : leaf + 1, :], (16, TILE)).astype(BF)
    return jnp.concatenate([part] * (CH // 16), axis=0)


def masked_tiles(field_ref, occ, leaf):
    return [
        field_ref[leaf, :, k * TILE : (k + 1) * TILE] * spread(occ[k], leaf) for k in range(4)
    ]


def reorder(tiles):
    n0, n1, n2, n3 = tiles
    r0, r1, r2, r3 = [swap(t) for t in tiles]
    order = [pick(left, n0, r2), pick(left, r0, n2), pick(left, n1, r3), pick(left, r1, n3)]
    flipped = [pick(left, n2, r0), pick(left, r2, n0), pick(left, n3, r1), pick(left, r3, n1)]
    return order, flipped


def restore(t0, t1, t2, t3):
    return [
        pick(left, t0, swap(t1)),
        pick(left, t2, swap(t3)),
        pick(left, swap(t0), t1),
        pick(left, swap(t2), t3),
    ]


def shift_q(center, flipped, q):
    test = row_last if q < 0 else row_first
    return [roll(pick(test, m, c), -q * EDGE) for m, c in zip(flipped, center)]


def write_tables(near, all_ref, own_ref, far_ref, flags_ref):
    leaves = near.shape[0]
    first = lax.axis_index("dom") * leaves
    slot = near - first
    absent = near < 0
    here = (slot >= 0) & (slot < leaves) & jnp.logical_not(absent)
    other = jnp.where(slot < 0, slot + leaves, slot - leaves)
    own_ref[...] = jnp.where(here, slot, leaves)
    far_ref[...] = jnp.where(here | absent, leaves, other)
    all_ref[...] = jnp.where(absent, 2 * leaves, jnp.where(here, slot, other + leaves))
    column = lax.broadcasted_iota(jnp.int32, near.shape, 1)
    cell = lax.rem(jnp.where(column < 13, column, column + 1), 3)
    flags = [
        jnp.max(jnp.where(present, 1, 0).astype(F32), axis=1, keepdims=True)
        for present in (
            jnp.logical_not(absent) & (cell == 0),
            jnp.logical_not(absent) & (cell == 2),
        )
    ]
    some = jnp.max(jnp.maximum(*flags), axis=0, keepdims=True)
    lane = lane_ids(leaves)
    table = jnp.where(lane == 0, flags[0], jnp.where(lane == 1, flags[1], some))
    flags_ref[...] = table.astype(jnp.int32)


def prepare_kernel(
    meta_ref, x_ref, d_ref, cross_ref, chip_ref, store, flip, store_dy, flip_dy, occ_ref,
    all_ref, own_ref, far_ref, flags_ref,
):
    leaves = x_ref.shape[0]
    words = meta_ref[:, NEAR:]
    occ = [occupancy_tile(words, k) for k in range(4)]
    occ_ref[...] = jnp.concatenate(occ, axis=1)
    write_tables(meta_ref[:, 0:NEAR], all_ref, own_ref, far_ref, flags_ref)
    first_core = lax.rem(lax.axis_index("dom"), 2) == 0
    for leaf in range(leaves):
        x_tiles, d_tiles = masked_tiles(x_ref, occ, leaf), masked_tiles(d_ref, occ, leaf)
        up = pick(left, swap(d_tiles[3]), x_tiles[3])
        down = pick(left, x_tiles[0], swap(d_tiles[0]))
        cross_ref[leaf] = jnp.where(first_core, down, up)
        chip_ref[leaf] = jnp.where(first_core, up, down)
        for tiles, order_ref, flip_ref in ((x_tiles, store, flip), (d_tiles, store_dy, flip_dy)):
            order, flipped = reorder(tiles)
            order_ref[leaf] = jnp.concatenate(order, axis=1)
            flip_ref[leaf] = jnp.concatenate(flipped, axis=1)
    for ref in (store, flip, store_dy, flip_dy):
        ref[leaves] = jnp.zeros(ref.shape[1:], BF)


def prepare(meta, x, dy):
    leaves = x.shape[0]
    planes = jax.ShapeDtypeStruct((leaves, CH, TILE), BF)
    store = jax.ShapeDtypeStruct((leaves + 1,) + x.shape[1:], BF)
    table = jax.ShapeDtypeStruct((leaves, NEAR), jnp.int32)
    return pl.pallas_call(
        prepare_kernel,
        out_shape=(planes,) * 2
        + (store,) * 4
        + (jax.ShapeDtypeStruct((leaves, 4 * TILE), F32),)
        + (table,) * 3
        + (jax.ShapeDtypeStruct((leaves, TILE), jnp.int32),),
        in_specs=[vmem_spec()] * 3,
        out_specs=(vmem_spec(),) * 11,
        cost_estimate=cost(10**6, 4 * 10**6),
        compiler_params=params(),
        name="prepare",
    )(meta, x, dy)


def split_far(cross_ref, chip_ref, leaf):
    first_core = lax.rem(lax.axis_index("dom"), 2) == 0
    low = jnp.where(first_core, chip_ref[leaf], cross_ref[leaf])
    high = jnp.where(first_core, cross_ref[leaf], chip_ref[leaf])
    return low, high


def with_far(store, own, cross_ref, chip_ref, turned):
    leaves = own.shape[0] - 1
    for leaf in range(leaves):
        store[leaf] = own[leaf]
        low, high = split_far(cross_ref, chip_ref, leaf)
        store[leaves + leaf, :, 0:TILE] = swap(low) if turned else low
        store[leaves + leaf, :, 3 * TILE :] = swap(high) if turned else high
    store[2 * leaves] = own[leaves]


def place(table_ref, leaf, p, q, z):
    if (p, q, z) == (0, 0, 0):
        return leaf
    return table_ref[leaf, column_of(p, q, z)]


def third(flags_ref, leaf, z):
    return flags_ref[leaf, 0 if z < 0 else 1] > 0


def any_third(flags_ref):
    return flags_ref[0, 2] > 0


def stacked(store, flip, table_ref, leaf, z):
    rows = {}
    center = None
    for q in (0, -1, 1):
        mid = place(table_ref, leaf, 0, q, z)
        after = place(table_ref, leaf, 1, q, z)
        before = place(table_ref, leaf, -1, q, z)
        mine = store[mid]
        past = pick(left, store[after, :, 0:TILE], tile_of(mine, 0))
        ahead = pick(left, tile_of(mine, 3), store[before, :, 3 * TILE :])
        if q == 0:
            center = [swap(ahead)] + [tile_of(mine, k) for k in range(4)] + [swap(past)]
            rows[q] = center
        else:
            other = flip[jnp.minimum(mid, flip.shape[0] - 1)]
            flipped = [ahead] + [tile_of(other, k) for k in range(4)] + [past]
            rows[q] = shift_q(center, flipped, q)
    return jnp.concatenate([jnp.concatenate(rows[q], axis=1) for q in (-1, 0, 1)], axis=0)


def unstack(stack):
    return jnp.concatenate([stack[:, i * TILE : (i + 4) * TILE] for i in range(3)], axis=0)


def shift_c(value, r):
    if r == 0:
        return value
    test = cell_last if r > 0 else cell_first
    tiles = [tile_of(value, k) for k in range(value.shape[1] // TILE)]
    return jnp.concatenate([pick(test, jnp.zeros_like(t), roll(t, -r)) for t in tiles], axis=1)


def across_c(value, z):
    test = cell_last if z > 0 else cell_first
    tiles = [tile_of(value, k) for k in range(value.shape[1] // TILE)]
    return jnp.concatenate(
        [pick(test, roll(t, z * (EDGE - 1)), jnp.zeros_like(t)) for t in tiles], axis=1
    )


CONTRACT_LANES = (((1,), (1,)), ((), ()))


def dot_lanes(a, b):
    return lax.dot_general(a, b, CONTRACT_LANES, preferred_element_type=F32)


def grad_kernel(
    table_ref, flags_ref, store, flip, store_dy, flip_dy, _, total, stack_ref, stack_dy_ref
):
    leaves = stack_ref.shape[0]
    for leaf in range(leaves):
        stack = stacked(store, flip, table_ref, leaf, 0)
        stack_ref[leaf] = stack
        stack_dy_ref[leaf] = stacked(store_dy, flip_dy, table_ref, leaf, 0)
        wide = jnp.concatenate([shift_c(store_dy[leaf], -r) for r in (-1, 0, 1)], axis=0)
        term = dot_lanes(unstack(stack), wide)
        if leaf == 0:
            total[...] = term
        else:
            total[...] += term

    @pl.when(any_third(flags_ref))
    def _():
        for z in (-1, 1):
            for leaf in range(leaves):

                @pl.when(third(flags_ref, leaf, z))
                def _():
                    stack = stacked(store, flip, table_ref, leaf, z)
                    edge = across_c(store_dy[leaf], -z)
                    total[:, (z + 1) * CH : (z + 2) * CH] += dot_lanes(unstack(stack), edge)


def grad_terms(table, flags, store, flip, store_dy, flip_dy, after):
    leaves = store.shape[0] - 1
    stack = jax.ShapeDtypeStruct((leaves,) + STACK, BF)
    return pl.pallas_call(
        grad_kernel,
        out_shape=(jax.ShapeDtypeStruct((KROWS, 3 * CH), F32), stack, stack),
        in_specs=[smem_spec()] * 2 + [vmem_spec()] * 4 + [any_spec()],
        out_specs=(vmem_spec(),) * 3,
        cost_estimate=cost(10**9, 2 * 10**6),
        compiler_params=params(),
        name="grad_terms",
    )(table, flags, store, flip, store_dy, flip_dy, after)


def third_part(row):
    return (KROWS + row, 0) if row < SPLIT else (KROWS + row - SPLIT, 1)


def grad_far_kernel(
    table_ref, flags_ref, store_dy, cross_ref, chip_ref, near_total, keep_ref, send_ref,
    store, packed,
):
    leaves = store_dy.shape[0] - 1
    for leaf in range(leaves):
        low, high = split_far(cross_ref, chip_ref, leaf)
        store[0, leaf], store[1, leaf] = low, high
        store[2, leaf], store[3, leaf] = swap(low), swap(high)
    for i in range(4):
        store[i, leaves] = jnp.zeros((CH, TILE), BF)

    def far_rows(p, one, two, z):
        at = lambda leaf, q: place(table_ref, leaf, p, q, z)
        first, second = (0, 2) if p > 0 else (3, 1)
        pair = lambda a, b, q: pick(left, store[first, at(a, q)], store[second, at(b, q)])
        center = pair(one, two, 0)
        sides = [shift_q([center], [pair(two, one, q)], q)[0] for q in (-1, 1)]
        return jnp.concatenate([sides[0], center, sides[1]], axis=0)

    def end_plane(p, one, two):
        if p > 0:
            return pick(left, swap(store_dy[one, :, 3 * TILE :]), store_dy[two, :, 3 * TILE :])
        return pick(left, store_dy[one, :, 0:TILE], swap(store_dy[two, :, 0:TILE]))

    pairs = [(leaf, leaf + 1) for leaf in range(0, leaves, 2)]
    for p in (-1, 0, 1):
        term = None
        if p != 0:
            rows = jnp.concatenate([far_rows(p, a, b, 0) for a, b in pairs], axis=1)
            planes = jnp.concatenate([end_plane(p, a, b) for a, b in pairs], axis=1)
            wide = jnp.concatenate([shift_c(planes, -r) for r in (-1, 0, 1)], axis=0)
            term = dot_lanes(rows, wide)
        for q in (-1, 0, 1):
            row = SHIFTS.index((p, q)) * CH
            block = near_total[row : row + CH, :]
            if p != 0:
                block = block + term[(q + 1) * CH : (q + 2) * CH, :]
            packed[row : row + CH, :] = block[:, 0:TILE]
            low, side = third_part(row)
            packed[low : low + CH, side * CH : (side + 1) * CH] = block[:, TILE:]
    packed[2 * KROWS - SPLIT :, CH:] = jnp.zeros((2 * SPLIT - KROWS, CH), F32)

    @pl.when(any_third(flags_ref))
    def _():
        for z in (-1, 1):
            for leaf in range(leaves):

                @pl.when(third(flags_ref, leaf, z))
                def _():
                    for p in (-1, 1):
                        plane = end_plane(p, leaf, leaf)
                        plane = across_c(pick(left, plane, jnp.zeros_like(plane)), -z)
                        term = dot_lanes(far_rows(p, leaf, leaf, z), plane)
                        for q in (-1, 0, 1):
                            row, side = SHIFTS.index((p, q)) * CH, 0
                            if z > 0:
                                row, side = third_part(row)
                            packed[row : row + CH, side * CH : (side + 1) * CH] += term[
                                (q + 1) * CH : (q + 2) * CH, :
                            ]

    core = lax.rem(lax.axis_index("dom"), 2)
    rows = packed.shape[0] // 2
    keep_ref[...] = packed[pl.ds(pl.multiple_of(core * rows, 8), rows), :]
    send_ref[...] = packed[pl.ds(pl.multiple_of((1 - core) * rows, 8), rows), :]


def grad_far(table, flags, store_dy, cross, chip, total):
    leaves = store_dy.shape[0] - 1
    rows = KROWS + SPLIT
    shape = jax.ShapeDtypeStruct((rows // 2, TILE), F32)
    return pl.pallas_call(
        grad_far_kernel,
        out_shape=(shape, shape),
        in_specs=[smem_spec()] * 2 + [vmem_spec()] * 4,
        out_specs=(vmem_spec(), vmem_spec()),
        scratch_shapes=[
            pltpu.VMEM((4, leaves + 1, CH, TILE), BF),
            pltpu.VMEM((rows, TILE), F32),
        ],
        cost_estimate=cost(10**8, 2 * 10**6),
        compiler_params=params(),
        name="grad_far",
    )(table, flags, store_dy, cross, chip, total)


def vmem_spec():
    return pl.BlockSpec(memory_space=pltpu.VMEM)


def any_spec():
    return pl.BlockSpec(memory_space=pl.ANY)


def smem_spec():
    return pl.BlockSpec(memory_space=pltpu.SMEM)


def params():
    return pltpu.CompilerParams(vmem_limit_bytes=VMEM_LIMIT)


def cost(flops, bytes_accessed):
    return pl.CostEstimate(flops=flops, bytes_accessed=bytes_accessed, transcendentals=0)


def ordered_taps(w_ref, turned):
    def tap(index, r):
        p, q = SHIFTS[index]
        return (p + 1) * 9 + (q + 1) * 3 + r + 1

    if turned:
        return jnp.concatenate(
            [
                jnp.concatenate([w_ref[26 - tap(index, r)] for index in range(9)], axis=1)
                for r in (-1, 0, 1)
            ],
            axis=0,
        )
    return jnp.concatenate(
        [
            jnp.concatenate([w_ref[tap(index, r)] for r in (-1, 0, 1)], axis=1)
            for index in range(9)
        ],
        axis=0,
    ).T


def finish(occ, leaf, total):
    rounded = total.astype(BF)
    tiles = restore(*[tile_of(rounded, k) for k in range(4)])
    return jnp.concatenate([t * spread(occ[k], leaf) for k, t in enumerate(tiles)], axis=1)


def leaf_sum(taps, near_x):
    wide = jnp.dot(taps, near_x, preferred_element_type=F32)
    total = wide[CH : 2 * CH]
    for r in (-1, 1):
        total = total + shift_c(wide[(r + 1) * CH : (r + 2) * CH], r)
    return total


def far_tiles(far, table_ref, leaf):
    at = lambda p, q: place(table_ref, leaf, p, q, 0)
    center = pick(left, far[1, at(-1, 0)], far[1, at(1, 0)])
    flipped = {q: pick(left, far[0, at(1, q)], far[0, at(-1, q)]) for q in (-1, 1)}
    sides = [shift_q([center], [flipped[q]], q)[0] for q in (-1, 1)]
    return jnp.concatenate([sides[0], center, sides[1]], axis=0)


def conv_kernel(
    turned, far_table_ref, all_table_ref, flags_ref, occ_ref, own, flip, cross_ref, chip_ref, w_ref,
    stack_ref, _, out_ref, done_ref, far, store,
):
    leaves = out_ref.shape[0]
    occ = [tile_of(occ_ref[...], k) for k in range(4)]
    done_ref[...] = jnp.zeros(done_ref.shape, F32)
    taps = ordered_taps(w_ref, turned)
    for leaf in range(leaves):
        low, high = split_far(cross_ref, chip_ref, leaf)
        both = pick(left, high, low) if turned else pick(left, low, high)
        far[0, leaf], far[1, leaf] = (swap(both), both) if turned else (both, swap(both))
    far[0, leaves] = far[1, leaves] = jnp.zeros((CH, TILE), BF)
    for leaf in range(leaves):
        planes = far_tiles(far, far_table_ref, leaf)
        zero = jnp.zeros_like(planes)
        stack = stack_ref[leaf]
        stack = jnp.concatenate(
            [
                tile_of(stack, 0) + pick(left, planes, zero),
                stack[:, TILE : 5 * TILE],
                tile_of(stack, 5) + pick(left, zero, planes),
            ],
            axis=1,
        )
        out_ref[leaf] = finish(occ, leaf, leaf_sum(taps, unstack(stack)))

    @pl.when(any_third(flags_ref))
    def _():
        with_far(store, own, cross_ref, chip_ref, turned)
        for leaf in range(leaves):
            total = leaf_sum(taps, unstack(stacked(store, flip, all_table_ref, leaf, 0)))
            for z in (-1, 1):
                near_z = unstack(stacked(store, flip, all_table_ref, leaf, z))
                part = jnp.dot(
                    taps[(z + 1) * CH : (z + 2) * CH], near_z, preferred_element_type=F32
                )
                total = total + across_c(part, z)
            out_ref[leaf] = finish(occ, leaf, total)


def conv(far_table, all_table, flags, occ, own, flip, cross, chip, weight, stack, after, turned):
    leaves = stack.shape[0]
    return pl.pallas_call(
        functools.partial(conv_kernel, turned),
        out_shape=(
            jax.ShapeDtypeStruct((leaves, CH, 4 * TILE), BF),
            jax.ShapeDtypeStruct((8, TILE), F32),
        ),
        in_specs=[smem_spec()] * 3 + [vmem_spec()] * 7 + [any_spec()],
        out_specs=(vmem_spec(),) * 2,
        scratch_shapes=[
            pltpu.VMEM((2, leaves + 1, CH, TILE), BF),
            pltpu.VMEM((2 * leaves + 1, CH, 4 * TILE), BF),
        ],
        cost_estimate=cost(10**9, 2 * 10**6),
        compiler_params=params(),
        name="in_grad_conv" if turned else "out_conv",
    )(far_table, all_table, flags, occ, own, flip, cross, chip, weight, stack, after)


def split_kernel(keep_ref, got_ref, *refs):
    *out_refs, total = refs
    total[...] = keep_ref[...] + got_ref[...]
    lane = lax.rem(lax.axis_index("dom") // 2, 4)
    rows = out_refs[0].shape[0]
    for mask, out_ref in enumerate(out_refs):
        at = pl.multiple_of(jnp.bitwise_xor(lane, mask) * rows, 8)
        out_ref[...] = total[pl.ds(at, rows), :]


def split_chunks(keep, got):
    chunk = jax.ShapeDtypeStruct((keep.shape[0] // 4, TILE), F32)
    return pl.pallas_call(
        split_kernel,
        out_shape=(chunk,) * 4,
        in_specs=[vmem_spec()] * 2,
        out_specs=(vmem_spec(),) * 4,
        scratch_shapes=[pltpu.VMEM(keep.shape, F32)],
        cost_estimate=cost(10**5, 10**6),
        compiler_params=params(),
        name="split_chunks",
    )(keep, got)


def sum_kernel(own_ref, *refs):
    *got_refs, _, out_ref = refs
    total = own_ref[...]
    for got_ref in got_refs:
        total = total + got_ref[...]
    out_ref[...] = total


def sum_chunks(own, got, after):
    return pl.pallas_call(
        sum_kernel,
        out_shape=jax.ShapeDtypeStruct(own.shape, F32),
        in_specs=[vmem_spec()] * (1 + len(got)) + [any_spec()],
        out_specs=vmem_spec(),
        cost_estimate=cost(10**5, 3 * 10**5),
        compiler_params=params(),
        name="sum_chunks",
    )(own, *got, after)


def join_kernel(*refs):
    *parts, _, out_ref = refs
    lane = lax.rem(lax.axis_index("dom") // 2, 4)
    rows = parts[0].shape[0]
    for mask, part in enumerate(parts):
        at = pl.multiple_of(jnp.bitwise_xor(lane, mask) * rows, 8)
        out_ref[pl.ds(at, rows), :] = part[...]


def join_chunks(parts, after):
    rows = parts[0].shape[0]
    return pl.pallas_call(
        join_kernel,
        out_shape=jax.ShapeDtypeStruct((len(parts) * rows, TILE), F32),
        in_specs=[vmem_spec()] * len(parts) + [any_spec()],
        out_specs=vmem_spec(),
        cost_estimate=cost(10**5, 5 * 10**5),
        compiler_params=params(),
        name="join_chunks",
    )(*parts, after)


def half_taps(half):
    found = []
    for index, (p, q) in enumerate(SHIFTS):
        for r in (-1, 0, 1):
            row, side = index * CH, r + 1
            if r == 1:
                row, side = third_part(row)
            if row // (7 * CH) == half:
                found.append(((p + 1) * 9 + (q + 1) * 3 + r + 1, row - half * 7 * CH, side))
    return found


def unpack_kernel(scale, mine, half_ref, *refs):
    *_, out_ref, taps, sem = refs
    core = lax.rem(lax.axis_index("dom"), 2)

    def write(half):
        found = half_taps(half)
        for i, (tap, row, side) in enumerate(found):
            block = half_ref[row : row + CH, side * CH : (side + 1) * CH]
            taps[i] = block * scale
            pltpu.make_async_copy(taps.at[i], out_ref.at[tap], sem.at[i]).start()
        for i, (tap, row, side) in enumerate(found):
            pltpu.make_async_copy(taps.at[i], out_ref.at[tap], sem.at[i]).wait()

    first = core == 0 if mine else core == 1
    pl.when(first)(lambda: write(0))
    pl.when(jnp.logical_not(first))(lambda: write(1))


def unpack(half, scale, so_far=None):
    rest = [] if so_far is None else [so_far]
    hbm = pl.BlockSpec(memory_space=pltpu.HBM)
    return pl.pallas_call(
        functools.partial(unpack_kernel, scale, not rest),
        out_shape=jax.ShapeDtypeStruct((27, CH, CH), F32),
        in_specs=[vmem_spec()] + [hbm] * len(rest),
        out_specs=hbm,
        input_output_aliases={1: 0} if rest else {},
        scratch_shapes=[pltpu.VMEM((14, CH, CH), F32), pltpu.SemaphoreType.DMA((14,))],
        cost_estimate=cost(10**6, 10**6),
        compiler_params=params(),
        name="unpack_other" if rest else "unpack_own",
    )(half, *rest)


def exchange(array, mask, size):
    return lax.ppermute(array, "dom", [(i, i ^ mask) for i in range(size)])


def shards(features, cotangent, weight, mask_words, neighbors):
    leaves, channels, voxels = features.shape
    size = lax.axis_size("dom")
    meta = jnp.concatenate([neighbors, mask_words], axis=1)
    to_cross, to_chip, *fields, occ, all_table, own_table, far_table, flags = prepare(
        meta, features, cotangent
    )
    store, flip, store_dy, flip_dy = fields
    forward = exchange(to_cross, 1, size)
    chip = exchange(to_chip, 1, size)
    steps = range(0, size - 2, 2)
    cross = lax.ppermute(
        forward, "dom", [(i, i + 2) for i in steps] + [(i + 3, i + 1) for i in steps]
    )

    total, stack, stack_dy = grad_terms(own_table, flags, *fields, forward)
    keep, send = grad_far(far_table, flags, store_dy, cross, chip, total)
    own, *to_send = split_chunks(keep, exchange(send, 1, size))
    got = [exchange(to_send[m - 1], 2 * m, size) for m in (3, 2, 1)]
    out_features, out_done = conv(
        far_table, all_table, flags, occ, store, flip, cross, chip, weight, stack,
        to_send[0], False,
    )
    own = sum_chunks(own, got, out_done)
    if size > GROUP:
        groups = [[j * GROUP + i for j in range(size // GROUP)] for i in range(GROUP)]
        own = lax.psum(own, "dom", axis_index_groups=groups)
    back = [exchange(own, 2 * m, size) for m in (1, 2, 3)]
    in_grad, in_done = conv(
        far_table, all_table, flags, occ, store_dy, flip_dy, cross, chip, weight, stack_dy,
        own, True,
    )
    half = join_chunks([own] + back, in_done)
    other = exchange(half, 1, size)
    scale = float(size * leaves * voxels) ** -0.5
    weight_grad = unpack(other, scale, unpack(half, scale))
    return (out_features, in_grad, weight_grad)


def solution(mesh):
    split = P(("scene", "dom"), None, None)
    flat = P(("scene", "dom"), None)
    return jax.shard_map(
        shards,
        mesh=mesh,
        in_specs=(split, split, P(), flat, flat),
        out_specs=(split, split, P("scene", None, None)),
        check_vma=False,
    )
```
